32 devices in a mesh: dp: 16 (over z, x, core), tensor: 2 (over y).
Axes of the slice: x: 2, y: 2, z: 4, core: 2. Of those that a mesh axis runs over, the one named last changes fastest.
Arguments:
- frames: bfloat16 [32, 1024, 512], P('dp', 'tensor'), may hold values from -6 to 6
- codes: int32 [32, 1024], P('dp', 'tensor'), may hold values from 0 to 8191
- clip_frames: int32 [8], replicated, may hold values from 1 to 12, 32 in all
- out_cotangent: bfloat16 [32, 1024, 512], P('dp', 'tensor'), may hold values from -6 to 6
- heads_weight: float32 [2, 3, 512, 512], P(None, None, 'dp', 'tensor'), may hold values from -0.25 to 0.25
- merge_weight: float32 [2, 512, 512], P(None, 'tensor', 'dp'), may hold values from -6 to 6
- expand_weight: float32 [2, 512, 2048], P(None, 'dp', 'tensor'), may hold values from -0.25 to 0.25
- shrink_weight: float32 [2, 2048, 512], P(None, 'tensor', 'dp'), may hold values from -0.125 to 0.125
- vectors: float32 [15, 512], P(None, ('dp', 'tensor')), may hold values from -0.9 to 2.7, as said below
- encode_weight: float32 [512, 32], P(('dp', 'tensor')), may hold values from -0.25 to 0.25
- codebook: float32 [8192, 32], P(('dp', 'tensor')), may hold values from -6 to 6
- decode_weight: float32 [32, 512], P(None, ('dp', 'tensor')), may hold values from -1 to 1
- heads_first: float32 [2, 3, 512, 512], P(None, None, 'dp', 'tensor'), may hold values from -0.00024414062 to 0.00024414062
- merge_first: float32 [2, 512, 512], P(None, 'tensor', 'dp'), may hold values from -5.340576e-05 to 5.340576e-05
- expand_first: float32 [2, 512, 2048], P(None, 'dp', 'tensor'), may hold values from -3.8146973e-05 to 3.8146973e-05
- shrink_first: float32 [2, 2048, 512], P(None, 'tensor', 'dp'), may hold values from -5.340576e-05 to 5.340576e-05
- vectors_first: float32 [15, 512], P(None, ('dp', 'tensor')), may hold values from -0.00024414062 to 0.00024414062
- encode_first: float32 [512, 32], P(('dp', 'tensor')), may hold values from -0.00024414062 to 0.00024414062
- codebook_first: float32 [8192, 32], P(('dp', 'tensor')), may hold values from -6.67572e-06 to 6.67572e-06
- decode_first: float32 [32, 512], P(None, ('dp', 'tensor')), may hold values from -0.00024414062 to 0.00024414062
- heads_second: float32 [2, 3, 512, 512], P(None, None, 'dp', 'tensor'), may hold values from 3.94295e-09 to 6.3693804e-08
- merge_second: float32 [2, 512, 512], P(None, 'tensor', 'dp'), may hold values from 1.7743274e-10 to 2.8662213e-09
- expand_second: float32 [2, 512, 2048], P(None, 'dp', 'tensor'), may hold values from 9.8573746e-11 to 1.5923451e-09
- shrink_second: float32 [2, 2048, 512], P(None, 'tensor', 'dp'), may hold values from 1.5771799e-10 to 2.5477522e-09
- vectors_second: float32 [15, 512], P(None, ('dp', 'tensor')), may hold values from 3.94295e-09 to 6.3693804e-08
- encode_second: float32 [512, 32], P(('dp', 'tensor')), may hold values from 3.94295e-09 to 6.3693804e-08
- codebook_second: float32 [8192, 32], P(('dp', 'tensor')), may hold values from 2.36577e-12 to 3.821628e-11
- decode_second: float32 [32, 512], P(None, ('dp', 'tensor')), may hold values from 3.94295e-09 to 6.3693804e-08
Outputs:
- decoded: float32 [32, 1024, 512], P('dp', 'tensor')
- frames_grad: float32 [32, 1024, 512], P('dp', 'tensor')
- norm_before: float32 [], replicated
- heads_mean: float32 [2, 3, 512, 512], P(None, None, 'dp', 'tensor')
- heads_square: float32 [2, 3, 512, 512], P(None, None, 'dp', 'tensor')
- heads_master: float32 [2, 3, 512, 512], P(None, None, 'dp', 'tensor')
- heads_copy: bfloat16 [2, 3, 512, 512], P(None, None, 'dp', 'tensor')
- merge_mean: float32 [2, 512, 512], P(None, 'tensor', 'dp')
- merge_square: float32 [2, 512, 512], P(None, 'tensor', 'dp')
- merge_master: float32 [2, 512, 512], P(None, 'tensor', 'dp')
- merge_copy: bfloat16 [2, 512, 512], P(None, 'tensor', 'dp')
- expand_mean: float32 [2, 512, 2048], P(None, 'dp', 'tensor')
- expand_square: float32 [2, 512, 2048], P(None, 'dp', 'tensor')
- expand_master: float32 [2, 512, 2048], P(None, 'dp', 'tensor')
- expand_copy: bfloat16 [2, 512, 2048], P(None, 'dp', 'tensor')
- shrink_mean: float32 [2, 2048, 512], P(None, 'tensor', 'dp')
- shrink_square: float32 [2, 2048, 512], P(None, 'tensor', 'dp')
- shrink_master: float32 [2, 2048, 512], P(None, 'tensor', 'dp')
- shrink_copy: bfloat16 [2, 2048, 512], P(None, 'tensor', 'dp')
- vectors_mean: float32 [15, 512], P(None, ('dp', 'tensor'))
- vectors_square: float32 [15, 512], P(None, ('dp', 'tensor'))
- vectors_master: float32 [15, 512], P(None, ('dp', 'tensor'))
- vectors_copy: bfloat16 [15, 512], P(None, ('dp', 'tensor'))
- encode_mean: float32 [512, 32], P(('dp', 'tensor'))
- encode_square: float32 [512, 32], P(('dp', 'tensor'))
- encode_master: float32 [512, 32], P(('dp', 'tensor'))
- encode_copy: bfloat16 [512, 32], P(('dp', 'tensor'))
- codebook_mean: float32 [8192, 32], P(('dp', 'tensor'))
- codebook_square: float32 [8192, 32], P(('dp', 'tensor'))
- codebook_master: float32 [8192, 32], P(('dp', 'tensor'))
- codebook_copy: bfloat16 [8192, 32], P(('dp', 'tensor'))
- decode_mean: float32 [32, 512], P(None, ('dp', 'tensor'))
- decode_square: float32 [32, 512], P(None, ('dp', 'tensor'))
- decode_master: float32 [32, 512], P(None, ('dp', 'tensor'))
- decode_copy: bfloat16 [32, 512], P(None, ('dp', 'tensor'))
The draws below stay inside these ranges and needn't reach their ends.
Inputs may be any that keep to these rules, and one draw needn't show every extreme that they name: Clip c holds clip_frames[c] consecutive frames, clips in order over all 32 frames; the counts sum to 32 and the largest is exactly 12. `vectors`: rows 0, 3, 6, 9 and 12 are positive gains.
All inputs are finite; a program needn't handle non-finite values.
Results may differ from the reference program's by a relative error of at most 0.015.
The reference program's roundings to bfloat16 on the way count: a program that leaves them out, or rounds other values in their place, can miss the bound.
Values may be sent and summed in bfloat16 or wider, within the bound.
A program may use at most 256 MiB of HBM per device.

```python
import math
import jax
import jax.numpy as jnp
import numpy as np
from jax import lax

D = 512
HEADS = 8
HEAD_DIM = 64
FF = 2048
CODE = 32
CODES = 8192
FRAME_TOK = 1024
MOST_CLIP = 12
NVEC = 15
STEP = 10
FRAMES = 32
CLIPS = 8
PARAMS = 6594048


def draw_vectors(key, part):
    jitter_key, shift_key = jax.random.split(key, 2)
    column = jnp.arange(D, dtype=jnp.float32) / max(D - 1, 1)
    rising = 0.6 * jnp.exp(jnp.log(3.0) * column)
    jitter = jax.random.uniform(jitter_key, (NVEC, D), jnp.float32, 0.8, 1.2)
    shifts = 0.3 * jnp.clip(jax.random.normal(shift_key, (NVEC, D), jnp.float32), -3.0, 3.0)
    row_ids = jnp.arange(NVEC)
    is_gain = (row_ids % 3 == 0)[:, None]
    return jnp.where(is_gain, rising[None, :] * jitter, shifts)


def plant(drawn, key, low, largest):
    longest = drawn.shape.index(max(drawn.shape))
    spots = []
    for shift in (0, 1):
        where = [jax.random.randint(jax.random.fold_in(key, axis), (), 0, length) for axis, length in enumerate(drawn.shape)]
        where[longest] = (where[longest] + shift) % drawn.shape[longest]
        spots.append(tuple(where))
    return drawn.at[spots[0]].set(low).at[spots[1]].set(largest)


def steps_of(key, dims, cuts, low, top_value):
    def one(dim, shards_of):
        steps = jax.random.uniform(jax.random.fold_in(jax.random.fold_in(key, 6), dim), (shards_of,), jnp.float32, low / len(cuts), top_value / len(cuts))
        return jnp.repeat(jnp.exp(steps), dims[dim] // shards_of).reshape((-1,) + (1,) * (len(dims) - dim - 1))

    gain = one(*cuts[0])
    for cut in cuts[1:]:
        gain = gain * one(*cut)
    return gain


def split_up(count, total, most, skew):
    weights = [(1 << 20) // math.isqrt(rank ** skew) + 1 for rank in range(2, count + 1)]
    surplus, holding = total - most - (count - 1), [1] * (count - 1)
    while surplus > 0:
        free = [i for i in range(count - 1) if holding[i] < most]
        whole, left = sum([weights[i] for i in free]), surplus
        for i in free:
            more = min(most - holding[i], max(1, left * weights[i] // whole), surplus)
            holding[i] = holding[i] + more
            surplus = surplus - more
    return np.array([most] + holding)


def uneven_parts(rng, amount, total, reach, lean):
    if amount == 2:
        one = jax.random.randint(rng, (), max(1, total - reach), min(reach, total - 1) + 1)
        return jnp.stack([one, total - one])
    tallies = jnp.asarray(split_up(amount, total, reach, lean), jnp.int32)
    twos = (amount - 1) // 2
    donor, sink = tallies[1:1 + 2 * twos:2], tallies[2:2 + 2 * twos:2]
    margin = jnp.minimum(donor - 1, reach - sink)
    shifted = jax.random.randint(jax.random.fold_in(rng, 1), (twos,), 0, 1 << 20) % (margin + 1)
    tallies = tallies.at[1:1 + 2 * twos:2].set(donor - shifted).at[2:2 + 2 * twos:2].set(sink + shifted)
    return tallies[jax.random.permutation(jax.random.fold_in(rng, 2), amount)]


def gaussian(rng, dims, scale, most, cuts=(), kind=jnp.bfloat16):
    result = scale * jax.random.normal(rng, dims, jnp.float32)
    if cuts:
        result = result * steps_of(rng, dims, cuts, -0.22, 0.18)
    return jnp.clip(result, -most, most).astype(kind)


def setup_inputs(seed: int = 0) -> dict:
    streams_of = jax.random.split(jax.random.key(seed), 29)
    frames = gaussian(streams_of[0], (FRAMES, FRAME_TOK, D), 1.0, 6.0, ((0, 16), (1, 2)))
    codes = plant(jax.random.randint(streams_of[1], (FRAMES, FRAME_TOK), 0, CODES), jax.random.fold_in(streams_of[1], 1), 0, CODES - 1).astype(jnp.int32)
    clip_frames = uneven_parts(streams_of[2], CLIPS, FRAMES, MOST_CLIP, 2).astype(jnp.int32)
    out_cotangent = gaussian(streams_of[3], (FRAMES, FRAME_TOK, D), 1.0, 6.0, ((0, 16), (1, 2)))
    heads_weight = gaussian(streams_of[4], (2, 3, D, HEADS * HEAD_DIM), D ** -0.5, 0.25, ((2, 16), (3, 2)), jnp.float32)
    merge_weight = gaussian(streams_of[5], (2, HEADS * HEAD_DIM, D), (max(1, 3 * D // FRAME_TOK)) ** -0.5, 6.0, ((1, 2), (2, 16)), jnp.float32)
    expand_weight = gaussian(streams_of[6], (2, D, FF), D ** -0.5, 0.25, ((1, 16), (2, 2)), jnp.float32)
    shrink_weight = gaussian(streams_of[7], (2, FF, D), FF ** -0.5, 0.125, ((1, 2), (2, 16)), jnp.float32)
    vectors = draw_vectors(jax.random.fold_in(streams_of[28], 71), 0)
    encode_weight = gaussian(streams_of[9], (D, CODE), D ** -0.5, 0.25, ((0, 32),), jnp.float32)
    codebook = gaussian(streams_of[10], (CODES, CODE), 1.0, 6.0, ((0, 32),), jnp.float32)
    decode_weight = gaussian(streams_of[11], (CODE, D), CODE ** -0.5, 1.0, ((1, 32),), jnp.float32)
    heads_first = gaussian(streams_of[12], (2, 3, D, HEADS * HEAD_DIM), (0.11 * PARAMS ** -0.5), 0.00024414062, ((2, 16), (3, 2)), jnp.float32)
    merge_first = gaussian(streams_of[13], (2, HEADS * HEAD_DIM, D), (0.023 * PARAMS ** -0.5), 5.340576171875e-05, ((1, 2), (2, 16)), jnp.float32)
    expand_first = gaussian(streams_of[14], (2, D, FF), (0.0174 * PARAMS ** -0.5), 3.814697265625e-05, ((1, 16), (2, 2)), jnp.float32)
    shrink_first = gaussian(streams_of[15], (2, FF, D), (0.022 * PARAMS ** -0.5), 5.340576171875e-05, ((1, 2), (2, 16)), jnp.float32)
    vectors_first = gaussian(streams_of[16], (NVEC, D), (0.11 * PARAMS ** -0.5), 0.00024414062, ((1, 32),), jnp.float32)
    encode_first = gaussian(streams_of[17], (D, CODE), (0.11 * PARAMS ** -0.5), 0.00024414062, ((0, 32),), jnp.float32)
    codebook_first = gaussian(streams_of[18], (CODES, CODE), (0.0027 * PARAMS ** -0.5), 6.67572021484375e-06, ((0, 32),), jnp.float32)
    decode_first = gaussian(streams_of[19], (CODE, D), (0.11 * PARAMS ** -0.5), 0.00024414062, ((1, 32),), jnp.float32)
    heads_second = jnp.clip(jnp.exp(math.log(6.369380400883529e-08) - 2.7821581 * jax.random.uniform(streams_of[20], (2, 3, D, HEADS * HEAD_DIM), jnp.float32) ** steps_of(streams_of[20], (2, 3, D, HEADS * HEAD_DIM), ((2, 16), (3, 2)), -0.2, 0.2)), 3.942949966528886e-09, 6.369380400883529e-08)
    merge_second = jnp.clip(jnp.exp(math.log(2.8662212603336457e-09) - 2.7821582 * jax.random.uniform(streams_of[21], (2, HEADS * HEAD_DIM, D), jnp.float32) ** steps_of(streams_of[21], (2, HEADS * HEAD_DIM, D), ((1, 2), (2, 16)), -0.2, 0.2)), 1.7743273517112357e-10, 2.8662212603336457e-09)
    expand_second = jnp.clip(jnp.exp(math.log(1.5923451446298031e-09) - 2.7821582 * jax.random.uniform(streams_of[22], (2, D, FF), jnp.float32) ** steps_of(streams_of[22], (2, D, FF), ((1, 16), (2, 2)), -0.2, 0.2)), 9.857374638766458e-11, 1.5923451446298031e-09)
    shrink_second = jnp.clip(jnp.exp(math.log(2.547752231407685e-09) - 2.7821582 * jax.random.uniform(streams_of[23], (2, FF, D), jnp.float32) ** steps_of(streams_of[23], (2, FF, D), ((1, 2), (2, 16)), -0.2, 0.2)), 1.5771799144470577e-10, 2.547752231407685e-09)
    vectors_second = jnp.clip(jnp.exp(math.log(6.369380400883529e-08) - 2.7821581 * jax.random.uniform(streams_of[24], (NVEC, D), jnp.float32) ** steps_of(streams_of[24], (NVEC, D), ((1, 32),), -0.2, 0.2)), 3.942949966528886e-09, 6.369380400883529e-08)
    encode_second = jnp.clip(jnp.exp(math.log(6.369380400883529e-08) - 2.7821581 * jax.random.uniform(streams_of[25], (D, CODE), jnp.float32) ** steps_of(streams_of[25], (D, CODE), ((0, 32),), -0.2, 0.2)), 3.942949966528886e-09, 6.369380400883529e-08)
    codebook_second = jnp.clip(jnp.exp(math.log(3.821628083433559e-11) - 2.7821581 * jax.random.uniform(streams_of[26], (CODES, CODE), jnp.float32) ** steps_of(streams_of[26], (CODES, CODE), ((0, 32),), -0.2, 0.2)), 2.365769906365056e-12, 3.821628083433559e-11)
    decode_second = jnp.clip(jnp.exp(math.log(6.369380400883529e-08) - 2.7821581 * jax.random.uniform(streams_of[27], (CODE, D), jnp.float32) ** steps_of(streams_of[27], (CODE, D), ((1, 32),), -0.2, 0.2)), 3.942949966528886e-09, 6.369380400883529e-08)
    return dict(frames=frames, codes=codes, clip_frames=clip_frames, out_cotangent=out_cotangent, heads_weight=heads_weight, merge_weight=merge_weight, expand_weight=expand_weight, shrink_weight=shrink_weight, vectors=vectors, encode_weight=encode_weight, codebook=codebook, decode_weight=decode_weight, heads_first=heads_first, merge_first=merge_first, expand_first=expand_first, shrink_first=shrink_first, vectors_first=vectors_first, encode_first=encode_first, codebook_first=codebook_first, decode_first=decode_first, heads_second=heads_second, merge_second=merge_second, expand_second=expand_second, shrink_second=shrink_second, vectors_second=vectors_second, encode_second=encode_second, codebook_second=codebook_second, decode_second=decode_second)


@jax.custom_vjp
def low(v):
    return lax.optimization_barrier(v.astype(jnp.bfloat16)).astype(jnp.float32)

@jax.custom_vjp
def low_back(v):
    return v

def low_keep(v):
    return (low(v), None)

def low_pass(kept, grad):
    return (grad,)

def back_keep(v):
    return (v, None)

def back_low(kept, grad):
    return (low(grad),)
low.defvjp(low_keep, low_pass)
low_back.defvjp(back_keep, back_low)
EPS_NORM = 1e-05
EPS_UNIT = 1e-06
COMMIT_WEIGHT = 100.0
MAX_NORM = 1.0
MEAN_DECAY = 0.9
SQUARE_DECAY = 0.95
ADAM_EPS = 1e-08
RATES = (0.1, 0.5, 0.1, 0.05, 1.0, 0.1, 1.0, 0.3)
DECAYS = (0.1, 0.1, 0.1, 0.1, 0.0, 0.1, 0.1, 0.1)

def matmul(first_arg, second_arg):
    return jnp.dot(first_arg, second_arg, precision=lax.Precision.HIGHEST, preferred_element_type=jnp.float32)

def layer_norm(token_rows, gain_row, shift_row):
    center = token_rows - lax.optimization_barrier(jnp.mean(token_rows, axis=-1, keepdims=True))
    spread = lax.optimization_barrier(jnp.mean(center * center, axis=-1, keepdims=True))
    return center * lax.rsqrt(spread + EPS_NORM) * gain_row + shift_row

def unit_rows(vectors_in):
    return vectors_in * lax.rsqrt(lax.optimization_barrier(jnp.sum(vectors_in * vectors_in, axis=-1, keepdims=True)) + EPS_UNIT)

def gelu_tanh(values):
    return jax.nn.gelu(values, approximate=True)

def block_forward(token_rows, head_proj, merge_proj, expand_proj, shrink_proj, vector_rows):
    length = token_rows.shape[0]
    normed = low(layer_norm(token_rows, vector_rows[0], vector_rows[1]))
    projected = [low(low_back(matmul(normed, head_proj[member]))) for member in range(3)]
    split_heads = [part_value.reshape(length, HEADS, HEAD_DIM) for part_value in projected]
    scores = low_back(jnp.einsum('qhd,khd->hqk', split_heads[0], split_heads[1], precision=lax.Precision.HIGHEST) * HEAD_DIM ** (-0.5))
    attend = low(jax.nn.softmax(scores, axis=-1))
    mixture = jnp.einsum('hqk,khd->qhd', attend, split_heads[2], precision=lax.Precision.HIGHEST).reshape(length, HEADS * HEAD_DIM)
    mixture = low(low_back(mixture))
    hidden = token_rows + low_back(matmul(mixture, merge_proj)) + vector_rows[2]
    normed_mlp = low(layer_norm(hidden, vector_rows[3], vector_rows[4]))
    expanded = low_back(matmul(normed_mlp, expand_proj))
    active = low(gelu_tanh(expanded))
    return hidden + low_back(matmul(active, shrink_proj)) + vector_rows[5]

def frame_loss(params, frame_rows, code_ids, clip_weight, cotangent):
    head_set, merge_set, expand_set, shrink_set, vector_set, encode_set, code_set, decode_set = [low(weight_array) for weight_array in params]
    encoded = block_forward(frame_rows, head_set[0], merge_set[0], expand_set[0], shrink_set[0], vector_set[0:6])
    normed = low(layer_norm(encoded, vector_set[12], vector_set[13]))
    latent = unit_rows(matmul(normed, encode_set))
    chosen = unit_rows(jnp.take(code_set, code_ids, axis=0))
    offset = latent - chosen
    commit = COMMIT_WEIGHT * clip_weight * jnp.sum(offset * offset)
    started = matmul(low(chosen), decode_set) + vector_set[14]
    decoded = block_forward(started, head_set[1], merge_set[1], expand_set[1], shrink_set[1], vector_set[6:12])
    return (jnp.sum(decoded * cotangent) + commit, decoded)

def adam_update(master, gradient, first_state, second_state, step_rate, decay_rate):
    mean_new = MEAN_DECAY * first_state + (1.0 - MEAN_DECAY) * gradient
    square_new = SQUARE_DECAY * second_state + (1.0 - SQUARE_DECAY) * gradient * gradient
    normal_step = mean_new / (1.0 - MEAN_DECAY ** STEP) / (jnp.sqrt(square_new / (1.0 - SQUARE_DECAY ** STEP)) + ADAM_EPS)
    updated = master - step_rate * (normal_step + decay_rate * master)
    return (mean_new, square_new, updated, updated.astype(jnp.bfloat16))

def reference(frames, codes, clip_frames, out_cotangent, heads_weight, merge_weight, expand_weight, shrink_weight, vectors, encode_weight, codebook, decode_weight, heads_first, merge_first, expand_first, shrink_first, vectors_first, encode_first, codebook_first, decode_first, heads_second, merge_second, expand_second, shrink_second, vectors_second, encode_second, codebook_second, decode_second):
    params = (heads_weight, merge_weight, expand_weight, shrink_weight, vectors, encode_weight, codebook, decode_weight)
    firsts = (heads_first, merge_first, expand_first, shrink_first, vectors_first, encode_first, codebook_first, decode_first)
    seconds = (heads_second, merge_second, expand_second, shrink_second, vectors_second, encode_second, codebook_second, decode_second)
    clip_ends = jnp.cumsum(clip_frames).astype(jnp.int32)
    frame_ids = jnp.arange(FRAMES, dtype=jnp.int32)
    clip_ids = lax.optimization_barrier(jnp.sum((clip_ends[None, :] <= frame_ids[:, None]).astype(jnp.int32), axis=1)).astype(jnp.int32)
    frame_weights = 1.0 / jnp.take(clip_frames, clip_ids).astype(jnp.float32)

    def one_frame(totals, inputs):
        frame_rows, code_ids, clip_weight, cotangent = inputs
        loss_value, pullback, decoded = jax.vjp(lambda weights, rows_in: frame_loss(weights, rows_in, code_ids, clip_weight, cotangent), params, frame_rows, has_aux=True)
        weight_grads, frame_grad = pullback(jnp.ones((), jnp.float32))
        totals = tuple((running + addition for running, addition in zip(totals, weight_grads)))
        return (totals, (decoded, frame_grad))
    initial = tuple((jnp.zeros_like(weight_array) for weight_array in params))
    totals, (decoded_all, frame_grads) = lax.scan(one_frame, initial, (frames.astype(jnp.float32), codes, frame_weights, out_cotangent.astype(jnp.float32)))
    squares = jnp.zeros((), jnp.float32)
    for gradient in totals:
        squares = squares + jnp.sum(gradient * gradient)
    norm_before = jnp.sqrt(squares)
    factor = MAX_NORM / jnp.maximum(norm_before, MAX_NORM)
    updates = [adam_update(params[member], totals[member] * factor, firsts[member], seconds[member], RATES[member], DECAYS[member]) for member in range(8)]
    return (decoded_all, frame_grads, norm_before, updates[0][0], updates[0][1], updates[0][2], updates[0][3], updates[1][0], updates[1][1], updates[1][2], updates[1][3], updates[2][0], updates[2][1], updates[2][2], updates[2][3], updates[3][0], updates[3][1], updates[3][2], updates[3][3], updates[4][0], updates[4][1], updates[4][2], updates[4][3], updates[5][0], updates[5][1], updates[5][2], updates[5][3], updates[6][0], updates[6][1], updates[6][2], updates[6][3], updates[7][0], updates[7][1], updates[7][2], updates[7][3])
```

```python
import jax
import jax.numpy as jnp
from jax import lax
from jax.sharding import PartitionSpec as P

HEAD_DIM = 64
STEP = 10


EPS_NORM = 1e-05
EPS_UNIT = 1e-06
COMMIT_WEIGHT = 100.0
MAX_NORM = 1.0
MEAN_DECAY = 0.9
SQUARE_DECAY = 0.95
ADAM_EPS = 1e-08
RATES = (0.1, 0.5, 0.1, 0.05, 1.0, 0.1, 1.0, 0.3)
DECAYS = (0.1, 0.1, 0.1, 0.1, 0.0, 0.1, 0.1, 0.1)


def layer_norm(token_rows, gain_row, shift_row):
    center = token_rows - jnp.mean(token_rows, axis=-1, keepdims=True)
    spread = jnp.mean(center * center, axis=-1, keepdims=True)
    return center * lax.rsqrt(spread + EPS_NORM) * gain_row + shift_row


def unit_rows(vectors_in):
    return vectors_in * lax.rsqrt(
        jnp.sum(vectors_in * vectors_in, axis=-1, keepdims=True) + EPS_UNIT
    )


def gelu_tanh(values):
    return jax.nn.gelu(values, approximate=True)


def fast_dot(formula, first_arg, second_arg):
    return jnp.einsum(formula, first_arg, second_arg, preferred_element_type=jnp.float32)


def exact_dot(formula, first_arg, second_arg):
    return jnp.einsum(
        formula,
        first_arg,
        second_arg,
        precision=lax.Precision.HIGHEST,
        preferred_element_type=jnp.float32,
    )


def attend_forward(projected, block_rows):
    length = projected.shape[1]
    head_count = projected.shape[2] // HEAD_DIM
    queries = projected[0].reshape(length, head_count, HEAD_DIM)
    keys_all = projected[1].reshape(length, head_count, HEAD_DIM)
    values_all = projected[2].reshape(length, head_count, HEAD_DIM)
    outputs = []
    log_parts = []
    for first_row in range(0, length, block_rows):
        query_block = queries[first_row : first_row + block_rows]
        scores = fast_dot("qhd,khd->hqk", query_block, keys_all) * HEAD_DIM ** (-0.5)
        top_score = jnp.max(scores, axis=-1, keepdims=True)
        exponent = jnp.exp(scores - top_score)
        totals = jnp.sum(exponent, axis=-1, keepdims=True)
        attend = (exponent / totals).astype(jnp.bfloat16)
        block_out = fast_dot("hqk,khd->qhd", attend, values_all).astype(jnp.bfloat16)
        outputs.append(block_out.reshape(block_rows, head_count * HEAD_DIM))
        log_parts.append((top_score + jnp.log(totals))[..., 0])
    return (jnp.concatenate(outputs, 0), jnp.concatenate(log_parts, 1))


def attend_backward(projected, log_sums, dmixture, block_rows):
    length = projected.shape[1]
    head_count = projected.shape[2] // HEAD_DIM
    queries = projected[0].reshape(length, head_count, HEAD_DIM)
    keys_all = projected[1].reshape(length, head_count, HEAD_DIM)
    values_all = projected[2].reshape(length, head_count, HEAD_DIM)
    dmix_heads = dmixture.reshape(length, head_count, HEAD_DIM)
    scale = HEAD_DIM ** (-0.5)
    dkeys_all = jnp.zeros((length, head_count, HEAD_DIM), jnp.float32)
    dvalues = jnp.zeros((length, head_count, HEAD_DIM), jnp.float32)
    dqueries = []
    for first_row in range(0, length, block_rows):
        query_block = queries[first_row : first_row + block_rows]
        dmix_block = dmix_heads[first_row : first_row + block_rows]
        scores = fast_dot("qhd,khd->hqk", query_block, keys_all) * scale
        attend = jnp.exp(scores - log_sums[:, first_row : first_row + block_rows, None])
        dvalues = dvalues + fast_dot("hqk,qhd->khd", attend.astype(jnp.bfloat16), dmix_block)
        dattend = fast_dot("qhd,khd->hqk", dmix_block, values_all)
        inner_sum = jnp.sum(attend * dattend, axis=-1, keepdims=True)
        dscores = (attend * (dattend - inner_sum)).astype(jnp.bfloat16)
        dqueries.append(fast_dot("hqk,khd->qhd", dscores, keys_all) * scale)
        dkeys_all = dkeys_all + fast_dot("hqk,qhd->khd", dscores, query_block) * scale
    width = head_count * HEAD_DIM
    stacked = jnp.stack(
        [
            jnp.concatenate(dqueries, 0).reshape(length, width),
            dkeys_all.reshape(length, width),
            dvalues.reshape(length, width),
        ]
    )
    return stacked.astype(jnp.bfloat16)


def block_forward(token_rows, weight_set, vector_rows, block_rows):
    head_proj, merge_proj, expand_proj, shrink_proj = weight_set
    normed = layer_norm(token_rows, vector_rows[0], vector_rows[1]).astype(jnp.bfloat16)
    projected = fast_dot("td,cde->cte", normed, head_proj).astype(jnp.bfloat16)
    mixture, log_sums = attend_forward(projected, block_rows)
    hidden = token_rows + fast_dot("te,de->td", mixture, merge_proj) + vector_rows[2]
    normed_mlp = layer_norm(hidden, vector_rows[3], vector_rows[4]).astype(jnp.bfloat16)
    expanded = fast_dot("td,df->tf", normed_mlp, expand_proj)
    active = gelu_tanh(expanded).astype(jnp.bfloat16)
    output = hidden + fast_dot("tf,df->td", active, shrink_proj) + vector_rows[5]
    kept_values = (
        token_rows,
        hidden,
        normed,
        normed_mlp,
        projected,
        mixture,
        log_sums,
        expanded,
        active,
    )
    return (output, kept_values)


def block_backward(kept_values, grad_out, weight_set, vector_rows, block_rows):
    head_proj, merge_proj, expand_proj, shrink_proj = weight_set
    (
        token_rows,
        hidden,
        normed,
        normed_mlp,
        projected,
        mixture,
        log_sums,
        expanded,
        active,
    ) = kept_values
    grad_low = grad_out.astype(jnp.bfloat16)
    dshrink = fast_dot("td,tf->df", grad_low, active)
    dactive = fast_dot("td,df->tf", grad_low, shrink_proj)
    dexpanded = jax.vjp(gelu_tanh, expanded)[1](dactive)[0].astype(jnp.bfloat16)
    dexpand = fast_dot("td,tf->df", normed_mlp, dexpanded)
    dnormed_mlp = fast_dot("tf,df->td", dexpanded, expand_proj)
    pullback_mlp = jax.vjp(layer_norm, hidden, vector_rows[3], vector_rows[4])[1]
    dhidden_norm, gain_grad_mlp, shift_grad_mlp = pullback_mlp(dnormed_mlp)
    dhidden = grad_out + dhidden_norm
    dhidden_low = dhidden.astype(jnp.bfloat16)
    dmerge = fast_dot("td,te->de", dhidden_low, mixture)
    dmixture = fast_dot("td,de->te", dhidden_low, merge_proj).astype(jnp.bfloat16)
    dprojected = attend_backward(projected, log_sums, dmixture, block_rows)
    dheads = fast_dot("td,cte->cde", normed, dprojected)
    dnormed = fast_dot("cte,cde->td", dprojected, head_proj)
    pullback_attn = jax.vjp(layer_norm, token_rows, vector_rows[0], vector_rows[1])[1]
    dtoken_norm, gain_grad, shift_grad = pullback_attn(dnormed)
    dvectors = jnp.stack(
        [
            gain_grad,
            shift_grad,
            jnp.sum(dhidden, axis=0),
            gain_grad_mlp,
            shift_grad_mlp,
            jnp.sum(grad_out, axis=0),
        ]
    )
    return (dhidden + dtoken_norm, (dheads, dmerge, dexpand, dshrink), dvectors)


def quantize_forward(encoded, code_ids, small_set):
    vector_set, encode_low, codebook_low, decode_low = small_set
    normed = layer_norm(encoded, vector_set[12], vector_set[13]).astype(jnp.bfloat16)
    latent_raw = fast_dot("td,dc->tc", normed, encode_low)
    latent = unit_rows(latent_raw)
    entries = jnp.take(codebook_low, code_ids, axis=0).astype(jnp.float32)
    chosen = unit_rows(entries)
    chosen_low = chosen.astype(jnp.bfloat16)
    started = fast_dot("tc,cd->td", chosen_low, decode_low) + vector_set[14]
    return (started, (encoded, normed, latent_raw, latent, entries, chosen, chosen_low))


def quantize_backward(kept_values, dstarted, code_ids, clip_weight, small_set):
    vector_set, encode_low, codebook_low, decode_low = small_set
    encoded, normed, latent_raw, latent, entries, chosen, chosen_low = kept_values
    dstart_bias = jnp.sum(dstarted, axis=0)
    ddecode = exact_dot("tc,td->cd", chosen_low.astype(jnp.float32), dstarted)
    pulled = 2.0 * COMMIT_WEIGHT * clip_weight * (latent - chosen)
    dchosen = exact_dot("td,cd->tc", dstarted, decode_low.astype(jnp.float32)) - pulled
    dentries = jax.vjp(unit_rows, entries)[1](dchosen)[0]
    dcodebook = jax.ops.segment_sum(dentries, code_ids, num_segments=codebook_low.shape[0])
    dlatent_raw = jax.vjp(unit_rows, latent_raw)[1](pulled)[0]
    dencode = exact_dot("td,tc->dc", normed.astype(jnp.float32), dlatent_raw)
    dnormed = exact_dot("tc,dc->td", dlatent_raw, encode_low.astype(jnp.float32))
    pullback = jax.vjp(layer_norm, encoded, vector_set[12], vector_set[13])[1]
    dencoded, gain_grad, shift_grad = pullback(dnormed)
    return (
        dencoded,
        (jnp.stack([gain_grad, shift_grad, dstart_bias]), dencode, dcodebook, ddecode),
    )


def pack_shard(heads, merge, expand, shrink):
    parts = [heads[0], heads[1], heads[2], merge.T, expand, shrink.T]
    return jnp.concatenate([part.astype(jnp.bfloat16) for part in parts], axis=1)


def unpack_shard(rows):
    width = rows.shape[1] // 12
    heads = jnp.stack([rows[:, 0:width], rows[:, width : 2 * width], rows[:, 2 * width : 3 * width]])
    merge = rows[:, 3 * width : 4 * width].T
    expand = rows[:, 4 * width : 8 * width]
    shrink = rows[:, 8 * width : 12 * width].T
    return (heads, merge, expand, shrink)


def gather_block(rows):
    gathered = lax.all_gather(rows, ("dp", "tensor"), axis=0, tiled=False)
    split = gathered.reshape(lax.axis_size("dp"), 2, rows.shape[0], rows.shape[1])
    return split.transpose(1, 0, 2, 3).reshape(2, -1, rows.shape[1])


def weight_views(packed):
    width = packed.shape[2] // 12

    def join(first, last):
        return jnp.concatenate([packed[0, :, first:last], packed[1, :, first:last]], axis=1)

    heads = jnp.stack([join(part * width, (part + 1) * width) for part in range(3)])
    merge = join(3 * width, 4 * width)
    expand = join(4 * width, 8 * width)
    shrink = join(8 * width, 12 * width)
    return (heads, merge, expand, shrink)


def pack_grads(heads, merge, expand, shrink):
    def halves(array):
        half = array.shape[1] // 2
        return jnp.stack([array[:, :half], array[:, half:]])

    parts = [halves(part) for part in (heads[0], heads[1], heads[2], merge, expand, shrink)]
    return jnp.concatenate(parts, axis=2).astype(jnp.bfloat16)


def reduce_block(packed):
    dp_size = lax.axis_size("dp")
    split = packed.reshape(2, dp_size, -1, packed.shape[2]).transpose(1, 0, 2, 3)
    split = split.reshape(-1, packed.shape[2])
    return lax.psum_scatter(split, ("dp", "tensor"), scatter_dimension=0, tiled=True).astype(jnp.float32)


def swap_half(rows):
    return lax.ppermute(rows, "tensor", [(0, 1), (1, 0)])


def pick_frame(pair, index):
    return lax.dynamic_index_in_dim(pair, index, axis=0, keepdims=False)


def join_frame(pair):
    mine = lax.axis_index("tensor")
    return jnp.concatenate([pick_frame(pair, mine), swap_half(pick_frame(pair, 1 - mine))], axis=0)


def split_frame(rows):
    mine = lax.axis_index("tensor")
    half = rows.shape[0] // 2
    other = swap_half(rows[half:].astype(jnp.bfloat16)).astype(jnp.float32)
    own = rows[:half]
    return jnp.where(mine == 0, jnp.stack([own, other]), jnp.stack([other, own]))


def adam_update(master, gradient, first_state, second_state, step_rate, decay_rate):
    mean_new = MEAN_DECAY * first_state + (1.0 - MEAN_DECAY) * gradient
    square_new = SQUARE_DECAY * second_state + (1.0 - SQUARE_DECAY) * gradient * gradient
    normal_step = (
        mean_new
        / (1.0 - MEAN_DECAY**STEP)
        / (jnp.sqrt(square_new / (1.0 - SQUARE_DECAY**STEP)) + ADAM_EPS)
    )
    updated = master - step_rate * (normal_step + decay_rate * master)
    return (mean_new, square_new, updated, updated.astype(jnp.bfloat16))


def local(
    frames,
    codes,
    clip_frames,
    out_cotangent,
    heads_weight,
    merge_weight,
    expand_weight,
    shrink_weight,
    vectors,
    encode_weight,
    codebook,
    decode_weight,
    heads_first,
    merge_first,
    expand_first,
    shrink_first,
    vectors_first,
    encode_first,
    codebook_first,
    decode_first,
    heads_second,
    merge_second,
    expand_second,
    shrink_second,
    vectors_second,
    encode_second,
    codebook_second,
    decode_second,
):
    own_rows = [
        pack_shard(heads_weight[b], merge_weight[b], expand_weight[b], shrink_weight[b])
        for b in range(2)
    ]
    small_parts = [vectors, encode_weight, codebook, decode_weight]
    small_flat = jnp.concatenate([part.astype(jnp.bfloat16).reshape(-1) for part in small_parts])
    small_all = lax.all_gather(small_flat, ("dp", "tensor"), axis=0, tiled=False)
    small_low = []
    offset = 0
    for part, cut_dim in zip(small_parts, (1, 0, 0, 1)):
        piece = small_all[:, offset : offset + part.size].reshape((-1,) + part.shape)
        offset += part.size
        if cut_dim == 1:
            piece = piece.transpose(1, 0, 2).reshape(part.shape[0], -1)
        else:
            piece = piece.reshape(-1, part.shape[1])
        small_low.append(piece)
    vector_set = small_low[0].astype(jnp.float32)
    small_set = (vector_set, small_low[1], small_low[2], small_low[3])
    frame_rows = join_frame(frames).astype(jnp.float32)
    code_ids = join_frame(codes)
    cotangent = join_frame(out_cotangent).astype(jnp.float32)
    weight_sets = [weight_views(gather_block(rows)) for rows in own_rows]
    block_rows = frame_rows.shape[0] // 2
    frame_id = lax.axis_index("dp") * frames.shape[0] + lax.axis_index("tensor")
    clip_ends = jnp.cumsum(clip_frames)
    clip_id = jnp.sum((clip_ends <= frame_id).astype(jnp.int32))
    clip_slots = jnp.arange(clip_frames.shape[0], dtype=jnp.int32)
    clip_count = jnp.sum(jnp.where(clip_slots == clip_id, clip_frames, 0))
    clip_weight = 1.0 / clip_count.astype(jnp.float32)
    encoded, kept_encoder = block_forward(
        frame_rows, weight_sets[0], vector_set[0:6], block_rows
    )
    started, kept_quant = quantize_forward(encoded, code_ids, small_set)
    decoded, kept_decoder = block_forward(started, weight_sets[1], vector_set[6:12], block_rows)
    dstarted, decoder_grads, decoder_vectors = block_backward(
        kept_decoder, cotangent, weight_sets[1], vector_set[6:12], block_rows
    )
    dencoded, quant_grads = quantize_backward(
        kept_quant, dstarted, code_ids, clip_weight, small_set
    )
    dframe, encoder_grads, encoder_vectors = block_backward(
        kept_encoder, dencoded, weight_sets[0], vector_set[0:6], block_rows
    )
    decoded_all = split_frame(decoded)
    frame_grads = split_frame(dframe)
    reduced = [
        unpack_shard(reduce_block(pack_grads(*grads))) for grads in (encoder_grads, decoder_grads)
    ]
    block_grads = [jnp.stack([first, second]) for first, second in zip(*reduced)]
    device_count = lax.axis_size("dp") * lax.axis_size("tensor")
    dvectors = jnp.concatenate([encoder_vectors, decoder_vectors, quant_grads[0]], axis=0)
    small_new = (dvectors, quant_grads[1], quant_grads[2], quant_grads[3])
    columns = []
    for gradient, part, cut_dim in zip(small_new, small_parts, (1, 0, 0, 1)):
        if cut_dim == 1:
            gradient = gradient.reshape(part.shape[0], device_count, -1).transpose(1, 0, 2)
        columns.append(gradient.reshape(device_count, -1))
    small_sum = lax.psum_scatter(
        jnp.concatenate(columns, axis=1), ("dp", "tensor"), scatter_dimension=0, tiled=True
    )
    small_sum = small_sum.reshape(-1)
    small_grads = []
    offset = 0
    for part in small_parts:
        small_grads.append(small_sum[offset : offset + part.size].reshape(part.shape))
        offset += part.size
    gradients = tuple(block_grads) + tuple(small_grads)
    local_squares = jnp.zeros((), jnp.float32)
    for gradient in gradients:
        local_squares = local_squares + jnp.sum(gradient * gradient)
    norm_before = jnp.sqrt(lax.psum(local_squares, ("dp", "tensor")))
    factor = MAX_NORM / jnp.maximum(norm_before, MAX_NORM)
    masters = (
        heads_weight,
        merge_weight,
        expand_weight,
        shrink_weight,
        vectors,
        encode_weight,
        codebook,
        decode_weight,
    )
    firsts = (
        heads_first,
        merge_first,
        expand_first,
        shrink_first,
        vectors_first,
        encode_first,
        codebook_first,
        decode_first,
    )
    seconds = (
        heads_second,
        merge_second,
        expand_second,
        shrink_second,
        vectors_second,
        encode_second,
        codebook_second,
        decode_second,
    )
    updates = [
        adam_update(
            masters[member],
            gradients[member] * factor,
            firsts[member],
            seconds[member],
            RATES[member],
            DECAYS[member],
        )
        for member in range(8)
    ]
    return (
        decoded_all,
        frame_grads,
        norm_before,
        updates[0][0],
        updates[0][1],
        updates[0][2],
        updates[0][3],
        updates[1][0],
        updates[1][1],
        updates[1][2],
        updates[1][3],
        updates[2][0],
        updates[2][1],
        updates[2][2],
        updates[2][3],
        updates[3][0],
        updates[3][1],
        updates[3][2],
        updates[3][3],
        updates[4][0],
        updates[4][1],
        updates[4][2],
        updates[4][3],
        updates[5][0],
        updates[5][1],
        updates[5][2],
        updates[5][3],
        updates[6][0],
        updates[6][1],
        updates[6][2],
        updates[6][3],
        updates[7][0],
        updates[7][1],
        updates[7][2],
        updates[7][3],
    )


def solution(mesh):
    return jax.shard_map(
        local,
        mesh=mesh,
        in_specs=(
            P("dp", "tensor", None),
            P("dp", "tensor"),
            P(),
            P("dp", "tensor", None),
            P(None, None, "dp", "tensor"),
            P(None, "tensor", "dp"),
            P(None, "dp", "tensor"),
            P(None, "tensor", "dp"),
            P(None, ("dp", "tensor")),
            P(("dp", "tensor"), None),
            P(("dp", "tensor"), None),
            P(None, ("dp", "tensor")),
            P(None, None, "dp", "tensor"),
            P(None, "tensor", "dp"),
            P(None, "dp", "tensor"),
            P(None, "tensor", "dp"),
            P(None, ("dp", "tensor")),
            P(("dp", "tensor"), None),
            P(("dp", "tensor"), None),
            P(None, ("dp", "tensor")),
            P(None, None, "dp", "tensor"),
            P(None, "tensor", "dp"),
            P(None, "dp", "tensor"),
            P(None, "tensor", "dp"),
            P(None, ("dp", "tensor")),
            P(("dp", "tensor"), None),
            P(("dp", "tensor"), None),
            P(None, ("dp", "tensor")),
        ),
        out_specs=(
            P("dp", "tensor", None),
            P("dp", "tensor", None),
            P(),
            P(None, None, "dp", "tensor"),
            P(None, None, "dp", "tensor"),
            P(None, None, "dp", "tensor"),
            P(None, None, "dp", "tensor"),
            P(None, "tensor", "dp"),
            P(None, "tensor", "dp"),
            P(None, "tensor", "dp"),
            P(None, "tensor", "dp"),
            P(None, "dp", "tensor"),
            P(None, "dp", "tensor"),
            P(None, "dp", "tensor"),
            P(None, "dp", "tensor"),
            P(None, "tensor", "dp"),
            P(None, "tensor", "dp"),
            P(None, "tensor", "dp"),
            P(None, "tensor", "dp"),
            P(None, ("dp", "tensor")),
            P(None, ("dp", "tensor")),
            P(None, ("dp", "tensor")),
            P(None, ("dp", "tensor")),
            P(("dp", "tensor"), None),
            P(("dp", "tensor"), None),
            P(("dp", "tensor"), None),
            P(("dp", "tensor"), None),
            P(("dp", "tensor"), None),
            P(("dp", "tensor"), None),
            P(("dp", "tensor"), None),
            P(("dp", "tensor"), None),
            P(None, ("dp", "tensor")),
            P(None, ("dp", "tensor")),
            P(None, ("dp", "tensor")),
            P(None, ("dp", "tensor")),
        ),
        check_vma=False,
    )
```

```python
import functools

import jax
import jax.numpy as jnp
from jax import lax
from jax.experimental import pallas as pl
from jax.experimental.pallas import tpu as pltpu
from jax.sharding import PartitionSpec as P

HEAD_DIM = 64
STEP = 10


EPS_NORM = 1e-05
EPS_UNIT = 1e-06
COMMIT_WEIGHT = 100.0
MAX_NORM = 1.0
MEAN_DECAY = 0.9
SQUARE_DECAY = 0.95
ADAM_EPS = 1e-08
RATES = (0.1, 0.5, 0.1, 0.05, 1.0, 0.1, 1.0, 0.3)
DECAYS = (0.1, 0.1, 0.1, 0.1, 0.0, 0.1, 0.1, 0.1)


def layer_norm(token_rows, gain_row, shift_row):
    center = token_rows - jnp.mean(token_rows, axis=-1, keepdims=True)
    spread = jnp.mean(center * center, axis=-1, keepdims=True)
    return center * lax.rsqrt(spread + EPS_NORM) * gain_row + shift_row


def unit_rows(vectors_in):
    return vectors_in * lax.rsqrt(
        jnp.sum(vectors_in * vectors_in, axis=-1, keepdims=True) + EPS_UNIT
    )


def gelu_tanh(values):
    return jax.nn.gelu(values, approximate=True)


def fast_dot(formula, first_arg, second_arg):
    return jnp.einsum(formula, first_arg, second_arg, preferred_element_type=jnp.float32)


def exact_dot(formula, first_arg, second_arg):
    return jnp.einsum(
        formula,
        first_arg,
        second_arg,
        precision=lax.Precision.HIGHEST,
        preferred_element_type=jnp.float32,
    )


def attend_forward(projected, block_rows):
    length = projected.shape[1]
    head_count = projected.shape[2] // HEAD_DIM
    queries = projected[0].reshape(length, head_count, HEAD_DIM)
    keys_all = projected[1].reshape(length, head_count, HEAD_DIM)
    values_all = projected[2].reshape(length, head_count, HEAD_DIM)
    outputs = []
    log_parts = []
    for first_row in range(0, length, block_rows):
        query_block = queries[first_row : first_row + block_rows]
        scores = fast_dot("qhd,khd->hqk", query_block, keys_all) * HEAD_DIM ** (-0.5)
        top_score = jnp.max(scores, axis=-1, keepdims=True)
        exponent = jnp.exp(scores - top_score)
        totals = jnp.sum(exponent, axis=-1, keepdims=True)
        attend = (exponent / totals).astype(jnp.bfloat16)
        block_out = fast_dot("hqk,khd->qhd", attend, values_all).astype(jnp.bfloat16)
        outputs.append(block_out.reshape(block_rows, head_count * HEAD_DIM))
        log_parts.append((top_score + jnp.log(totals))[..., 0])
    return (jnp.concatenate(outputs, 0), jnp.concatenate(log_parts, 1))


def attend_backward(projected, log_sums, dmixture, block_rows):
    length = projected.shape[1]
    head_count = projected.shape[2] // HEAD_DIM
    queries = projected[0].reshape(length, head_count, HEAD_DIM)
    keys_all = projected[1].reshape(length, head_count, HEAD_DIM)
    values_all = projected[2].reshape(length, head_count, HEAD_DIM)
    dmix_heads = dmixture.reshape(length, head_count, HEAD_DIM)
    scale = HEAD_DIM ** (-0.5)
    dkeys_all = jnp.zeros((length, head_count, HEAD_DIM), jnp.float32)
    dvalues = jnp.zeros((length, head_count, HEAD_DIM), jnp.float32)
    dqueries = []
    for first_row in range(0, length, block_rows):
        query_block = queries[first_row : first_row + block_rows]
        dmix_block = dmix_heads[first_row : first_row + block_rows]
        scores = fast_dot("qhd,khd->hqk", query_block, keys_all) * scale
        attend = jnp.exp(scores - log_sums[:, first_row : first_row + block_rows, None])
        dvalues = dvalues + fast_dot("hqk,qhd->khd", attend.astype(jnp.bfloat16), dmix_block)
        dattend = fast_dot("qhd,khd->hqk", dmix_block, values_all)
        inner_sum = jnp.sum(attend * dattend, axis=-1, keepdims=True)
        dscores = (attend * (dattend - inner_sum)).astype(jnp.bfloat16)
        dqueries.append(fast_dot("hqk,khd->qhd", dscores, keys_all) * scale)
        dkeys_all = dkeys_all + fast_dot("hqk,qhd->khd", dscores, query_block) * scale
    width = head_count * HEAD_DIM
    stacked = jnp.stack(
        [
            jnp.concatenate(dqueries, 0).reshape(length, width),
            dkeys_all.reshape(length, width),
            dvalues.reshape(length, width),
        ]
    )
    return stacked.astype(jnp.bfloat16)


def block_forward(token_rows, weight_set, vector_rows, block_rows):
    head_proj, merge_proj, expand_proj, shrink_proj = weight_set
    normed = layer_norm(token_rows, vector_rows[0], vector_rows[1]).astype(jnp.bfloat16)
    projected = fast_dot("td,cde->cte", normed, head_proj).astype(jnp.bfloat16)
    mixture, log_sums = attend_forward(projected, block_rows)
    hidden = token_rows + fast_dot("te,de->td", mixture, merge_proj) + vector_rows[2]
    normed_mlp = layer_norm(hidden, vector_rows[3], vector_rows[4]).astype(jnp.bfloat16)
    expanded = fast_dot("td,df->tf", normed_mlp, expand_proj)
    active = gelu_tanh(expanded).astype(jnp.bfloat16)
    output = hidden + fast_dot("tf,df->td", active, shrink_proj) + vector_rows[5]
    kept_values = (
        token_rows,
        hidden,
        normed,
        normed_mlp,
        projected,
        mixture,
        log_sums,
        expanded,
        active,
    )
    return (output, kept_values)


def block_backward(kept_values, grad_out, weight_set, vector_rows, block_rows):
    head_proj, merge_proj, expand_proj, shrink_proj = weight_set
    (
        token_rows,
        hidden,
        normed,
        normed_mlp,
        projected,
        mixture,
        log_sums,
        expanded,
        active,
    ) = kept_values
    grad_low = grad_out.astype(jnp.bfloat16)
    dshrink = fast_dot("td,tf->df", grad_low, active)
    dactive = fast_dot("td,df->tf", grad_low, shrink_proj)
    dexpanded = jax.vjp(gelu_tanh, expanded)[1](dactive)[0].astype(jnp.bfloat16)
    dexpand = fast_dot("td,tf->df", normed_mlp, dexpanded)
    dnormed_mlp = fast_dot("tf,df->td", dexpanded, expand_proj)
    pullback_mlp = jax.vjp(layer_norm, hidden, vector_rows[3], vector_rows[4])[1]
    dhidden_norm, gain_grad_mlp, shift_grad_mlp = pullback_mlp(dnormed_mlp)
    dhidden = grad_out + dhidden_norm
    dhidden_low = dhidden.astype(jnp.bfloat16)
    dmerge = fast_dot("td,te->de", dhidden_low, mixture)
    dmixture = fast_dot("td,de->te", dhidden_low, merge_proj).astype(jnp.bfloat16)
    dprojected = attend_backward(projected, log_sums, dmixture, block_rows)
    dheads = fast_dot("td,cte->cde", normed, dprojected)
    dnormed = fast_dot("cte,cde->td", dprojected, head_proj)
    pullback_attn = jax.vjp(layer_norm, token_rows, vector_rows[0], vector_rows[1])[1]
    dtoken_norm, gain_grad, shift_grad = pullback_attn(dnormed)
    dvectors = jnp.stack(
        [
            gain_grad,
            shift_grad,
            jnp.sum(dhidden, axis=0),
            gain_grad_mlp,
            shift_grad_mlp,
            jnp.sum(grad_out, axis=0),
        ]
    )
    return (dhidden + dtoken_norm, (dheads, dmerge, dexpand, dshrink), dvectors)


def quantize_forward(encoded, code_ids, small_set):
    vector_set, encode_low, codebook_low, decode_low = small_set
    normed = layer_norm(encoded, vector_set[12], vector_set[13]).astype(jnp.bfloat16)
    latent_raw = fast_dot("td,dc->tc", normed, encode_low)
    latent = unit_rows(latent_raw)
    entries = jnp.take(codebook_low, code_ids, axis=0).astype(jnp.float32)
    chosen = unit_rows(entries)
    chosen_low = chosen.astype(jnp.bfloat16)
    started = fast_dot("tc,cd->td", chosen_low, decode_low) + vector_set[14]
    return (started, (encoded, normed, latent_raw, latent, entries, chosen, chosen_low))


def quantize_backward(kept_values, dstarted, code_ids, clip_weight, small_set):
    vector_set, encode_low, codebook_low, decode_low = small_set
    encoded, normed, latent_raw, latent, entries, chosen, chosen_low = kept_values
    dstart_bias = jnp.sum(dstarted, axis=0)
    ddecode = exact_dot("tc,td->cd", chosen_low.astype(jnp.float32), dstarted)
    pulled = 2.0 * COMMIT_WEIGHT * clip_weight * (latent - chosen)
    dchosen = exact_dot("td,cd->tc", dstarted, decode_low.astype(jnp.float32)) - pulled
    dentries = jax.vjp(unit_rows, entries)[1](dchosen)[0]
    dcodebook = jax.ops.segment_sum(dentries, code_ids, num_segments=codebook_low.shape[0])
    dlatent_raw = jax.vjp(unit_rows, latent_raw)[1](pulled)[0]
    dencode = exact_dot("td,tc->dc", normed.astype(jnp.float32), dlatent_raw)
    dnormed = exact_dot("tc,dc->td", dlatent_raw, encode_low.astype(jnp.float32))
    pullback = jax.vjp(layer_norm, encoded, vector_set[12], vector_set[13])[1]
    dencoded, gain_grad, shift_grad = pullback(dnormed)
    return (
        dencoded,
        (jnp.stack([gain_grad, shift_grad, dstart_bias]), dencode, dcodebook, ddecode),
    )


MESH = pl.DeviceIdType.MESH


def remote(src, dst, sems, slot, target):
    send, recv = sems
    return pltpu.make_async_remote_copy(
        src_ref=src,
        dst_ref=dst,
        send_sem=send.at[slot],
        recv_sem=recv.at[slot],
        device_id=target,
        device_id_type=MESH,
    )


def coordinates():
    dp_index = lax.axis_index("dp")
    y = lax.axis_index("tensor")
    return dp_index // 4, (dp_index // 2) % 2, dp_index % 2, y


def partners(z, x, c, y):
    along_z = [(((z + step) % 4) * 4 + x * 2 + c, y) for step in (1, 2, 3)]
    along_x = (z * 4 + (1 - x) * 2 + c, y)
    along_y = (z * 4 + x * 2 + c, 1 - y)
    along_core = (z * 4 + x * 2 + (1 - c), y)
    return along_z, along_x, along_y, along_core


def greet(targets):
    barrier = pltpu.get_barrier_semaphore()
    for target in targets:
        pl.semaphore_signal(barrier, inc=1, device_id=target, device_id_type=MESH)
    pl.semaphore_wait(barrier, len(targets))


def gather_kernel(count, orders, *refs):
    shards = refs[:count]
    frames, cotangent, codes = refs[count : count + 3]
    outs = refs[count + 3 : 2 * count + 3]
    frame_out, cotangent_out, codes_out = refs[2 * count + 3 : 2 * count + 6]
    local_sems, send_sems, recv_sems, swap_send, swap_recv = refs[2 * count + 6 :]
    z, x, c, y = coordinates()
    along_z, along_x, along_y, along_core = partners(z, x, c, y)
    greet(along_z + [along_x, along_y, along_core])
    sems, swaps = (send_sems, recv_sems), (swap_send, swap_recv)
    pending = []
    for slot, (source, target) in enumerate(
        ((codes, codes_out), (frames, frame_out), (cotangent, cotangent_out))
    ):
        copy = remote(source.at[1 - y], target, swaps, slot, along_y)
        pending.append(copy)
        copy.start()
    first, second, third, to_core = [], [], [], []
    own = []
    for i in range(count):
        slot = outs[i].at[y, z, x, c]
        copy = pltpu.make_async_copy(shards[i], slot, local_sems.at[i])
        copy.start()
        own.append(copy)
        first.append([remote(shards[i], slot, sems, (i, k), along_z[k]) for k in range(3)])
        for copy in first[i]:
            copy.start()
        by_x = orders[i] == "xy"
        column = outs[i].at[y, :, x, c]
        second.append(remote(column, column, sems, (i, 3), along_x if by_x else along_y))
        plane = outs[i].at[y, :, :, c] if by_x else outs[i].at[:, :, x, c]
        third.append(remote(plane, plane, sems, (i, 4), along_y if by_x else along_x))
        got_second = outs[i].at[y, :, 1 - x, c] if by_x else outs[i].at[1 - y, :, x, c]
        got_third = outs[i].at[1 - y, :, :, c] if by_x else outs[i].at[:, :, 1 - x, c]
        to_core.append(
            [
                remote(part, part, sems, (i, 5 + k), along_core)
                for k, part in enumerate((column, got_second, got_third))
            ]
        )
    for step in range(count + 2):
        i = step
        if i < count:
            own[i].wait()
            for copy in first[i]:
                copy.wait_recv()
            second[i].start()
            to_core[i][0].start()
        i = step - 1
        if 0 <= i < count:
            second[i].wait_recv()
            third[i].start()
            to_core[i][1].start()
        i = step - 2
        if 0 <= i < count:
            third[i].wait_recv()
            to_core[i][2].start()
    for i in range(count):
        for copy in first[i] + [second[i], third[i]]:
            copy.wait_send()
        for copy in to_core[i]:
            copy.wait()
    for copy in pending:
        copy.wait()


ORDERS = ("xy", "yx", "xy", "yx", "xy", "yx", "yx")


def gather_tuned(shards, frames, cotangent, codes):
    count = len(shards)
    any_spec = pl.BlockSpec(memory_space=pl.ANY)
    outs = [jax.ShapeDtypeStruct((2, 4, 2, 2) + s.shape, s.dtype) for s in shards]
    outs += [jax.ShapeDtypeStruct(a.shape[1:], a.dtype) for a in (frames, cotangent, codes)]
    results = pl.pallas_call(
        functools.partial(gather_kernel, count, ORDERS),
        out_shape=outs,
        in_specs=[any_spec] * (count + 3),
        out_specs=[any_spec] * (count + 3),
        scratch_shapes=[
            pltpu.SemaphoreType.DMA((count,)),
            pltpu.SemaphoreType.DMA((count, 8)),
            pltpu.SemaphoreType.DMA((count, 8)),
            pltpu.SemaphoreType.DMA((3,)),
            pltpu.SemaphoreType.DMA((3,)),
        ],
        compiler_params=pltpu.CompilerParams(collective_id=0, has_side_effects=True),
        name="gather",
    )(*shards, frames, cotangent, codes)
    full = [r.reshape(2, 16 * r.shape[4], r.shape[5]) for r in results[:count]]
    return full, results[count], results[count + 1], results[count + 2]


def reduce_kernel(count, orders, *refs):
    partial = refs[:count]
    outs = refs[count : 2 * count]
    total_out = refs[2 * count]
    scratch = refs[2 * count + 1 :]
    held = scratch[:count]
    from_core = scratch[count : 2 * count]
    from_third = scratch[2 * count : 3 * count]
    from_second = scratch[3 * count : 4 * count]
    from_first = scratch[4 * count : 5 * count]
    squares, local_sems, send_sems, recv_sems, sum_send, sum_recv = scratch[5 * count :]
    z, x, c, y = coordinates()
    along_z, along_x, along_y, along_core = partners(z, x, c, y)
    greet(along_z + [along_x, along_y, along_core])
    sems = (send_sems, recv_sems)
    own, core, third, second, first = [], [], [], [], []
    for i in range(count):
        by_x = orders[i] == "xy"
        copy = remote(partial[i].at[:, :, :, 1 - c], from_core[i], sems, (i, 0), along_core)
        copy.start()
        core.append(copy)
        copy = pltpu.make_async_copy(partial[i].at[:, :, :, c], held[i], local_sems.at[i])
        copy.start()
        own.append(copy)
        if by_x:
            third.append(remote(held[i].at[1 - y], from_third[i], sems, (i, 1), along_y))
            second.append(remote(held[i].at[y, :, 1 - x], from_second[i], sems, (i, 2), along_x))
        else:
            third.append(remote(held[i].at[:, :, 1 - x], from_third[i], sems, (i, 1), along_x))
            second.append(remote(held[i].at[1 - y, :, x], from_second[i], sems, (i, 2), along_y))
        first.append(
            [
                remote(
                    held[i].at[y, (z + k + 1) % 4, x],
                    from_first[i].at[k],
                    sems,
                    (i, 3 + k),
                    along_z[k],
                )
                for k in range(3)
            ]
        )

    def add(into, index, other, other_index):
        total = into[index].astype(jnp.float32) + other[other_index].astype(jnp.float32)
        into[index] = total.astype(jnp.bfloat16)

    for step in range(count + 3):
        i = step
        if i < count:
            core[i].wait_recv()
            own[i].wait()

            @pl.loop(0, 16)
            def _(n, i=i):
                a, b, d = n // 8, (n // 2) % 4, n % 2
                add(held[i], (a, b, d), from_core[i], (a, b, d))

            third[i].start()
        i = step - 1
        if 0 <= i < count:
            third[i].wait_recv()
            by_x = orders[i] == "xy"

            @pl.loop(0, 8)
            def _(n, i=i, by_x=by_x):
                if by_x:
                    a, b = n // 2, n % 2
                    add(held[i], (y, a, b), from_third[i], (a, b))
                else:
                    a, b = n // 4, n % 4
                    add(held[i], (a, b, x), from_third[i], (a, b))

            second[i].start()
        i = step - 2
        if 0 <= i < count:
            second[i].wait_recv()
            for k in range(4):
                add(held[i], (y, k, x), from_second[i], (k,))
            for copy in first[i]:
                copy.start()
        i = step - 3
        if 0 <= i < count:
            total = held[i][y, z, x].astype(jnp.float32)
            for k in range(3):
                first[i][k].wait_recv()
                total = total + from_first[i][k].astype(jnp.float32)
            outs[i][...] = total
    square = jnp.zeros((8, 128), jnp.float32)
    for i in range(count):
        whole = outs[i][...]
        rows, width = whole.shape
        whole = whole * whole
        for r in range(0, rows, 8):
            for w in range(0, width, 128):
                square = square + whole[r : r + 8, w : w + 128]
    square = jnp.broadcast_to(jnp.sum(square, keepdims=True), (8, 128))
    squares[0] = square
    sums = (sum_send, sum_recv)
    stage = 0
    for n, targets in enumerate(([along_core], [along_x], [along_y], along_z)):
        copies = []
        for k, target in enumerate(targets):
            copy = remote(squares.at[n], squares.at[4 + stage], sums, stage, target)
            copy.start()
            copies.append((copy, 4 + stage))
            stage += 1
        total = squares[n]
        for copy, place in copies:
            copy.wait()
            total = total + squares[place]
        if n < 3:
            squares[n + 1] = total
    total_out[...] = total
    for i in range(count):
        core[i].wait_send()
        third[i].wait_send()
        second[i].wait_send()
        for copy in first[i]:
            copy.wait_send()


def reduce_tuned(partials):
    count = len(partials)
    rows = [p.shape[1] // 16 for p in partials]
    widths = [p.shape[2] for p in partials]
    split = [p.reshape(2, 4, 2, 2, r, w) for p, r, w in zip(partials, rows, widths)]
    any_spec = pl.BlockSpec(memory_space=pl.ANY)
    vmem = pl.BlockSpec(memory_space=pltpu.VMEM)
    sizes = list(zip(rows, widths))
    scratch = [pltpu.VMEM((2, 4, 2) + s, jnp.bfloat16) for s in sizes] * 2
    scratch += [
        pltpu.VMEM(((4, 2) if ORDERS[i] == "xy" else (2, 4)) + s, jnp.bfloat16)
        for i, s in enumerate(sizes)
    ]
    scratch += [pltpu.VMEM((4,) + s, jnp.bfloat16) for s in sizes]
    scratch += [pltpu.VMEM((3,) + s, jnp.bfloat16) for s in sizes]
    scratch += [
        pltpu.VMEM((10, 8, 128), jnp.float32),
        pltpu.SemaphoreType.DMA((count,)),
        pltpu.SemaphoreType.DMA((count, 6)),
        pltpu.SemaphoreType.DMA((count, 6)),
        pltpu.SemaphoreType.DMA((6,)),
        pltpu.SemaphoreType.DMA((6,)),
    ]
    results = pl.pallas_call(
        functools.partial(reduce_kernel, count, ORDERS),
        out_shape=[jax.ShapeDtypeStruct(s, jnp.float32) for s in sizes]
        + [jax.ShapeDtypeStruct((8, 128), jnp.float32)],
        in_specs=[any_spec] * count,
        out_specs=[vmem] * (count + 1),
        scratch_shapes=scratch,
        compiler_params=pltpu.CompilerParams(
            collective_id=1, has_side_effects=True, vmem_limit_bytes=48 * 1024 * 1024
        ),
        name="reduce",
    )(*split)
    return results[:count], results[count][0, 0]


def pack_shard(heads, merge, expand, shrink):
    first = jnp.concatenate([heads[0], heads[1], heads[2], merge.T], axis=1)
    return [part.astype(jnp.bfloat16) for part in (first, expand, shrink.T)]


def unpack_shard(parts):
    first, expand, shrink = parts
    width = first.shape[1] // 4
    heads = jnp.stack([first[:, part * width : (part + 1) * width] for part in range(3)])
    return (heads, first[:, 3 * width :].T, expand, shrink.T)


def weight_views(packed):
    first, expand, shrink = packed
    width = first.shape[2] // 4

    def join(array):
        return jnp.concatenate([array[0], array[1]], axis=1)

    heads = jnp.stack([join(first[:, :, part * width : (part + 1) * width]) for part in range(3)])
    return (heads, join(first[:, :, 3 * width :]), join(expand), join(shrink))


def pack_grads(heads, merge, expand, shrink):
    def halves(array):
        half = array.shape[1] // 2
        return jnp.stack([array[:, :half], array[:, half:]])

    first = jnp.concatenate([halves(part) for part in (heads[0], heads[1], heads[2], merge)], axis=2)
    return [part.astype(jnp.bfloat16) for part in (first, halves(expand), halves(shrink))]


def swap_half(rows):
    return lax.ppermute(rows, "tensor", [(0, 1), (1, 0)])


def pick_frame(pair, index):
    return lax.dynamic_index_in_dim(pair, index, axis=0, keepdims=False)


def is_tuned():
    return lax.axis_size("dp") == 16 and lax.axis_size("tensor") == 2


def gather_plain(shards, frames, cotangent, codes):
    full = []
    for shard in shards:
        gathered = lax.all_gather(shard, ("dp", "tensor"), axis=0, tiled=False)
        split = gathered.reshape((lax.axis_size("dp"), 2) + shard.shape)
        full.append(split.transpose(1, 0, 2, 3).reshape(2, -1, shard.shape[1]))
    mine = lax.axis_index("tensor")
    swapped = [swap_half(pick_frame(pair, 1 - mine)) for pair in (frames, cotangent, codes)]
    return full, swapped[0], swapped[1], swapped[2]


def reduce_plain(partials):
    dp_size = lax.axis_size("dp")
    sums = []
    squares = jnp.zeros((), jnp.float32)
    for partial in partials:
        split = partial.reshape(2, dp_size, -1, partial.shape[2]).transpose(1, 0, 2, 3)
        split = split.reshape(-1, partial.shape[2])
        total = lax.psum_scatter(split, ("dp", "tensor"), scatter_dimension=0, tiled=True)
        total = total.astype(jnp.float32)
        squares = squares + jnp.sum(total * total)
        sums.append(total)
    return sums, lax.psum(squares, ("dp", "tensor"))


def split_frame(rows):
    mine = lax.axis_index("tensor")
    half = rows.shape[0] // 2
    other = swap_half(rows[half:].astype(jnp.bfloat16)).astype(jnp.float32)
    own = rows[:half]
    return jnp.where(mine == 0, jnp.stack([own, other]), jnp.stack([other, own]))


def small_rows(flat, row_count):
    width = -(-flat.shape[-1] // (row_count * 128)) * 128
    short = row_count * width - flat.shape[-1]
    lead = [(0, 0)] * (flat.ndim - 1)
    return jnp.pad(flat, lead + [(0, short)]).reshape(flat.shape[:-1] + (row_count, width))


def adam_update(master, gradient, first_state, second_state, step_rate, decay_rate):
    mean_new = MEAN_DECAY * first_state + (1.0 - MEAN_DECAY) * gradient
    square_new = SQUARE_DECAY * second_state + (1.0 - SQUARE_DECAY) * gradient * gradient
    normal_step = (
        mean_new
        / (1.0 - MEAN_DECAY**STEP)
        / (jnp.sqrt(square_new / (1.0 - SQUARE_DECAY**STEP)) + ADAM_EPS)
    )
    updated = master - step_rate * (normal_step + decay_rate * master)
    return (mean_new, square_new, updated, updated.astype(jnp.bfloat16))


def local(
    frames,
    codes,
    clip_frames,
    out_cotangent,
    heads_weight,
    merge_weight,
    expand_weight,
    shrink_weight,
    vectors,
    encode_weight,
    codebook,
    decode_weight,
    heads_first,
    merge_first,
    expand_first,
    shrink_first,
    vectors_first,
    encode_first,
    codebook_first,
    decode_first,
    heads_second,
    merge_second,
    expand_second,
    shrink_second,
    vectors_second,
    encode_second,
    codebook_second,
    decode_second,
):
    shards = []
    for b in range(2):
        shards += pack_shard(heads_weight[b], merge_weight[b], expand_weight[b], shrink_weight[b])
    row_count = shards[0].shape[0]
    small_parts = [vectors, encode_weight, codebook, decode_weight]
    small_flat = jnp.concatenate([part.astype(jnp.bfloat16).reshape(-1) for part in small_parts])
    small_size = small_flat.shape[0]
    shards.append(small_rows(small_flat, row_count))
    code_tiles = codes.reshape(codes.shape[0], -1, 128)
    mine = lax.axis_index("tensor")
    gather = gather_tuned if is_tuned() else gather_plain
    full, frame_other, cotangent_other, codes_other = gather(
        shards, frames, out_cotangent, code_tiles
    )
    frame_rows = jnp.concatenate([pick_frame(frames, mine), frame_other], axis=0)
    frame_rows = frame_rows.astype(jnp.float32)
    cotangent = jnp.concatenate([pick_frame(out_cotangent, mine), cotangent_other], axis=0)
    cotangent = cotangent.astype(jnp.float32)
    code_ids = jnp.concatenate([pick_frame(code_tiles, mine), codes_other], axis=0).reshape(-1)
    device_count = lax.axis_size("dp") * lax.axis_size("tensor")
    small_all = full[6].reshape(2, -1, row_count * full[6].shape[2]).transpose(1, 0, 2)
    small_all = small_all.reshape(device_count, -1)
    small_low = []
    offset = 0
    for part, cut_dim in zip(small_parts, (1, 0, 0, 1)):
        piece = small_all[:, offset : offset + part.size].reshape((-1,) + part.shape)
        offset += part.size
        if cut_dim == 1:
            piece = piece.transpose(1, 0, 2).reshape(part.shape[0], -1)
        else:
            piece = piece.reshape(-1, part.shape[1])
        small_low.append(piece)
    vector_set = small_low[0].astype(jnp.float32)
    small_set = (vector_set, small_low[1], small_low[2], small_low[3])
    weight_sets = [weight_views(full[0:3]), weight_views(full[3:6])]
    block_rows = frame_rows.shape[0] // 2
    frame_id = lax.axis_index("dp") * frames.shape[0] + lax.axis_index("tensor")
    clip_ends = jnp.cumsum(clip_frames)
    clip_id = jnp.sum((clip_ends <= frame_id).astype(jnp.int32))
    clip_slots = jnp.arange(clip_frames.shape[0], dtype=jnp.int32)
    clip_count = jnp.sum(jnp.where(clip_slots == clip_id, clip_frames, 0))
    clip_weight = 1.0 / clip_count.astype(jnp.float32)
    encoded, kept_encoder = block_forward(
        frame_rows, weight_sets[0], vector_set[0:6], block_rows
    )
    started, kept_quant = quantize_forward(encoded, code_ids, small_set)
    decoded, kept_decoder = block_forward(started, weight_sets[1], vector_set[6:12], block_rows)
    dstarted, decoder_grads, decoder_vectors = block_backward(
        kept_decoder, cotangent, weight_sets[1], vector_set[6:12], block_rows
    )
    dencoded, quant_grads = quantize_backward(
        kept_quant, dstarted, code_ids, clip_weight, small_set
    )
    dframe, encoder_grads, encoder_vectors = block_backward(
        kept_encoder, dencoded, weight_sets[0], vector_set[0:6], block_rows
    )
    decoded_all = split_frame(decoded)
    frame_grads = split_frame(dframe)
    dvectors = jnp.concatenate([encoder_vectors, decoder_vectors, quant_grads[0]], axis=0)
    small_new = (dvectors, quant_grads[1], quant_grads[2], quant_grads[3])
    columns = []
    for gradient, part, cut_dim in zip(small_new, small_parts, (1, 0, 0, 1)):
        if cut_dim == 1:
            gradient = gradient.reshape(part.shape[0], device_count, -1).transpose(1, 0, 2)
        columns.append(gradient.reshape(device_count, -1).astype(jnp.bfloat16))
    small_grad = small_rows(jnp.concatenate(columns, axis=1), row_count)
    small_grad = small_grad.reshape((-1, 2) + small_grad.shape[1:]).transpose(1, 0, 2, 3)
    small_grad = small_grad.reshape(2, -1, small_grad.shape[3])
    partials = pack_grads(*encoder_grads) + pack_grads(*decoder_grads) + [small_grad]
    reduce = reduce_tuned if is_tuned() else reduce_plain
    sums, squares = reduce(partials)
    reduced = [unpack_shard(sums[0:3]), unpack_shard(sums[3:6])]
    block_grads = [jnp.stack([first, second]) for first, second in zip(*reduced)]
    small_sum = sums[6].reshape(-1)[:small_size]
    small_grads = []
    offset = 0
    for part in small_parts:
        small_grads.append(small_sum[offset : offset + part.size].reshape(part.shape))
        offset += part.size
    gradients = tuple(block_grads) + tuple(small_grads)
    norm_before = jnp.sqrt(squares)
    factor = MAX_NORM / jnp.maximum(norm_before, MAX_NORM)
    masters = (
        heads_weight,
        merge_weight,
        expand_weight,
        shrink_weight,
        vectors,
        encode_weight,
        codebook,
        decode_weight,
    )
    firsts = (
        heads_first,
        merge_first,
        expand_first,
        shrink_first,
        vectors_first,
        encode_first,
        codebook_first,
        decode_first,
    )
    seconds = (
        heads_second,
        merge_second,
        expand_second,
        shrink_second,
        vectors_second,
        encode_second,
        codebook_second,
        decode_second,
    )
    updates = [
        adam_update(
            masters[member],
            gradients[member] * factor,
            firsts[member],
            seconds[member],
            RATES[member],
            DECAYS[member],
        )
        for member in range(8)
    ]
    return (
        decoded_all,
        frame_grads,
        norm_before,
        updates[0][0],
        updates[0][1],
        updates[0][2],
        updates[0][3],
        updates[1][0],
        updates[1][1],
        updates[1][2],
        updates[1][3],
        updates[2][0],
        updates[2][1],
        updates[2][2],
        updates[2][3],
        updates[3][0],
        updates[3][1],
        updates[3][2],
        updates[3][3],
        updates[4][0],
        updates[4][1],
        updates[4][2],
        updates[4][3],
        updates[5][0],
        updates[5][1],
        updates[5][2],
        updates[5][3],
        updates[6][0],
        updates[6][1],
        updates[6][2],
        updates[6][3],
        updates[7][0],
        updates[7][1],
        updates[7][2],
        updates[7][3],
    )


def solution(mesh):
    return jax.shard_map(
        local,
        mesh=mesh,
        in_specs=(
            P("dp", "tensor", None),
            P("dp", "tensor"),
            P(),
            P("dp", "tensor", None),
            P(None, None, "dp", "tensor"),
            P(None, "tensor", "dp"),
            P(None, "dp", "tensor"),
            P(None, "tensor", "dp"),
            P(None, ("dp", "tensor")),
            P(("dp", "tensor"), None),
            P(("dp", "tensor"), None),
            P(None, ("dp", "tensor")),
            P(None, None, "dp", "tensor"),
            P(None, "tensor", "dp"),
            P(None, "dp", "tensor"),
            P(None, "tensor", "dp"),
            P(None, ("dp", "tensor")),
            P(("dp", "tensor"), None),
            P(("dp", "tensor"), None),
            P(None, ("dp", "tensor")),
            P(None, None, "dp", "tensor"),
            P(None, "tensor", "dp"),
            P(None, "dp", "tensor"),
            P(None, "tensor", "dp"),
            P(None, ("dp", "tensor")),
            P(("dp", "tensor"), None),
            P(("dp", "tensor"), None),
            P(None, ("dp", "tensor")),
        ),
        out_specs=(
            P("dp", "tensor", None),
            P("dp", "tensor", None),
            P(),
            P(None, None, "dp", "tensor"),
            P(None, None, "dp", "tensor"),
            P(None, None, "dp", "tensor"),
            P(None, None, "dp", "tensor"),
            P(None, "tensor", "dp"),
            P(None, "tensor", "dp"),
            P(None, "tensor", "dp"),
            P(None, "tensor", "dp"),
            P(None, "dp", "tensor"),
            P(None, "dp", "tensor"),
            P(None, "dp", "tensor"),
            P(None, "dp", "tensor"),
            P(None, "tensor", "dp"),
            P(None, "tensor", "dp"),
            P(None, "tensor", "dp"),
            P(None, "tensor", "dp"),
            P(None, ("dp", "tensor")),
            P(None, ("dp", "tensor")),
            P(None, ("dp", "tensor")),
            P(None, ("dp", "tensor")),
            P(("dp", "tensor"), None),
            P(("dp", "tensor"), None),
            P(("dp", "tensor"), None),
            P(("dp", "tensor"), None),
            P(("dp", "tensor"), None),
            P(("dp", "tensor"), None),
            P(("dp", "tensor"), None),
            P(("dp", "tensor"), None),
            P(None, ("dp", "tensor")),
            P(None, ("dp", "tensor")),
            P(None, ("dp", "tensor")),
            P(None, ("dp", "tensor")),
        ),
        check_vma=False,
    )
```

```python
import functools

import jax
import jax.numpy as jnp
from jax import lax
from jax.experimental import pallas as pl
from jax.experimental.pallas import tpu as pltpu
from jax.sharding import PartitionSpec as P

HEAD_DIM = 64
STEP = 10


EPS_NORM = 1e-05
EPS_UNIT = 1e-06
COMMIT_WEIGHT = 100.0
MAX_NORM = 1.0
MEAN_DECAY = 0.9
SQUARE_DECAY = 0.95
ADAM_EPS = 1e-08
RATES = (0.1, 0.5, 0.1, 0.05, 1.0, 0.1, 1.0, 0.3)
DECAYS = (0.1, 0.1, 0.1, 0.1, 0.0, 0.1, 0.1, 0.1)


NT = (((1,), (1,)), ((), ()))
NN = (((1,), (0,)), ((), ()))
PAIR = 128
GELU_SCALE = (2.0 / 3.141592653589793) ** 0.5
GELU_CUBE = 0.044715


def mxu(first, second, dims=NN):
    return lax.dot_general(first, second, dims, preferred_element_type=jnp.float32)


def low(values):
    return values.astype(jnp.bfloat16)


def wide(values):
    return values.astype(jnp.float32)


def two_low(values):
    top = low(values)
    return top, low(values - wide(top))


def head_mask(shape, head):
    return (lax.broadcasted_iota(jnp.int32, shape, 1) // HEAD_DIM) == head


def keep_head(values, head):
    return jnp.where(head_mask(values.shape, head), values, jnp.zeros_like(values))


def norm_parts(rows):
    center = rows - jnp.mean(rows, axis=-1, keepdims=True)
    spread = jnp.mean(center * center, axis=-1, keepdims=True)
    scale = lax.rsqrt(spread + EPS_NORM)
    return center * scale, scale


def norm_back(xhat, scale, gain, grad):
    dxhat = grad * gain
    mean_grad = jnp.mean(dxhat, axis=-1, keepdims=True)
    mean_cross = jnp.mean(dxhat * xhat, axis=-1, keepdims=True)
    return scale * (dxhat - mean_grad - xhat * mean_cross)


def unit_back(values, grad):
    inverse = lax.rsqrt(jnp.sum(values * values, axis=-1, keepdims=True) + EPS_UNIT)
    cross = jnp.sum(values * grad, axis=-1, keepdims=True)
    return inverse * grad - values * (inverse * inverse * inverse * cross)


def add_row(ref, row, values):
    ref[row : row + 1, :] += jnp.sum(values, axis=0, keepdims=True)


def tile_rows(step, tile):
    return pl.ds(pl.multiple_of(step * tile, tile), tile)


def project_stage(x_ref, vec, base, first_w, n_ref, q_ref, k_ref, v_ref, tile):
    length = x_ref.shape[0]

    @pl.loop(0, length // tile)
    def _(step):
        rows = tile_rows(step, tile)
        xhat, _ = norm_parts(wide(x_ref[rows, :]))
        normed = low(xhat * vec[base : base + 1, :] + vec[base + 1 : base + 2, :])
        n_ref[rows, :] = normed
        for half in range(2):
            columns = slice(half * 256, half * 256 + 256)
            projected = low(mxu(normed, first_w[half, :, 0:768]))
            q_ref[rows, columns] = projected[:, 0:256] * (HEAD_DIM**-0.5)
            k_ref[rows, columns] = projected[:, 256:512]
            v_ref[rows, columns] = projected[:, 512:768]


def attend_stage(q_ref, k_ref, v_ref, mix_ref, lse_ref, tile):
    length = q_ref.shape[0]

    @pl.loop(0, 4)
    def _(pair):
        columns = pl.ds(pl.multiple_of(pair * PAIR, PAIR), PAIR)
        keys = k_ref[:, columns]
        values = v_ref[:, columns]
        for start in range(0, length, tile):
            query = q_ref[start : start + tile, columns]
            out = None
            for head in range(2):
                ones_beside = jnp.where(
                    head_mask(values.shape, head), values, jnp.ones_like(values)
                )
                scores = mxu(keep_head(query, head), keys, NT)
                top = jnp.max(scores, axis=1, keepdims=True)
                raised = low(jnp.exp(scores - top))
                mixed = mxu(raised, ones_beside)
                total = pltpu.roll(mixed, HEAD_DIM, 1)
                mixed = mixed / total
                log_sum = top + jnp.log(total)
                if out is None:
                    out, log_sums = mixed, log_sum
                else:
                    first = head_mask(mixed.shape, 0)
                    out = jnp.where(first, out, mixed)
                    log_sums = jnp.where(first, log_sums, log_sum)
            mix_ref[start : start + tile, columns] = low(out)
            turned = log_sums.T
            for head in range(2):
                lse_ref[pair * 2 + head, :, start : start + tile] = jnp.broadcast_to(
                    turned[head * HEAD_DIM : head * HEAD_DIM + 1], (8, tile)
                )


def mlp_stage(
    x_ref, mix_ref, vec, base, first_w, expand_w, shrink_w, h_ref, nm_ref, ex_ref, act_ref, tile, give
):
    length = x_ref.shape[0]

    @pl.loop(0, length // tile)
    def _(step):
        rows = tile_rows(step, tile)
        hidden = wide(x_ref[rows, :]) + vec[base + 2 : base + 3, :]
        for half in range(2):
            hidden = hidden + mxu(
                mix_ref[rows, half * 256 : half * 256 + 256], first_w[half, :, 768:1024], NT
            )
        h_ref[rows, :] = hidden
        xhat, _ = norm_parts(hidden)
        normed = low(xhat * vec[base + 3 : base + 4, :] + vec[base + 4 : base + 5, :])
        nm_ref[rows, :] = normed
        out = hidden + vec[base + 5 : base + 6, :]
        for half in range(2):
            for start in range(0, 1024, 512):
                expanded = mxu(normed, expand_w[half, :, start : start + 512])
                place = slice(half * 1024 + start, half * 1024 + start + 512)
                ex_ref[rows, place] = expanded
                inner = GELU_SCALE * (expanded + GELU_CUBE * (expanded * expanded * expanded))
                active = low(0.5 * expanded * (1.0 + jnp.tanh(inner)))
                act_ref[rows, place] = active
                out = out + mxu(active, shrink_w[half, :, start : start + 512], NT)
        give(rows, out)


def mlp_back_stage(
    dout_ref, h_ref, ex_ref, vec, base, first_w, expand_w, shrink_w, dex_ref, dh_ref, dmix_ref, vg_ref, tile
):
    length = h_ref.shape[0]

    @pl.loop(0, length // tile)
    def _(step):
        rows = tile_rows(step, tile)
        dout = wide(dout_ref[rows, :])
        dout_low = low(dout)
        dnormed = None
        for half in range(2):
            for start in range(0, 1024, 512):
                place = slice(half * 1024 + start, half * 1024 + start + 512)
                dactive = mxu(dout_low, shrink_w[half, :, start : start + 512])
                expanded = ex_ref[rows, place]
                square = expanded * expanded
                inner = GELU_SCALE * expanded * (1.0 + GELU_CUBE * square)
                bend = jnp.tanh(inner)
                slope = 0.5 * (1.0 + bend) + (0.5 * GELU_SCALE) * expanded * (
                    1.0 - bend * bend
                ) * (1.0 + 3.0 * GELU_CUBE * square)
                dexpanded = low(dactive * slope)
                dex_ref[rows, place] = dexpanded
                part = mxu(dexpanded, expand_w[half, :, start : start + 512], NT)
                dnormed = part if dnormed is None else dnormed + part
        xhat, scale = norm_parts(h_ref[rows, :])
        dhidden = dout + norm_back(xhat, scale, vec[base + 3 : base + 4, :], dnormed)
        dh_ref[rows, :] = dhidden
        dhidden_low = low(dhidden)
        for half in range(2):
            dmix_ref[rows, half * 256 : half * 256 + 256] = low(
                mxu(dhidden_low, first_w[half, :, 768:1024])
            )
        add_row(vg_ref, base + 2, dhidden)
        add_row(vg_ref, base + 3, dnormed * xhat)
        add_row(vg_ref, base + 4, dnormed)
        add_row(vg_ref, base + 5, dout)


def turn_stage(source_ref, turned_ref):
    length = source_ref.shape[0]
    for start in range(0, length, 256):
        turned_ref[:, start : start + 256] = low(source_ref[start : start + 256, :]).T


def weight_grad_stage(turned_ref, right_ref, out_ref, half, first, target, width):
    out_ref[half, :, target : target + width] = low(
        mxu(turned_ref[...], right_ref[:, first : first + width])
    )


def attend_back_stage(
    q_ref, k_ref, v_ref, mix_ref, dmix_ref, lse_ref, dq_ref, dk_ref, dv_ref, dk_acc, dv_acc, tile
):
    length = q_ref.shape[0]

    @pl.loop(0, 4)
    def _(pair):
        columns = pl.ds(pl.multiple_of(pair * PAIR, PAIR), PAIR)
        keys = k_ref[:, columns]
        values = v_ref[:, columns]
        keys_turned = keys.T
        for start in range(0, length, tile):
            rows = slice(start, start + tile)
            query = q_ref[rows, columns]
            dmix = dmix_ref[rows, columns]
            inner = (wide(dmix) * wide(mix_ref[rows, columns])).T
            dquery, dkeys, dvalues = [], None, None
            for head in range(2):
                span = slice(head * HEAD_DIM, head * HEAD_DIM + HEAD_DIM)
                query_here = keep_head(query, head)
                dmix_here = keep_head(dmix, head)
                delta = jnp.sum(inner[span], axis=0, keepdims=True)
                log_sum = lse_ref[pair * 2 + head, 0:1, rows]
                attend = jnp.exp(mxu(keys, query_here, NT) - log_sum)
                dscores = low(attend * (mxu(values, dmix_here, NT) - delta))
                part = mxu(low(attend), dmix_here)
                dvalues = part if dvalues is None else dvalues + part
                part = mxu(dscores, query_here)
                dkeys = part if dkeys is None else dkeys + part
                dquery.append(mxu(keys_turned[span], dscores))
            dq_ref[rows, columns] = low(
                (jnp.concatenate(dquery, axis=0) * (HEAD_DIM**-0.5)).T
            )
            if start == 0:
                dk_acc[...] = dkeys
                dv_acc[...] = dvalues
            elif start + tile < length:
                dk_acc[...] += dkeys
                dv_acc[...] += dvalues
            else:
                dk_ref[:, columns] = low(dk_acc[...] + dkeys)
                dv_ref[:, columns] = low(dv_acc[...] + dvalues)


def project_back_stage(
    x_ref, dh_ref, dq_ref, dk_ref, dv_ref, vec, base, first_w, vg_ref, tile, give
):
    length = x_ref.shape[0]

    @pl.loop(0, length // tile)
    def _(step):
        rows = tile_rows(step, tile)
        dnormed = None
        for part, ref in enumerate((dq_ref, dk_ref, dv_ref)):
            for half in range(2):
                product = mxu(
                    ref[rows, half * 256 : half * 256 + 256],
                    first_w[half, :, part * 256 : part * 256 + 256],
                    NT,
                )
                dnormed = product if dnormed is None else dnormed + product
        xhat, scale = norm_parts(wide(x_ref[rows, :]))
        dx = dh_ref[rows, :] + norm_back(xhat, scale, vec[base : base + 1, :], dnormed)
        add_row(vg_ref, base, dnormed * xhat)
        add_row(vg_ref, base + 1, dnormed)
        give(rows, dx)


def block_kernel(encoder, *refs):
    if encoder:
        weight, frame, entries, vec, encode, first_w, expand_w, shrink_w = refs[:8]
        dx_out, pulled_out, dencode_out, vg_ref, dfirst, dexpand, dshrink = refs[8:15]
        scratch = refs[15:]
        base = 0
    else:
        cotangent, entries, pulled, vec, decode, first_w, expand_w, shrink_w = refs[:8]
        out_ref, dentries_out, ddecode_out, vg_ref, dfirst, dexpand, dshrink = refs[8:15]
        scratch = refs[15:]
        base = 6
    (x_buf, n_ref, q_ref, k_ref, v_ref, mix_ref, lse_ref, h_ref, nm_ref, ex_ref, act_ref) = scratch[:11]
    (dout_buf, dex_ref, dh_ref, dmix_ref, dq_ref, dk_ref, dv_ref, dk_acc, dv_acc, turned) = scratch[11:]
    vg_ref[...] = jnp.zeros_like(vg_ref)
    tile = 512
    if encoder:
        x_ref = frame
    else:
        x_ref = x_buf
        values = wide(entries[...])
        inverse = lax.rsqrt(jnp.sum(values * values, axis=-1, keepdims=True) + EPS_UNIT)
        x_buf[...] = mxu(low(values * inverse), decode[...]) + vec[14:15, :]
    project_stage(x_ref, vec, base, first_w, n_ref, q_ref, k_ref, v_ref, tile)
    attend_stage(q_ref, k_ref, v_ref, mix_ref, lse_ref, tile)

    def give_out(rows, out):
        if not encoder:
            out_ref[rows, :] = out
            return
        xhat, scale = norm_parts(out)
        normed = low(xhat * vec[12:13, :] + vec[13:14, :])
        raw = mxu(normed, encode[...])
        raw_inverse = lax.rsqrt(jnp.sum(raw * raw, axis=-1, keepdims=True) + EPS_UNIT)
        picked = wide(entries[rows, :])
        inverse = lax.rsqrt(jnp.sum(picked * picked, axis=-1, keepdims=True) + EPS_UNIT)
        pull = (2.0 * COMMIT_WEIGHT * weight[0, 0]) * (raw * raw_inverse - picked * inverse)
        pulled_out[rows, :] = pull
        draw = unit_back(raw, pull)
        dnormed = None
        for part in two_low(draw):
            product = mxu(part, encode[...], NT)
            dnormed = product if dnormed is None else dnormed + product
            dencode_out[...] += mxu(part.T[0:32], normed)
        dout_buf[rows, :] = norm_back(xhat, scale, vec[12:13, :], dnormed)
        add_row(vg_ref, 12, dnormed * xhat)
        add_row(vg_ref, 13, dnormed)

    if encoder:
        dencode_out[...] = jnp.zeros_like(dencode_out)
    mlp_stage(
        x_ref, mix_ref, vec, base, first_w, expand_w, shrink_w, h_ref, nm_ref, ex_ref, act_ref, tile, give_out
    )
    dout_ref = dout_buf if encoder else cotangent
    mlp_back_stage(
        dout_ref, h_ref, ex_ref, vec, base, first_w, expand_w, shrink_w, dex_ref, dh_ref, dmix_ref, vg_ref, tile
    )
    turn_stage(dout_ref, turned)
    for half in range(2):
        for start in range(0, 1024, 512):
            weight_grad_stage(turned, act_ref, dshrink, half, half * 1024 + start, start, 512)
    turn_stage(nm_ref, turned)
    for half in range(2):
        for start in range(0, 1024, 512):
            weight_grad_stage(turned, dex_ref, dexpand, half, half * 1024 + start, start, 512)
    attend_back_stage(
        q_ref, k_ref, v_ref, mix_ref, dmix_ref, lse_ref, dq_ref, dk_ref, dv_ref, dk_acc, dv_acc, tile
    )
    turn_stage(dh_ref, turned)
    for half in range(2):
        weight_grad_stage(turned, mix_ref, dfirst, half, half * 256, 768, 256)
    turn_stage(n_ref, turned)
    for half in range(2):
        for part, ref in enumerate((dq_ref, dk_ref, dv_ref)):
            weight_grad_stage(turned, ref, dfirst, half, half * 256, part * 256, 256)

    def give_dx(rows, dx):
        if encoder:
            dx_out[rows, :] = dx
            return
        add_row(vg_ref, 14, dx)
        values = wide(entries[rows, :])
        inverse = lax.rsqrt(jnp.sum(values * values, axis=-1, keepdims=True) + EPS_UNIT)
        turned_low = low(values * inverse).T[0:32]
        dchosen = -pulled[rows, :]
        for part in two_low(dx):
            ddecode_out[...] += mxu(turned_low, part)
            dchosen = dchosen + mxu(part, decode[...], NT)
        dentries_out[rows, :] = unit_back(values, dchosen)

    if not encoder:
        ddecode_out[...] = jnp.zeros_like(ddecode_out)
    project_back_stage(
        x_ref, dh_ref, dq_ref, dk_ref, dv_ref, vec, base, first_w, vg_ref, tile, give_dx
    )


def run_block(encoder, *args):
    length = args[1].shape[0]
    hidden = 2048
    f32, bf16 = jnp.float32, jnp.bfloat16
    vmem = pl.BlockSpec(memory_space=pltpu.VMEM)
    in_specs = [vmem] * 8
    if encoder:
        in_specs[0] = pl.BlockSpec(memory_space=pltpu.SMEM)
    outs = [((length, 512), f32), ((length, PAIR), f32), ((32, 512), f32), ((16, 512), f32)]
    outs += [((2, 512, 1024), bf16)] * 3
    shapes = [
        ((8, 128) if encoder else (length, 512), f32),
        ((length, 512), bf16),
        ((length, 512), bf16),
        ((length, 512), bf16),
        ((length, 512), bf16),
        ((length, 512), bf16),
        ((8, 8, length), f32),
        ((length, 512), f32),
        ((length, 512), bf16),
        ((length, hidden), f32),
        ((length, hidden), bf16),
        ((length, 512) if encoder else (8, 128), f32),
        ((length, hidden), bf16),
        ((length, 512), f32),
        ((length, 512), bf16),
        ((length, 512), bf16),
        ((length, 512), bf16),
        ((length, 512), bf16),
        ((length, PAIR), f32),
        ((length, PAIR), f32),
        ((512, length), bf16),
    ]
    return pl.pallas_call(
        functools.partial(block_kernel, encoder),
        out_shape=[jax.ShapeDtypeStruct(s, d) for s, d in outs],
        in_specs=in_specs,
        out_specs=[vmem] * 7,
        scratch_shapes=[pltpu.VMEM(s, d) for s, d in shapes],
        compiler_params=pltpu.CompilerParams(vmem_limit_bytes=60 * 1024 * 1024),
        name="encoder" if encoder else "decoder",
    )(*args)


MESH = pl.DeviceIdType.MESH


def remote(src, dst, sems, slot, target):
    send, recv = sems
    return pltpu.make_async_remote_copy(
        src_ref=src,
        dst_ref=dst,
        send_sem=send.at[slot],
        recv_sem=recv.at[slot],
        device_id=target,
        device_id_type=MESH,
    )


def coordinates():
    dp_index = lax.axis_index("dp")
    y = lax.axis_index("tensor")
    return dp_index // 4, (dp_index // 2) % 2, dp_index % 2, y


def partners(z, x, c, y):
    along_z = [(((z + step) % 4) * 4 + x * 2 + c, y) for step in (1, 2, 3)]
    along_x = (z * 4 + (1 - x) * 2 + c, y)
    along_y = (z * 4 + x * 2 + c, 1 - y)
    along_core = (z * 4 + x * 2 + (1 - c), y)
    return along_z, along_x, along_y, along_core


def greet(targets):
    barrier = pltpu.get_barrier_semaphore()
    for target in targets:
        pl.semaphore_signal(barrier, inc=1, device_id=target, device_id_type=MESH)
    pl.semaphore_wait(barrier, len(targets))


def gather_kernel(count, orders, *refs):
    shards = refs[:count]
    frames, cotangent, codes = refs[count : count + 3]
    outs = refs[count + 3 : 2 * count + 3]
    frame_out, cotangent_out, codes_out = refs[2 * count + 3 : 2 * count + 6]
    local_sems, send_sems, recv_sems, swap_send, swap_recv = refs[2 * count + 6 :]
    z, x, c, y = coordinates()
    along_z, along_x, along_y, along_core = partners(z, x, c, y)
    greet(along_z + [along_x, along_y, along_core])
    sems, swaps = (send_sems, recv_sems), (swap_send, swap_recv)
    pending = []
    for slot, (source, target) in enumerate(
        ((codes, codes_out), (frames, frame_out), (cotangent, cotangent_out))
    ):
        copy = remote(source.at[1 - y], target, swaps, slot, along_y)
        pending.append(copy)
        copy.start()
    first, second, third, to_core = [], [], [], []
    own = []
    for i in range(count):
        slot = outs[i].at[y, z, x, c]
        copy = pltpu.make_async_copy(shards[i], slot, local_sems.at[i])
        copy.start()
        own.append(copy)
        first.append([remote(shards[i], slot, sems, (i, k), along_z[k]) for k in range(3)])
        for copy in first[i]:
            copy.start()
        by_x = orders[i] == "xy"
        column = outs[i].at[y, :, x, c]
        second.append(remote(column, column, sems, (i, 3), along_x if by_x else along_y))
        plane = outs[i].at[y, :, :, c] if by_x else outs[i].at[:, :, x, c]
        third.append(remote(plane, plane, sems, (i, 4), along_y if by_x else along_x))
        got_second = outs[i].at[y, :, 1 - x, c] if by_x else outs[i].at[1 - y, :, x, c]
        got_third = outs[i].at[1 - y, :, :, c] if by_x else outs[i].at[:, :, 1 - x, c]
        to_core.append(
            [
                remote(part, part, sems, (i, 5 + k), along_core)
                for k, part in enumerate((column, got_second, got_third))
            ]
        )
    for step in range(count + 2):
        i = step
        if i < count:
            own[i].wait()
            for copy in first[i]:
                copy.wait_recv()
            second[i].start()
            to_core[i][0].start()
        i = step - 1
        if 0 <= i < count:
            second[i].wait_recv()
            third[i].start()
            to_core[i][1].start()
        i = step - 2
        if 0 <= i < count:
            third[i].wait_recv()
            to_core[i][2].start()
    for i in range(count):
        for copy in first[i] + [second[i], third[i]]:
            copy.wait_send()
        for copy in to_core[i]:
            copy.wait()
    for copy in pending:
        copy.wait()


ORDERS = ("xy", "yx", "xy", "yx", "xy", "yx", "yx")


def gather_tuned(shards, frames, cotangent, codes):
    count = len(shards)
    any_spec = pl.BlockSpec(memory_space=pl.ANY)
    outs = [jax.ShapeDtypeStruct((2, 4, 2, 2) + s.shape, s.dtype) for s in shards]
    outs += [jax.ShapeDtypeStruct(a.shape[1:], a.dtype) for a in (frames, cotangent, codes)]
    results = pl.pallas_call(
        functools.partial(gather_kernel, count, ORDERS),
        out_shape=outs,
        in_specs=[any_spec] * (count + 3),
        out_specs=[any_spec] * (count + 3),
        scratch_shapes=[
            pltpu.SemaphoreType.DMA((count,)),
            pltpu.SemaphoreType.DMA((count, 8)),
            pltpu.SemaphoreType.DMA((count, 8)),
            pltpu.SemaphoreType.DMA((3,)),
            pltpu.SemaphoreType.DMA((3,)),
        ],
        compiler_params=pltpu.CompilerParams(collective_id=0, has_side_effects=True),
        name="gather",
    )(*shards, frames, cotangent, codes)
    full = [r.reshape(2, 16 * r.shape[4], r.shape[5]) for r in results[:count]]
    return full, results[count], results[count + 1], results[count + 2]


def reduce_kernel(count, orders, *refs):
    partial = refs[:count]
    outs = refs[count : 2 * count]
    total_out = refs[2 * count]
    scratch = refs[2 * count + 1 :]
    held = scratch[:count]
    from_core = scratch[count : 2 * count]
    from_third = scratch[2 * count : 3 * count]
    from_second = scratch[3 * count : 4 * count]
    from_first = scratch[4 * count : 5 * count]
    squares, local_sems, send_sems, recv_sems, sum_send, sum_recv = scratch[5 * count :]
    z, x, c, y = coordinates()
    along_z, along_x, along_y, along_core = partners(z, x, c, y)
    greet(along_z + [along_x, along_y, along_core])
    sems = (send_sems, recv_sems)
    own, core, third, second, first = [], [], [], [], []
    for i in range(count):
        by_x = orders[i] == "xy"
        copy = remote(partial[i].at[:, :, :, 1 - c], from_core[i], sems, (i, 0), along_core)
        copy.start()
        core.append(copy)
        copy = pltpu.make_async_copy(partial[i].at[:, :, :, c], held[i], local_sems.at[i])
        copy.start()
        own.append(copy)
        if by_x:
            third.append(remote(held[i].at[1 - y], from_third[i], sems, (i, 1), along_y))
            second.append(remote(held[i].at[y, :, 1 - x], from_second[i], sems, (i, 2), along_x))
        else:
            third.append(remote(held[i].at[:, :, 1 - x], from_third[i], sems, (i, 1), along_x))
            second.append(remote(held[i].at[1 - y, :, x], from_second[i], sems, (i, 2), along_y))
        first.append(
            [
                remote(
                    held[i].at[y, (z + k + 1) % 4, x],
                    from_first[i].at[k],
                    sems,
                    (i, 3 + k),
                    along_z[k],
                )
                for k in range(3)
            ]
        )

    def add(into, index, other, other_index):
        total = into[index].astype(jnp.float32) + other[other_index].astype(jnp.float32)
        into[index] = total.astype(jnp.bfloat16)

    for step in range(count + 3):
        i = step
        if i < count:
            core[i].wait_recv()
            own[i].wait()

            @pl.loop(0, 16)
            def _(n, i=i):
                a, b, d = n // 8, (n // 2) % 4, n % 2
                add(held[i], (a, b, d), from_core[i], (a, b, d))

            third[i].start()
        i = step - 1
        if 0 <= i < count:
            third[i].wait_recv()
            by_x = orders[i] == "xy"

            @pl.loop(0, 8)
            def _(n, i=i, by_x=by_x):
                if by_x:
                    a, b = n // 2, n % 2
                    add(held[i], (y, a, b), from_third[i], (a, b))
                else:
                    a, b = n // 4, n % 4
                    add(held[i], (a, b, x), from_third[i], (a, b))

            second[i].start()
        i = step - 2
        if 0 <= i < count:
            second[i].wait_recv()
            for k in range(4):
                add(held[i], (y, k, x), from_second[i], (k,))
            for copy in first[i]:
                copy.start()
        i = step - 3
        if 0 <= i < count:
            total = held[i][y, z, x].astype(jnp.float32)
            for k in range(3):
                first[i][k].wait_recv()
                total = total + from_first[i][k].astype(jnp.float32)
            outs[i][...] = total
    square = jnp.zeros((8, 128), jnp.float32)
    for i in range(count):
        whole = outs[i][...]
        rows, width = whole.shape
        whole = whole * whole
        for r in range(0, rows, 8):
            for w in range(0, width, 128):
                square = square + whole[r : r + 8, w : w + 128]
    square = jnp.broadcast_to(jnp.sum(square, keepdims=True), (8, 128))
    squares[0] = square
    sums = (sum_send, sum_recv)
    stage = 0
    for n, targets in enumerate(([along_core], [along_x], [along_y], along_z)):
        copies = []
        for k, target in enumerate(targets):
            copy = remote(squares.at[n], squares.at[4 + stage], sums, stage, target)
            copy.start()
            copies.append((copy, 4 + stage))
            stage += 1
        total = squares[n]
        for copy, place in copies:
            copy.wait()
            total = total + squares[place]
        if n < 3:
            squares[n + 1] = total
    total_out[...] = total
    for i in range(count):
        core[i].wait_send()
        third[i].wait_send()
        second[i].wait_send()
        for copy in first[i]:
            copy.wait_send()


def reduce_tuned(partials):
    count = len(partials)
    rows = [p.shape[1] // 16 for p in partials]
    widths = [p.shape[2] for p in partials]
    split = [p.reshape(2, 4, 2, 2, r, w) for p, r, w in zip(partials, rows, widths)]
    any_spec = pl.BlockSpec(memory_space=pl.ANY)
    vmem = pl.BlockSpec(memory_space=pltpu.VMEM)
    sizes = list(zip(rows, widths))
    scratch = [pltpu.VMEM((2, 4, 2) + s, jnp.bfloat16) for s in sizes] * 2
    scratch += [
        pltpu.VMEM(((4, 2) if ORDERS[i] == "xy" else (2, 4)) + s, jnp.bfloat16)
        for i, s in enumerate(sizes)
    ]
    scratch += [pltpu.VMEM((4,) + s, jnp.bfloat16) for s in sizes]
    scratch += [pltpu.VMEM((3,) + s, jnp.bfloat16) for s in sizes]
    scratch += [
        pltpu.VMEM((10, 8, 128), jnp.float32),
        pltpu.SemaphoreType.DMA((count,)),
        pltpu.SemaphoreType.DMA((count, 6)),
        pltpu.SemaphoreType.DMA((count, 6)),
        pltpu.SemaphoreType.DMA((6,)),
        pltpu.SemaphoreType.DMA((6,)),
    ]
    results = pl.pallas_call(
        functools.partial(reduce_kernel, count, ORDERS),
        out_shape=[jax.ShapeDtypeStruct(s, jnp.float32) for s in sizes]
        + [jax.ShapeDtypeStruct((8, 128), jnp.float32)],
        in_specs=[any_spec] * count,
        out_specs=[vmem] * (count + 1),
        scratch_shapes=scratch,
        compiler_params=pltpu.CompilerParams(
            collective_id=1, has_side_effects=True, vmem_limit_bytes=48 * 1024 * 1024
        ),
        name="reduce",
    )(*split)
    return results[:count], results[count][0, 0]


def pack_shard(heads, merge, expand, shrink):
    first = jnp.concatenate([heads[0], heads[1], heads[2], merge.T], axis=1)
    return [part.astype(jnp.bfloat16) for part in (first, expand, shrink.T)]


def unpack_shard(parts):
    first, expand, shrink = parts
    width = first.shape[1] // 4
    heads = jnp.stack([first[:, part * width : (part + 1) * width] for part in range(3)])
    return (heads, first[:, 3 * width :].T, expand, shrink.T)


def swap_half(rows):
    return lax.ppermute(rows, "tensor", [(0, 1), (1, 0)])


def pick_frame(pair, index):
    return lax.dynamic_index_in_dim(pair, index, axis=0, keepdims=False)


def is_tuned():
    return lax.axis_size("dp") == 16 and lax.axis_size("tensor") == 2


def gather_plain(shards, frames, cotangent, codes):
    full = []
    for shard in shards:
        gathered = lax.all_gather(shard, ("dp", "tensor"), axis=0, tiled=False)
        split = gathered.reshape((lax.axis_size("dp"), 2) + shard.shape)
        full.append(split.transpose(1, 0, 2, 3).reshape(2, -1, shard.shape[1]))
    mine = lax.axis_index("tensor")
    swapped = [swap_half(pick_frame(pair, 1 - mine)) for pair in (frames, cotangent, codes)]
    return full, swapped[0], swapped[1], swapped[2]


def reduce_plain(partials):
    dp_size = lax.axis_size("dp")
    sums = []
    squares = jnp.zeros((), jnp.float32)
    for partial in partials:
        split = partial.reshape(2, dp_size, -1, partial.shape[2]).transpose(1, 0, 2, 3)
        split = split.reshape(-1, partial.shape[2])
        total = lax.psum_scatter(split, ("dp", "tensor"), scatter_dimension=0, tiled=True)
        total = total.astype(jnp.float32)
        squares = squares + jnp.sum(total * total)
        sums.append(total)
    return sums, lax.psum(squares, ("dp", "tensor"))


def split_frame(rows):
    mine = lax.axis_index("tensor")
    half = rows.shape[0] // 2
    other = swap_half(rows[half:].astype(jnp.bfloat16)).astype(jnp.float32)
    own = rows[:half]
    return jnp.where(mine == 0, jnp.stack([own, other]), jnp.stack([other, own]))


def small_rows(flat, row_count):
    width = -(-flat.shape[-1] // (row_count * 128)) * 128
    short = row_count * width - flat.shape[-1]
    lead = [(0, 0)] * (flat.ndim - 1)
    return jnp.pad(flat, lead + [(0, short)]).reshape(flat.shape[:-1] + (row_count, width))


def adam_update(master, gradient, first_state, second_state, step_rate, decay_rate):
    mean_new = MEAN_DECAY * first_state + (1.0 - MEAN_DECAY) * gradient
    square_new = SQUARE_DECAY * second_state + (1.0 - SQUARE_DECAY) * gradient * gradient
    normal_step = (
        mean_new
        / (1.0 - MEAN_DECAY**STEP)
        / (jnp.sqrt(square_new / (1.0 - SQUARE_DECAY**STEP)) + ADAM_EPS)
    )
    updated = master - step_rate * (normal_step + decay_rate * master)
    return (mean_new, square_new, updated, updated.astype(jnp.bfloat16))


def local(
    frames,
    codes,
    clip_frames,
    out_cotangent,
    heads_weight,
    merge_weight,
    expand_weight,
    shrink_weight,
    vectors,
    encode_weight,
    codebook,
    decode_weight,
    heads_first,
    merge_first,
    expand_first,
    shrink_first,
    vectors_first,
    encode_first,
    codebook_first,
    decode_first,
    heads_second,
    merge_second,
    expand_second,
    shrink_second,
    vectors_second,
    encode_second,
    codebook_second,
    decode_second,
):
    shards = []
    for b in range(2):
        shards += pack_shard(heads_weight[b], merge_weight[b], expand_weight[b], shrink_weight[b])
    row_count = shards[0].shape[0]
    small_parts = [vectors, encode_weight, codebook, decode_weight]
    small_flat = jnp.concatenate([part.astype(jnp.bfloat16).reshape(-1) for part in small_parts])
    small_size = small_flat.shape[0]
    shards.append(small_rows(small_flat, row_count))
    code_tiles = codes.reshape(codes.shape[0], -1, 128)
    mine = lax.axis_index("tensor")
    gather = gather_tuned if is_tuned() else gather_plain
    full, frame_other, cotangent_other, codes_other = gather(
        shards, frames, out_cotangent, code_tiles
    )
    frame_rows = jnp.concatenate([pick_frame(frames, mine), frame_other], axis=0)
    cotangent = jnp.concatenate([pick_frame(out_cotangent, mine), cotangent_other], axis=0)
    code_ids = jnp.concatenate([pick_frame(code_tiles, mine), codes_other], axis=0).reshape(-1)
    device_count = lax.axis_size("dp") * lax.axis_size("tensor")
    small_all = full[6].reshape(2, -1, row_count * full[6].shape[2]).transpose(1, 0, 2)
    small_all = small_all.reshape(device_count, -1)
    small_low = []
    offset = 0
    for part, cut_dim in zip(small_parts, (1, 0, 0, 1)):
        piece = small_all[:, offset : offset + part.size].reshape((-1,) + part.shape)
        offset += part.size
        if cut_dim == 1:
            piece = piece.transpose(1, 0, 2).reshape(part.shape[0], -1)
        else:
            piece = piece.reshape(-1, part.shape[1])
        small_low.append(piece)
    vector_set = jnp.pad(small_low[0].astype(jnp.float32), ((0, 1), (0, 0)))
    code_width = small_low[1].shape[1]
    spare = PAIR - code_width
    encode_low = jnp.pad(small_low[1], ((0, 0), (0, spare)))
    decode_low = jnp.pad(small_low[3], ((0, spare), (0, 0)))
    entries = jnp.pad(jnp.take(small_low[2], code_ids, axis=0), ((0, 0), (0, spare)))
    frame_id = lax.axis_index("dp") * frames.shape[0] + lax.axis_index("tensor")
    clip_ends = jnp.cumsum(clip_frames)
    clip_id = jnp.sum((clip_ends <= frame_id).astype(jnp.int32))
    clip_slots = jnp.arange(clip_frames.shape[0], dtype=jnp.int32)
    clip_count = jnp.sum(jnp.where(clip_slots == clip_id, clip_frames, 0))
    clip_weight = 1.0 / clip_count.astype(jnp.float32)
    dframe, pulled, dencode, encoder_vectors, *encoder_grads = run_block(
        True, clip_weight.reshape(1, 1), frame_rows, entries, vector_set, encode_low, *full[0:3]
    )
    decoded, dentries, ddecode, decoder_vectors, *decoder_grads = run_block(
        False, cotangent, entries, pulled, vector_set, decode_low, *full[3:6]
    )
    dcodebook = jax.ops.segment_sum(
        dentries[:, :code_width], code_ids, num_segments=small_low[2].shape[0]
    )
    decoded_all = split_frame(decoded)
    frame_grads = split_frame(dframe)
    dvectors = (encoder_vectors + decoder_vectors)[: vectors.shape[0]]
    small_new = (dvectors, dencode.T, dcodebook, ddecode)
    columns = []
    for gradient, part, cut_dim in zip(small_new, small_parts, (1, 0, 0, 1)):
        if cut_dim == 1:
            gradient = gradient.reshape(part.shape[0], device_count, -1).transpose(1, 0, 2)
        columns.append(gradient.reshape(device_count, -1).astype(jnp.bfloat16))
    small_grad = small_rows(jnp.concatenate(columns, axis=1), row_count)
    small_grad = small_grad.reshape((-1, 2) + small_grad.shape[1:]).transpose(1, 0, 2, 3)
    small_grad = small_grad.reshape(2, -1, small_grad.shape[3])
    partials = encoder_grads + decoder_grads + [small_grad]
    reduce = reduce_tuned if is_tuned() else reduce_plain
    sums, squares = reduce(partials)
    reduced = [unpack_shard(sums[0:3]), unpack_shard(sums[3:6])]
    block_grads = [jnp.stack([first, second]) for first, second in zip(*reduced)]
    small_sum = sums[6].reshape(-1)[:small_size]
    small_grads = []
    offset = 0
    for part in small_parts:
        small_grads.append(small_sum[offset : offset + part.size].reshape(part.shape))
        offset += part.size
    gradients = tuple(block_grads) + tuple(small_grads)
    norm_before = jnp.sqrt(squares)
    factor = MAX_NORM / jnp.maximum(norm_before, MAX_NORM)
    masters = (
        heads_weight,
        merge_weight,
        expand_weight,
        shrink_weight,
        vectors,
        encode_weight,
        codebook,
        decode_weight,
    )
    firsts = (
        heads_first,
        merge_first,
        expand_first,
        shrink_first,
        vectors_first,
        encode_first,
        codebook_first,
        decode_first,
    )
    seconds = (
        heads_second,
        merge_second,
        expand_second,
        shrink_second,
        vectors_second,
        encode_second,
        codebook_second,
        decode_second,
    )
    updates = [
        adam_update(
            masters[member],
            gradients[member] * factor,
            firsts[member],
            seconds[member],
            RATES[member],
            DECAYS[member],
        )
        for member in range(8)
    ]
    return (
        decoded_all,
        frame_grads,
        norm_before,
        updates[0][0],
        updates[0][1],
        updates[0][2],
        updates[0][3],
        updates[1][0],
        updates[1][1],
        updates[1][2],
        updates[1][3],
        updates[2][0],
        updates[2][1],
        updates[2][2],
        updates[2][3],
        updates[3][0],
        updates[3][1],
        updates[3][2],
        updates[3][3],
        updates[4][0],
        updates[4][1],
        updates[4][2],
        updates[4][3],
        updates[5][0],
        updates[5][1],
        updates[5][2],
        updates[5][3],
        updates[6][0],
        updates[6][1],
        updates[6][2],
        updates[6][3],
        updates[7][0],
        updates[7][1],
        updates[7][2],
        updates[7][3],
    )


def solution(mesh):
    return jax.shard_map(
        local,
        mesh=mesh,
        in_specs=(
            P("dp", "tensor", None),
            P("dp", "tensor"),
            P(),
            P("dp", "tensor", None),
            P(None, None, "dp", "tensor"),
            P(None, "tensor", "dp"),
            P(None, "dp", "tensor"),
            P(None, "tensor", "dp"),
            P(None, ("dp", "tensor")),
            P(("dp", "tensor"), None),
            P(("dp", "tensor"), None),
            P(None, ("dp", "tensor")),
            P(None, None, "dp", "tensor"),
            P(None, "tensor", "dp"),
            P(None, "dp", "tensor"),
            P(None, "tensor", "dp"),
            P(None, ("dp", "tensor")),
            P(("dp", "tensor"), None),
            P(("dp", "tensor"), None),
            P(None, ("dp", "tensor")),
            P(None, None, "dp", "tensor"),
            P(None, "tensor", "dp"),
            P(None, "dp", "tensor"),
            P(None, "tensor", "dp"),
            P(None, ("dp", "tensor")),
            P(("dp", "tensor"), None),
            P(("dp", "tensor"), None),
            P(None, ("dp", "tensor")),
        ),
        out_specs=(
            P("dp", "tensor", None),
            P("dp", "tensor", None),
            P(),
            P(None, None, "dp", "tensor"),
            P(None, None, "dp", "tensor"),
            P(None, None, "dp", "tensor"),
            P(None, None, "dp", "tensor"),
            P(None, "tensor", "dp"),
            P(None, "tensor", "dp"),
            P(None, "tensor", "dp"),
            P(None, "tensor", "dp"),
            P(None, "dp", "tensor"),
            P(None, "dp", "tensor"),
            P(None, "dp", "tensor"),
            P(None, "dp", "tensor"),
            P(None, "tensor", "dp"),
            P(None, "tensor", "dp"),
            P(None, "tensor", "dp"),
            P(None, "tensor", "dp"),
            P(None, ("dp", "tensor")),
            P(None, ("dp", "tensor")),
            P(None, ("dp", "tensor")),
            P(None, ("dp", "tensor")),
            P(("dp", "tensor"), None),
            P(("dp", "tensor"), None),
            P(("dp", "tensor"), None),
            P(("dp", "tensor"), None),
            P(("dp", "tensor"), None),
            P(("dp", "tensor"), None),
            P(("dp", "tensor"), None),
            P(("dp", "tensor"), None),
            P(None, ("dp", "tensor")),
            P(None, ("dp", "tensor")),
            P(None, ("dp", "tensor")),
            P(None, ("dp", "tensor")),
        ),
        check_vma=False,
    )
```

```python
import functools

import jax
import jax.numpy as jnp
from jax import lax
from jax.experimental import pallas as pl
from jax.experimental.pallas import tpu as pltpu
from jax.sharding import PartitionSpec as P

HEAD_DIM = 64
STEP = 10


EPS_NORM = 1e-05
EPS_UNIT = 1e-06
COMMIT_WEIGHT = 100.0
MAX_NORM = 1.0
MEAN_DECAY = 0.9
SQUARE_DECAY = 0.95
ADAM_EPS = 1e-08
RATES = (0.1, 0.5, 0.1, 0.05, 1.0, 0.1, 1.0, 0.3)
DECAYS = (0.1, 0.1, 0.1, 0.1, 0.0, 0.1, 0.1, 0.1)

NT = (((1,), (1,)), ((), ()))
NN = (((1,), (0,)), ((), ()))
MESH = pl.DeviceIdType.MESH
PAIR = 128
WIDTH = 512
HIDDEN = 2048
CODE = 32
VEC_ROW = 32
DECODE_ROW = 64
SPLIT = (2, 4, 2, 2)
GELU_SCALE = (2.0 / 3.141592653589793) ** 0.5
GELU_CUBE = 0.044715
PARTS = ("even", "odd", "merge", "expand", "shrink")
COLUMNS = (384, 384, 256, 1024, 1024)


def mxu(first, second, dims=NN):
    return lax.dot_general(first, second, dims, preferred_element_type=jnp.float32)


def low(values):
    return values.astype(jnp.bfloat16)


def wide(values):
    return values.astype(jnp.float32)


def two_low(values):
    top = low(values)
    return top, low(values - wide(top))


def head_mask(shape, head):
    return (lax.broadcasted_iota(jnp.int32, shape, 1) // HEAD_DIM) == head


def keep_head(values, head):
    return jnp.where(head_mask(values.shape, head), values, jnp.zeros_like(values))


def norm_parts(rows):
    center = rows - jnp.mean(rows, axis=-1, keepdims=True)
    spread = jnp.mean(center * center, axis=-1, keepdims=True)
    scale = lax.rsqrt(spread + EPS_NORM)
    return center * scale, scale


def norm_back(xhat, scale, gain, grad):
    dxhat = grad * gain
    mean_grad = jnp.mean(dxhat, axis=-1, keepdims=True)
    mean_cross = jnp.mean(dxhat * xhat, axis=-1, keepdims=True)
    return scale * (dxhat - mean_grad - xhat * mean_cross)


def unit_scale(values):
    return lax.rsqrt(jnp.sum(values * values, axis=-1, keepdims=True) + EPS_UNIT)


def unit_back(values, grad):
    inverse = unit_scale(values)
    cross = jnp.sum(values * grad, axis=-1, keepdims=True)
    return inverse * grad - values * (inverse * inverse * inverse * cross)


def add_row(ref, row, values):
    ref[row : row + 1, :] += jnp.sum(values, axis=0, keepdims=True)


def tile_rows(step, tile):
    return pl.ds(pl.multiple_of(step * tile, tile), tile)


def half_of(ref, half, columns=slice(None)):
    if len(ref.shape) == 3:
        return ref[half, :, columns]
    values = ref[half, :, :, :, :, columns]
    return values.reshape(WIDTH, values.shape[-1])


def put_half(ref, half, columns, values):
    if len(ref.shape) == 3:
        ref[half, :, columns] = values
    else:
        ref[half, :, :, :, :, columns] = values.reshape(ref.shape[1:5] + (values.shape[-1],))


def remote(src, dst, sems, slot, target):
    send, recv = sems
    return pltpu.make_async_remote_copy(
        src_ref=src,
        dst_ref=dst,
        send_sem=send.at[slot],
        recv_sem=recv.at[slot],
        device_id=target,
        device_id_type=MESH,
    )


def coordinates():
    dp_index = lax.axis_index("dp")
    y = lax.axis_index("tensor")
    return dp_index // 4, (dp_index // 2) % 2, dp_index % 2, y


def partners(z, x, c, y):
    along_z = [(((z + step) % 4) * 4 + x * 2 + c, y) for step in (1, 2, 3)]
    along_x = (z * 4 + (1 - x) * 2 + c, y)
    along_y = (z * 4 + x * 2 + c, 1 - y)
    along_core = (z * 4 + x * 2 + (1 - c), y)
    return along_z, along_x, along_y, along_core


def octet(z, x, c, y):
    places = [(dx, dy, dc) for dx in (0, 1) for dy in (0, 1) for dc in (0, 1)][1:]
    return [
        (z * 4 + ((x + dx) % 2) * 2 + (c + dc) % 2, (y + dy) % 2) for dx, dy, dc in places
    ]


def greet(targets):
    barrier = pltpu.get_barrier_semaphore()
    for target in targets:
        pl.semaphore_signal(barrier, inc=1, device_id=target, device_id_type=MESH)
    return functools.partial(pl.semaphore_wait, barrier, len(targets))


def cuts_of(rows):
    if rows < 32:
        return ((0, rows, True),)
    middle = rows // 32 * 16
    return ((0, middle, True), (middle, rows, False))


class GatherFlow:
    def __init__(self, shard, out, local_sem, sems, slot):
        z, x, c, y = coordinates()
        along_z, along_x, along_y, along_core = partners(z, x, c, y)
        mine = out.at[y, z, x, c]
        column = out.at[y, :, x, c]
        self.own = pltpu.make_async_copy(shard, mine, local_sem.at[slot])
        self.first = [remote(shard, mine, sems, (slot, k), along_z[k]) for k in range(3)]
        self.core_first = [remote(column, column, sems, (slot, 3), along_core)]
        self.second, self.third, self.core_second, self.core_third = [], [], [], []
        for n, (start, stop, by_x) in enumerate(cuts_of(shard.shape[0])):
            rows = slice(start, stop)
            part = out.at[y, :, x, c, rows]
            plane = out.at[y, :, :, c, rows] if by_x else out.at[:, :, x, c, rows]
            got_second = out.at[y, :, 1 - x, c, rows] if by_x else out.at[1 - y, :, x, c, rows]
            got_third = out.at[1 - y, :, :, c, rows] if by_x else out.at[:, :, 1 - x, c, rows]
            near, far = (along_x, along_y) if by_x else (along_y, along_x)
            base = 4 + 4 * n
            self.second.append(remote(part, part, sems, (slot, base), near))
            self.third.append(remote(plane, plane, sems, (slot, base + 1), far))
            self.core_second.append(remote(got_second, got_second, sems, (slot, base + 2), along_core))
            self.core_third.append(remote(got_third, got_third, sems, (slot, base + 3), along_core))

    def begin(self):
        self.own.start()
        for copy in self.first:
            copy.start()

    def after_first(self):
        self.own.wait()
        for copy in self.first:
            copy.wait_recv()
        for copy in self.second + self.core_first:
            copy.start()

    def after_second(self):
        for copy in self.second:
            copy.wait_recv()
        for copy in self.third + self.core_second:
            copy.start()

    def after_third(self):
        for copy in self.third:
            copy.wait_recv()
        for copy in self.core_third:
            copy.start()

    def arrived(self):
        for copy in self.core_first + self.core_second + self.core_third:
            copy.wait_recv()

    def sent(self):
        for copy in self.first + self.second + self.third:
            copy.wait_send()
        for copy in self.core_first + self.core_second + self.core_third:
            copy.wait_send()


class ReduceFlow:
    def __init__(self, partial, held, scratch, local_sem, sems, slot, out):
        z, x, c, y = coordinates()
        along_z, along_x, along_y, along_core = partners(z, x, c, y)
        from_core, from_second, from_first, *from_third = scratch
        self.scratch, self.place, self.out = scratch, (z, x, y), out
        self.own = None
        if held is None:
            self.held, self.tail = partial, (c,)
        else:
            self.held, self.tail = held, ()
            self.own = pltpu.make_async_copy(partial.at[:, :, :, c], held, local_sem.at[slot])
        every = slice(None)
        self.cuts = cuts_of(partial.shape[4])

        def part(*index):
            return self.held.at[index[:3] + self.tail + index[3:]]

        self.core = remote(partial.at[:, :, :, 1 - c], from_core, sems, (slot, 0), along_core)
        self.third, self.second = [], []
        for n, (start, stop, by_x) in enumerate(self.cuts):
            rows = slice(start, stop)
            if by_x:
                leaving, target = part(1 - y, every, every, rows), along_y
                going, near = part(y, every, 1 - x, rows), along_x
            else:
                leaving, target = part(every, every, 1 - x, rows), along_x
                going, near = part(1 - y, every, x, rows), along_y
            self.third.append(remote(leaving, from_third[n], sems, (slot, 1 + n), target))
            landing = from_second.at[:, rows]
            self.second.append(remote(going, landing, sems, (slot, 3 + n), near))
        self.first = [
            remote(
                part(y, (z + k + 1) % 4, x), from_first.at[k], sems, (slot, 5 + k), along_z[k]
            )
            for k in range(3)
        ]

    def begin(self):
        self.core.start()
        if self.own is not None:
            self.own.start()

    def add(self, index, rows, values):
        place = index + self.tail + (rows,)
        self.held[place] = self.held[place] + values

    def after_core(self):
        self.core.wait_recv()
        if self.own is not None:
            self.own.wait()

        @pl.loop(0, 16)
        def _(n):
            index = (n // 8, (n // 2) % 4, n % 2)
            self.add(index, slice(None), self.scratch[0][index])

        for copy in self.third:
            copy.start()

    def after_third(self):
        z, x, y = self.place
        for cut, (start, stop, by_x) in enumerate(self.cuts):
            self.third[cut].wait_recv()

            @pl.loop(0, 8)
            def _(n):
                index = (n // 2, n % 2) if by_x else (n // 4, n % 4)
                place = (y,) + index if by_x else index + (x,)
                self.add(place, slice(start, stop), self.scratch[3 + cut][index])

            self.second[cut].start()

    def after_second(self):
        for copy in self.second:
            copy.wait_recv()
        z, x, y = self.place
        for k in range(4):
            self.add((y, k, x), slice(None), self.scratch[1][k])
        for copy in self.first:
            copy.start()

    def finish(self):
        z, x, y = self.place
        result = wide(self.held[(y, z, x) + self.tail])
        for k in range(3):
            self.first[k].wait_recv()
            result = result + wide(self.scratch[2][k])
        self.out[...] = result

    def sent(self):
        for copy in [self.core] + self.third + self.second + self.first:
            copy.wait_send()


def dma(*shape):
    return pltpu.SemaphoreType.DMA(shape)


def reduce_scratch(size, dtype):
    shapes = [(2, 4, 2) + size, (4,) + size, (3,) + size]
    for start, stop, by_x in cuts_of(size[0]):
        shapes.append(((4, 2) if by_x else (2, 4)) + (stop - start, size[1]))
    return [pltpu.VMEM(shape, dtype) for shape in shapes]


def run_plan(plan, flows, name):
    for step in plan.get(name, ()):
        action, *members = step
        for member in members:
            if member in flows:
                getattr(flows[member], action)()


def pair_plan(plan, flows, name):
    def run(count):
        for n in range(4):
            if f"{name}{n}" in plan:
                pl.when(count == n)(functools.partial(run_plan, plan, flows, f"{name}{n}"))

    return run


def pair_place(count):
    pair = (count % 2) * 2 + count // 2
    wide_start = pl.multiple_of(pair * 384, 384)
    return pair, wide_start, pl.ds(pl.multiple_of(pair * PAIR, PAIR), PAIR)


def pair_columns(wide_start):
    return [pl.ds(pl.multiple_of(wide_start + member * PAIR, PAIR), PAIR) for member in range(3)]


def norm_stage(x_rows, vec, base, n_ref, tile):
    @pl.loop(0, n_ref.shape[0] // tile)
    def _(step):
        rows = tile_rows(step, tile)
        xhat, _ = norm_parts(x_rows(rows, step))
        n_ref[rows, :] = low(xhat * vec[base : base + 1, :] + vec[base + 1 : base + 2, :])


def project_stage(n_ref, weights, p_ref, tile, odd):
    @pl.loop(0, n_ref.shape[0] // tile)
    def _(step):
        rows = tile_rows(step, tile)
        normed = n_ref[rows, :]
        for half in range(2):
            start = (half * 2 + odd) * 384
            p_ref[rows, start : start + 384] = low(mxu(normed, half_of(weights[odd], half)))


def attend_stage(p_ref, mix_ref, lse_ref, tile, first, last, after_pair):
    length = p_ref.shape[0]

    @pl.loop(first, last)
    def _(count):
        pair, wide_start, columns = pair_place(count)
        query_at, key_at, value_at = pair_columns(wide_start)
        keys = p_ref[:, key_at] * (HEAD_DIM**-0.5)
        values = p_ref[:, value_at]
        for start in range(0, length, tile):
            query = p_ref[start : start + tile, query_at]
            out = None
            for head in range(2):
                ones_beside = jnp.where(
                    head_mask(values.shape, head), values, jnp.ones_like(values)
                )
                scores = mxu(keep_head(query, head), keys, NT)
                top = jnp.max(scores, axis=1, keepdims=True)
                raised = low(jnp.exp(scores - top))
                mixed = mxu(raised, ones_beside)
                total = pltpu.roll(mixed, HEAD_DIM, 1)
                mixed = mixed / total
                log_sum = top + jnp.log(total)
                if out is None:
                    out, log_sums = mixed, log_sum
                else:
                    is_first = head_mask(mixed.shape, 0)
                    out = jnp.where(is_first, out, mixed)
                    log_sums = jnp.where(is_first, log_sums, log_sum)
            mix_ref[start : start + tile, columns] = low(out)
            turned = log_sums.T
            for head in range(2):
                lse_ref[pair * 2 + head, :, start : start + tile] = jnp.broadcast_to(
                    turned[head * HEAD_DIM : head * HEAD_DIM + 1], (8, tile)
                )
        after_pair(count)


def expand_stage(x_rows, mix_ref, vec, base, merge_w, expand_w, h_ref, nm_ref, slope_ref, act_ref, tile):
    @pl.loop(0, h_ref.shape[0] // tile)
    def _(step):
        rows = tile_rows(step, tile)
        hidden = x_rows(rows, step) + vec[base + 2 : base + 3, :]
        for half in range(2):
            hidden = hidden + mxu(
                mix_ref[rows, half * 256 : half * 256 + 256], half_of(merge_w, half), NT
            )
        h_ref[rows, :] = hidden
        xhat, _ = norm_parts(hidden)
        normed = low(xhat * vec[base + 3 : base + 4, :] + vec[base + 4 : base + 5, :])
        nm_ref[rows, :] = normed
        for half in range(2):
            for start in range(0, 1024, 512):
                values = mxu(normed, half_of(expand_w, half, slice(start, start + 512)))
                place = slice(half * 1024 + start, half * 1024 + start + 512)
                square = values * values
                bend = jnp.tanh(values * (GELU_SCALE + (GELU_SCALE * GELU_CUBE) * square))
                share = 0.5 + 0.5 * bend
                active = values * share
                act_ref[rows, place] = low(active)
                slope_ref[rows, place] = low(
                    share
                    + (active - active * share)
                    * (2.0 * GELU_SCALE + (6.0 * GELU_SCALE * GELU_CUBE) * square)
                )


def shrink_stage(h_ref, act_ref, vec, base, shrink_w, tile, give):
    @pl.loop(0, h_ref.shape[0] // tile)
    def _(step):
        rows = tile_rows(step, tile)
        out = h_ref[rows, :] + vec[base + 5 : base + 6, :]
        for half in range(2):
            out = out + mxu(
                act_ref[rows, half * 1024 : half * 1024 + 1024], half_of(shrink_w, half), NT
            )
        give(rows, out, step)


def mlp_back_stage(
    dout_rows, h_ref, slope_ref, vec, base, merge_w, expand_w, shrink_w, dmix_ref, vg_ref, tile
):
    @pl.loop(0, h_ref.shape[0] // tile)
    def _(step):
        rows = tile_rows(step, tile)
        dout = wide(dout_rows(rows, step))
        dout_low = low(dout)
        dnormed = None
        for half in range(2):
            for start in range(0, 1024, 512):
                place = slice(half * 1024 + start, half * 1024 + start + 512)
                dactive = mxu(dout_low, half_of(shrink_w, half, slice(start, start + 512)))
                dexpanded = low(dactive * wide(slope_ref[rows, place]))
                slope_ref[rows, place] = dexpanded
                part = mxu(dexpanded, half_of(expand_w, half, slice(start, start + 512)), NT)
                dnormed = part if dnormed is None else dnormed + part
        xhat, scale = norm_parts(h_ref[rows, :])
        dhidden = dout + norm_back(xhat, scale, vec[base + 3 : base + 4, :], dnormed)
        h_ref[rows, :] = dhidden
        dhidden_low = low(dhidden)
        for half in range(2):
            dmix_ref[rows, half * 256 : half * 256 + 256] = low(
                mxu(dhidden_low, half_of(merge_w, half))
            )
        add_row(vg_ref, base + 2, dhidden)
        add_row(vg_ref, base + 3, dnormed * xhat)
        add_row(vg_ref, base + 4, dnormed)
        add_row(vg_ref, base + 5, dout)


def turn_stage(read, turned_ref):
    length = turned_ref.shape[1]
    for start in range(0, length, 256):
        turned_ref[:, start : start + 256] = low(read(start, start + 256)).T


def weight_grad_stage(turned_ref, right_ref, out_ref, half, first, width, chunk):
    for start in range(0, width, chunk):
        product = mxu(turned_ref[...], right_ref[:, first + start : first + start + chunk])
        put_half(out_ref, half, slice(start, start + chunk), low(product))


def attend_back_stage(
    p_ref, mix_ref, dmix_ref, lse_ref, dk_acc, dv_acc, tile, first, last, after_pair
):
    length = p_ref.shape[0]

    @pl.loop(first, last)
    def _(count):
        pair, wide_start, columns = pair_place(count)
        query_at, key_at, value_at = pair_columns(wide_start)
        keys = p_ref[:, key_at] * (HEAD_DIM**-0.5)
        values = p_ref[:, value_at]
        keys_turned = keys.T
        for start in range(0, length, tile):
            rows = slice(start, start + tile)
            query = p_ref[rows, query_at]
            dmix = dmix_ref[rows, columns]
            inner = (wide(dmix) * wide(mix_ref[rows, columns])).T
            dquery, dkeys, dvalues = [], None, None
            for head in range(2):
                span = slice(head * HEAD_DIM, head * HEAD_DIM + HEAD_DIM)
                query_here = keep_head(query, head)
                dmix_here = keep_head(dmix, head)
                delta = jnp.sum(inner[span], axis=0, keepdims=True)
                log_sum = lse_ref[pair * 2 + head, 0:1, rows]
                attend = jnp.exp(mxu(keys, query_here, NT) - log_sum)
                dscores = low(attend * (mxu(values, dmix_here, NT) - delta))
                part = mxu(low(attend), dmix_here)
                dvalues = part if dvalues is None else dvalues + part
                part = mxu(dscores, query_here)
                dkeys = part if dkeys is None else dkeys + part
                dquery.append(mxu(keys_turned[span], dscores))
            p_ref[rows, query_at] = low(jnp.concatenate(dquery, axis=0).T)
            if start == 0:
                dk_acc[...] = dkeys
                dv_acc[...] = dvalues
            elif start + tile < length:
                dk_acc[...] += dkeys
                dv_acc[...] += dvalues
            else:
                p_ref[:, key_at] = low((dk_acc[...] + dkeys) * (HEAD_DIM**-0.5))
                p_ref[:, value_at] = low(dv_acc[...] + dvalues)
        after_pair(count)


def project_back_tile(step, tile, x_rows, h_ref, p_ref, vec, base, weights, vg_ref, give):
    rows = slice(step * tile, step * tile + tile)
    dnormed = None
    for odd in range(2):
        for half in range(2):
            start = (half * 2 + odd) * 384
            product = mxu(p_ref[rows, start : start + 384], half_of(weights[odd], half), NT)
            dnormed = product if dnormed is None else dnormed + product
    xhat, scale = norm_parts(x_rows(rows, step))
    dx = h_ref[rows, :] + norm_back(xhat, scale, vec[base : base + 1, :], dnormed)
    add_row(vg_ref, base, dnormed * xhat)
    add_row(vg_ref, base + 1, dnormed)
    give(rows, dx)


def code_place(codes, tuned):
    if tuned:
        owner = codes // 256
        return ((owner % 2) * 16 + owner // 2) * 64 + codes % 64, (codes // 64) % 4
    return codes % 2048, codes // 2048


def one_hot(place):
    shape = (2048, place.shape[1])
    return low(jnp.where(lax.broadcasted_iota(jnp.int32, shape, 0) == place, 1.0, 0.0))


def in_group(group, values):
    rows = lax.broadcasted_iota(jnp.int32, values.shape, 0) // CODE
    return jnp.where(rows == group, values, jnp.zeros_like(values))


def look_up_stage(codes, codebook, entries_ref, tuned):
    tile = 256
    book_turned = codebook.T
    for start in range(0, entries_ref.shape[0], tile):
        place, group = code_place(codes(start, tile), tuned)
        found = in_group(group, mxu(book_turned, one_hot(place)))
        found = found[0:32] + found[32:64] + found[64:96] + found[96:128]
        found = jnp.concatenate([found, jnp.zeros((96, tile), jnp.float32)], axis=0)
        entries_ref[start : start + tile, :] = low(found.T)


def scatter_stage(codes, dentries_ref, give, tuned):
    tile = 512
    total = None
    for start in range(0, dentries_ref.shape[0], tile):
        place, group = code_place(codes(start, tile), tuned)
        turned = low(dentries_ref[start : start + tile, :].T[0:CODE])
        placed = in_group(group, wide(jnp.concatenate([turned] * 4, axis=0)))
        part = mxu(one_hot(place), low(placed), NT)
        total = part if total is None else total + part
    give(low(total))


def square_sum(values):
    rows, width = values.shape
    values = values * values
    total = jnp.zeros((8, 128), jnp.float32)
    for r in range(0, rows, 8):
        for w in range(0, width, 128):
            total = total + values[r : r + 8, w : w + 128]
    return total


def sum_over_devices(square, squares, sums):
    z, x, c, y = coordinates()
    total = jnp.broadcast_to(jnp.sum(square, keepdims=True), (8, 128))
    stage = 0
    for n, targets in enumerate((octet(z, x, c, y), partners(z, x, c, y)[0])):
        squares[n] = total
        copies = []
        for target in targets:
            copy = remote(squares.at[n], squares.at[2 + stage], sums, stage, target)
            copy.start()
            copies.append((copy, 2 + stage))
            stage += 1
        for copy, place in copies:
            copy.wait()
            total = total + squares[place]
    return total


class Swap:
    def __init__(self, source, target, sems, local_sem, slot):
        z, x, c, y = coordinates()
        along_y = partners(z, x, c, y)[2]
        self.own = pltpu.make_async_copy(source.at[y], target.at[0], local_sem.at[slot])
        self.other = remote(source.at[1 - y], target.at[1], sems, slot, along_y)

    def begin(self):
        self.other.start()
        self.own.start()

    def arrived(self):
        self.own.wait()
        self.other.wait_recv()

    def sent(self):
        self.other.wait_send()


class Send:
    def __init__(self, give, got, sems, slot):
        z, x, c, y = coordinates()
        self.other = remote(give, got, sems, slot, partners(z, x, c, y)[2])

    def begin(self):
        self.other.start()

    def arrived(self):
        self.other.wait_recv()

    def sent(self):
        self.other.wait_send()


DECODER_PLAN = {
    "start": [
        ("begin", "codes", "small", "even", "odd", "cot"),
    ],
    "packed": [
        ("after_first", "small", "even", "odd"),
        ("begin", "expand", "merge"),
        ("after_second", "small", "even", "odd"),
        ("after_third", "small"),
        ("arrived", "small", "codes"),
    ],
    "look": [
        ("after_third", "even", "odd"),
        ("after_first", "expand", "merge"),
        ("begin", "shrink"),
        ("arrived", "even", "odd"),
    ],
    "attend0": [
        ("after_second", "expand", "merge"),
    ],
    "attend1": [
        ("after_first", "shrink"),
        ("begin", "e_even", "e_odd"),
    ],
    "attend2": [
        ("after_third", "expand", "merge"),
        ("after_second", "shrink"),
        ("begin", "e_merge", "e_expand"),
    ],
    "attend3": [
        ("arrived", "merge", "expand"),
    ],
    "expand": [
        ("after_third", "shrink"),
        ("after_first", "e_even", "e_odd", "e_merge", "e_expand"),
        ("arrived", "shrink"),
    ],
    "shrink": [
        ("begin", "e_shrink"),
        ("arrived", "cot"),
    ],
    "mlp_back": [
        ("after_second", "e_even", "e_odd", "e_merge", "e_expand"),
    ],
    "dexpand": [
        ("after_first", "e_shrink"),
    ],
    "back0": [
        ("after_third", "e_even", "e_odd", "e_merge", "e_expand"),
        ("after_second", "e_shrink"),
        ("begin", "frame"),
    ],
    "back2": [
        ("after_third", "e_shrink"),
    ],
    "end": [
        ("arrived", "e_even", "e_odd", "e_merge", "e_expand", "e_shrink", "frame"),
        ("sent", "codes", "small", "even", "odd", "merge", "expand", "shrink", "cot", "frame"),
        ("sent", "e_even", "e_odd", "e_merge", "e_expand", "e_shrink"),
    ],
}
ENCODER_PLAN = {
    "start": [
        ("begin", "d_shrink", "d_expand", "d_merge", "d_even", "d_odd"),
    ],
    "project": [
        ("after_core", "d_shrink"),
    ],
    "attend0": [
        ("after_core", "d_expand", "d_merge"),
    ],
    "attend1": [
        ("after_core", "d_even", "d_odd"),
    ],
    "attend2": [
        ("after_third", "d_shrink"),
    ],
    "attend3": [
        ("after_third", "d_expand", "d_merge"),
    ],
    "expand": [
        ("after_second", "d_shrink"),
        ("after_third", "d_even", "d_odd"),
    ],
    "shrink": [
        ("after_second", "d_expand", "d_merge"),
        ("finish", "d_shrink"),
        ("begin", "decoded"),
    ],
    "mlp_back": [
        ("after_second", "d_even", "d_odd"),
        ("finish", "d_expand", "d_merge"),
        ("begin", "book"),
    ],
    "dshrink": [
        ("after_core", "book"),
        ("begin", "shrink"),
        ("finish", "d_even", "d_odd"),
    ],
    "dexpand": [
        ("begin", "expand"),
    ],
    "dmerge": [
        ("begin", "merge"),
        ("after_third", "book"),
        ("after_core", "shrink"),
    ],
    "back0": [
        ("after_second", "book"),
        ("after_core", "expand", "merge"),
    ],
    "back1": [
        ("finish", "book"),
        ("after_third", "shrink"),
    ],
    "deven": [
        ("begin", "even"),
    ],
    "back2": [
        ("after_third", "expand", "merge"),
        ("after_second", "shrink"),
        ("after_core", "even"),
    ],
    "back3": [
        ("after_second", "expand", "merge"),
        ("after_third", "even"),
        ("finish", "shrink"),
    ],
    "dodd": [
        ("begin", "odd"),
        ("after_core", "odd"),
    ],
    "far": [
        ("after_second", "even"),
    ],
    "near": [
        ("finish", "expand", "merge"),
    ],
    "vectors": [
        ("begin", "small"),
        ("after_third", "odd"),
        ("begin", "dframe"),
        ("after_core", "small"),
        ("finish", "even"),
        ("after_third", "small"),
        ("after_second", "odd"),
        ("after_second", "small"),
    ],
    "last": [
        ("finish", "odd", "small"),
    ],
    "end": [
        ("arrived", "decoded", "dframe"),
        ("sent", "d_shrink", "d_expand", "d_merge", "d_even", "d_odd", "decoded", "dframe"),
        ("sent", "even", "odd", "merge", "expand", "shrink", "small", "book"),
    ],
}


def name_refs(names, refs, start):
    return dict(zip(names, refs[start : start + len(names)])), start + len(names)


BLOCK_SCRATCH = ("n", "p", "mix", "lse", "h", "nm", "slope", "act", "dmix", "dk", "dv", "turned")


def block_scratch(length):
    f32, bf16 = jnp.float32, jnp.bfloat16
    shapes = [
        ((length, WIDTH), bf16),
        ((length, 3 * WIDTH), bf16),
        ((length, WIDTH), bf16),
        ((8, 8, length), f32),
        ((length, WIDTH), f32),
        ((length, WIDTH), bf16),
        ((length, HIDDEN), bf16),
        ((length, HIDDEN), bf16),
        ((length, WIDTH), bf16),
        ((length, PAIR), f32),
        ((length, PAIR), f32),
        ((WIDTH, length), bf16),
    ]
    return [pltpu.VMEM(shape, dtype) for shape, dtype in shapes]


def pack_heads(raw, shards, prefix, b):
    for odd, name in enumerate(("even", "odd")):
        for member in range(3):
            shards[prefix + name][:, member * PAIR : member * PAIR + PAIR] = low(
                raw["heads"][b, member, :, odd * PAIR : odd * PAIR + PAIR]
            )


def pack_rest(raw, shards, prefix, b):
    for name in ("merge", "expand", "shrink"):
        shards[prefix + name][...] = low(raw[name][b])


def pack_small(raw, small, turn):
    turn[...] = jnp.zeros_like(turn)
    turn[VEC_ROW : VEC_ROW + 15, 0:16] = raw["vectors"][...]
    rows = turn[...].T[0:16]
    blank = jnp.zeros((16, CODE), jnp.float32)
    sides = jnp.concatenate([raw["encode"][...], blank, raw["decode"][...], blank], axis=1)
    small[0:16, :] = low(rows + sides)
    codebook = raw["codebook"][...].T
    book = [codebook[j * 64 : j * 64 + 64, :] for j in range(4)]
    small[16:80, :] = low(jnp.concatenate(book, axis=1))


RAW = ("heads", "merge", "expand", "shrink", "vectors", "encode", "codebook", "decode")
E_PARTS = tuple("e_" + name for name in PARTS)
D_PARTS = tuple("d_" + name for name in PARTS)


def decoder_kernel(tuned, *refs):
    at = 0
    if tuned:
        (codes_in, frames_in, cot_in), at = refs[:3], 3
        raw, at = name_refs(RAW, refs, at)
    else:
        (codes, cot, ved, book), at = refs[:4], 4
        weights, at = name_refs(PARTS, refs, at)
    (entries, dchosen, vg, ddecode), at = refs[at : at + 4], at + 4
    grads, at = name_refs(PARTS, refs, at)
    if tuned:
        (near, far, frame, codes_out, ved), at = refs[at : at + 5], at + 5
        moved, at = name_refs(E_PARTS, refs, at)
    else:
        (out_buf,), at = refs[at : at + 1], at + 1
    s, at = name_refs(BLOCK_SCRATCH, refs, at)
    (x_buf, vec), at = refs[at : at + 2], at + 2
    flows = {}
    tile = 512
    if tuned:
        (cot, codes, code_give, turn), at = refs[at : at + 4], at + 4
        shards, at = name_refs(PARTS + E_PARTS + ("small",), refs, at)
        weights, at = name_refs(PARTS + ("small",), refs, at)
        local_sem, send, recv, swap_local, swap_send, swap_recv = refs[at:]
        for slot, name in enumerate(PARTS + ("small",) + E_PARTS):
            target = moved[name] if name in moved else weights[name]
            flows[name] = GatherFlow(shards[name], target, local_sem, (send, recv), slot)
        swaps = (swap_send, swap_recv)
        flows["codes"] = Send(code_give, codes.at[1], swaps, 0)
        flows["cot"] = Swap(cot_in, cot, swaps, swap_local, 1)
        flows["frame"] = Swap(frames_in, frame, swaps, swap_local, 2)
        along_z, along_x, along_y, along_core = partners(*coordinates())
        greeted = greet(along_z + [along_x, along_y, along_core])
        pack_small(raw, shards["small"], turn)
        pack_heads(raw, shards, "", 1)
        y = lax.axis_index("tensor")
        codes[0] = jnp.where(y == 0, codes_in[0:1, :], codes_in[1:2, :])
        code_give[...] = jnp.where(y == 0, codes_in[1:2, :], codes_in[0:1, :])
        greeted()
    step = functools.partial(run_plan, DECODER_PLAN, flows)
    step("start")
    if tuned:
        pack_rest(raw, shards, "", 1)
        pack_heads(raw, shards, "e_", 0)
        pack_rest(raw, shards, "e_", 0)
        step("packed")
        for dp in range(16):
            for t in range(2):
                row = (dp * 2 + t) * 16
                ved[row : row + 16, :] = weights["small"][t, dp // 4, (dp // 2) % 2, dp % 2, 0:16, :]
        book_rows = weights["small"][:, :, :, :, 16:80, :].reshape(2048, PAIR)
        codes_out[...] = codes[...]
    else:
        book_rows = book[...]
    turned_small = wide(ved[...]).T
    vec[...] = turned_small[VEC_ROW : VEC_ROW + 16]
    decode = low(turned_small[DECODE_ROW : DECODE_ROW + CODE])
    decode = jnp.concatenate([decode, jnp.zeros((96, WIDTH), jnp.bfloat16)], axis=0)

    def read_codes(start, size):
        half, first = start // 512, start % 512
        return codes[half, :, first : first + size]

    vg[...] = jnp.zeros_like(vg)
    ddecode[...] = jnp.zeros_like(ddecode)
    look_up_stage(read_codes, book_rows, entries, tuned)
    values = wide(entries[...])
    x_buf[...] = mxu(low(values * unit_scale(values)), decode) + vec[14:15, :]
    base = 6
    x_rows = lambda rows, _: x_buf[rows, :]
    norm_stage(x_rows, vec, base, s["n"], tile)
    step("look")
    first_w = (weights["even"], weights["odd"])
    for odd in range(2):
        project_stage(s["n"], first_w, s["p"], tile, odd)
    step("project")
    attend_stage(
        s["p"], s["mix"], s["lse"], tile, 0, 4, pair_plan(DECODER_PLAN, flows, "attend")
    )
    expand_stage(
        x_rows, s["mix"], vec, base, weights["merge"], weights["expand"], s["h"], s["nm"],
        s["slope"], s["act"], tile,
    )
    step("expand")

    def give_out(rows, out, part):
        if not tuned:
            out_buf[rows, :] = out
            return

        @pl.when(part == 0)
        def _():
            near[...] = out

        @pl.when(part == 1)
        def _():
            far[...] = low(out)

    shrink_stage(s["h"], s["act"], vec, base, weights["shrink"], tile, give_out)
    step("shrink")
    mlp_back_stage(
        lambda rows, half: cot[half], s["h"], s["slope"], vec, base, weights["merge"],
        weights["expand"], weights["shrink"], s["dmix"], vg, tile,
    )
    step("mlp_back")
    turned = s["turned"]
    turn_stage(lambda a, b: cot[a // 512, a % 512 : a % 512 + 256, :], turned)
    for half in range(2):
        weight_grad_stage(turned, s["act"], grads["shrink"], half, half * 1024, 1024, 512)
    step("dshrink")
    turn_stage(lambda a, b: s["nm"][a:b, :], turned)
    for half in range(2):
        weight_grad_stage(turned, s["slope"], grads["expand"], half, half * 1024, 1024, 512)
    step("dexpand")
    turn_stage(lambda a, b: s["h"][a:b, :], turned)
    for half in range(2):
        weight_grad_stage(turned, s["mix"], grads["merge"], half, half * 256, 256, 256)
    attend_back_stage(
        s["p"], s["mix"], s["dmix"], s["lse"], s["dk"], s["dv"], tile, 0, 4,
        pair_plan(DECODER_PLAN, flows, "back"),
    )
    turn_stage(lambda a, b: s["n"][a:b, :], turned)
    for odd, name in enumerate(("even", "odd")):
        for half in range(2):
            weight_grad_stage(turned, s["p"], grads[name], half, (half * 2 + odd) * 384, 384, 384)

    def give_dx(rows, dx):
        add_row(vg, 14, dx)
        picked = wide(entries[rows, :])
        chosen_turned = low(picked * unit_scale(picked)).T[0:CODE]
        total = None
        for part in two_low(dx):
            ddecode[...] += mxu(chosen_turned, part)
            product = mxu(part, decode, NT)
            total = product if total is None else total + product
        dchosen[rows, :] = total

    for half in (1, 0):
        project_back_tile(
            half, tile, x_rows, s["h"], s["p"], vec, base, first_w, vg, give_dx
        )
    step("end")


def encoder_kernel(tuned, *refs):
    (clip_frames, codes, frame, entries, dchosen, ved), at = refs[:6], 6
    weights, at = name_refs(PARTS, refs, at)
    if tuned:
        (vg_other, ddecode, decoded_far), at = refs[at : at + 3], at + 3
        partial, at = name_refs(D_PARTS, refs, at)
        (decoded_got, dx_near, dx_got, norm), at = refs[at : at + 4], at + 4
        totals, at = name_refs(PARTS + ("book", "small") + D_PARTS, refs, at)
    else:
        (dx_buf, vg, dencode, dbook), at = refs[at : at + 4], at + 4
        grads, at = name_refs(PARTS, refs, at)
    s, at = name_refs(BLOCK_SCRATCH, refs, at)
    (vec, dout_buf, dentries), at = refs[at : at + 3], at + 3
    flows = {}
    tile = 512
    if tuned:
        (vg, dencode, give, collect, squares), at = refs[at : at + 5], at + 5
        grads, at = name_refs(PARTS + ("book", "small"), refs, at)
        held, at = name_refs(D_PARTS, refs, at)
        names = D_PARTS + PARTS + ("book", "small")
        receive = {}
        for name in PARTS + ("book", "small"):
            count = 3 + len(cuts_of(totals[name].shape[0]))
            receive[name], at = refs[at : at + count], at + count
        local_sem, send, recv, swap_send, swap_recv, sum_send, sum_recv = refs[at:]
        for slot, name in enumerate(names):
            source = partial[name] if name in partial else grads[name]
            flows[name] = ReduceFlow(
                source, held.get(name), receive[name.replace("d_", "")], local_sem, (send, recv),
                slot, totals[name],
            )
        swaps = (swap_send, swap_recv)
        flows["decoded"] = Send(decoded_far, decoded_got, swaps, 0)
        flows["dframe"] = Send(give, dx_got, swaps, 1)
        place = coordinates()
        greet(octet(*place) + partners(*place)[0])()
    step = functools.partial(run_plan, ENCODER_PLAN, flows)
    step("start")
    turned_small = wide(ved[...]).T
    vec[...] = turned_small[VEC_ROW : VEC_ROW + 16]
    encode = jnp.where(
        lax.broadcasted_iota(jnp.int32, ved.shape, 1) < CODE, ved[...], jnp.zeros_like(ved)
    )
    frame_id = lax.axis_index("dp") * 2 + lax.axis_index("tensor")
    clip_end, clip_count = 0, 1
    for clip in range(clip_frames.shape[0]):
        size = clip_frames[clip]
        inside = (frame_id >= clip_end) & (frame_id < clip_end + size)
        clip_count = jnp.where(inside, size, clip_count)
        clip_end = clip_end + size
    clip_weight = (2.0 * COMMIT_WEIGHT) / jnp.full((1, 1), clip_count).astype(jnp.float32)
    vg[...] = jnp.zeros_like(vg)
    dencode[...] = jnp.zeros_like(dencode)
    base = 0
    x_rows = lambda rows, half: wide(frame[half])
    norm_stage(x_rows, vec, base, s["n"], tile)
    first_w = (weights["even"], weights["odd"])
    for odd in range(2):
        project_stage(s["n"], first_w, s["p"], tile, odd)
    step("project")
    attend_stage(
        s["p"], s["mix"], s["lse"], tile, 0, 4, pair_plan(ENCODER_PLAN, flows, "attend")
    )
    expand_stage(
        x_rows, s["mix"], vec, base, weights["merge"], weights["expand"], s["h"], s["nm"],
        s["slope"], s["act"], tile,
    )
    step("expand")

    def give_out(rows, out, _):
        xhat, scale = norm_parts(out)
        normed = low(xhat * vec[12:13, :] + vec[13:14, :])
        raw = mxu(normed, encode)
        picked = wide(entries[rows, :])
        pull = clip_weight * (
            raw * unit_scale(raw) - picked * unit_scale(picked)
        )
        dentries[rows, :] = unit_back(picked, dchosen[rows, :] - pull)
        draw = unit_back(raw, pull)
        dnormed = None
        for part in two_low(draw):
            product = mxu(part, encode, NT)
            dnormed = product if dnormed is None else dnormed + product
            dencode[...] += mxu(part.T[0:CODE], normed)
        dout_buf[rows, :] = norm_back(xhat, scale, vec[12:13, :], dnormed)
        add_row(vg, 12, dnormed * xhat)
        add_row(vg, 13, dnormed)

    shrink_stage(s["h"], s["act"], vec, base, weights["shrink"], tile, give_out)
    step("shrink")

    def read_codes(start, size):
        half, first = start // 512, start % 512
        return codes[half, :, first : first + size]

    def give_book(total):
        if tuned:
            grads["book"][...] = total.reshape(SPLIT + (64, PAIR))
        else:
            dbook[...] = total

    scatter_stage(read_codes, dentries, give_book, tuned)
    mlp_back_stage(
        lambda rows, _: dout_buf[rows, :], s["h"], s["slope"], vec, base, weights["merge"],
        weights["expand"], weights["shrink"], s["dmix"], vg, tile,
    )
    step("mlp_back")
    turned = s["turned"]
    turn_stage(lambda a, b: dout_buf[a:b, :], turned)
    for half in range(2):
        weight_grad_stage(turned, s["act"], grads["shrink"], half, half * 1024, 1024, 512)
    step("dshrink")
    turn_stage(lambda a, b: s["nm"][a:b, :], turned)
    for half in range(2):
        weight_grad_stage(turned, s["slope"], grads["expand"], half, half * 1024, 1024, 512)
    step("dexpand")
    turn_stage(lambda a, b: s["h"][a:b, :], turned)
    for half in range(2):
        weight_grad_stage(turned, s["mix"], grads["merge"], half, half * 256, 256, 256)
    step("dmerge")
    turn_stage(lambda a, b: s["n"][a:b, :], turned)
    for odd, name in enumerate(("even", "odd")):
        attend_back_stage(
            s["p"], s["mix"], s["dmix"], s["lse"], s["dk"], s["dv"], tile, odd * 2, odd * 2 + 2,
            pair_plan(ENCODER_PLAN, flows, "back"),
        )
        for half in range(2):
            weight_grad_stage(turned, s["p"], grads[name], half, (half * 2 + odd) * 384, 384, 384)
        step("d" + name)

    def give_dx(rows, dx):
        if not tuned:
            dx_buf[rows, :] = dx
        elif rows.start == 0:
            dx_near[...] = dx
        else:
            give[...] = low(dx)

    for half, name in ((1, "far"), (0, "near")):
        project_back_tile(
            half, tile, x_rows, s["h"], s["p"], vec, base, first_w, vg, give_dx
        )
        step(name)
    if not tuned:
        return
    collect[...] = jnp.zeros_like(collect)
    collect[0:CODE, :] = dencode[...]
    collect[VEC_ROW : VEC_ROW + 16, :] = vg[...] + vg_other[...]
    collect[DECODE_ROW : DECODE_ROW + CODE, :] = ddecode[...]
    rows = collect[...].T
    for dp in range(16):
        for t in range(2):
            row = (dp * 2 + t) * 16
            grads["small"][t, dp // 4, (dp // 2) % 2, dp % 2] = rows[row : row + 16]
    step("vectors")
    square = jnp.zeros((8, 128), jnp.float32)
    for name in names:
        if name not in ("odd", "small"):
            square = square + square_sum(totals[name][...])
    step("last")
    for name in ("odd", "small"):
        square = square + square_sum(totals[name][...])
    norm[...] = jnp.sqrt(sum_over_devices(square, squares, (sum_send, sum_recv)))[0:1, 0:1]
    step("end")


def adam_parts(master, gradient, first_state, second_state, step_rate, decay_rate):
    mean_new = MEAN_DECAY * first_state + (1.0 - MEAN_DECAY) * gradient
    square_new = SQUARE_DECAY * second_state + (1.0 - SQUARE_DECAY) * gradient * gradient
    normal_step = (
        mean_new
        / (1.0 - MEAN_DECAY**STEP)
        / (jnp.sqrt(square_new / (1.0 - SQUARE_DECAY**STEP)) + ADAM_EPS)
    )
    updated = master - step_rate * (normal_step + decay_rate * master)
    return (mean_new, square_new, updated, updated.astype(jnp.bfloat16))


def update_kernel(*refs):
    y = lax.axis_index("tensor")
    for n in range(2):
        refs[n - 2][y] = refs[2 * n][...]
        refs[n - 2][1 - y] = wide(refs[2 * n + 1][...])
    norm = refs[4]
    totals, at = name_refs(PARTS + ("book", "small") + D_PARTS, refs, 5)
    masters, firsts, seconds = refs[at : at + 8], refs[at + 8 : at + 16], refs[at + 16 : at + 24]
    outs = refs[at + 24 :]
    factor = MAX_NORM / jnp.maximum(norm[...], MAX_NORM)

    def apply(member, index, gradient):
        results = adam_parts(
            masters[member][index],
            gradient * factor,
            firsts[member][index],
            seconds[member][index],
            RATES[member],
            DECAYS[member],
        )
        for k, result in enumerate(results):
            outs[member * 4 + k][index] = result

    for b, prefix in ((0, ""), (1, "d_")):
        for m in range(3):
            span = slice(m * PAIR, m * PAIR + PAIR)
            for odd, name in enumerate(("even", "odd")):
                columns = slice(odd * PAIR, odd * PAIR + PAIR)
                apply(0, (b, m, slice(None), columns), totals[prefix + name][:, span])
        apply(1, (b,), totals[prefix + "merge"][...])
        apply(2, (b,), totals[prefix + "expand"][...])
        apply(3, (b,), totals[prefix + "shrink"][...])
    small = totals["small"][...]
    turned = jnp.concatenate([small, jnp.zeros((112, PAIR), jnp.float32)], axis=0).T
    everything = (slice(None), slice(None))
    apply(4, everything, turned[VEC_ROW : VEC_ROW + 15, 0:16])
    apply(5, everything, small[:, 0:CODE])
    book = totals["book"][...].T
    book = jnp.concatenate([book[j * CODE : j * CODE + CODE] for j in range(4)], axis=1)
    apply(6, everything, book)
    apply(7, everything, small[:, DECODE_ROW : DECODE_ROW + CODE])


VMEM_LIMIT = 62 * 1024 * 1024


def run_decoder(tuned, inputs, raw=()):
    f32, bf16, i32 = jnp.float32, jnp.bfloat16, jnp.int32
    any_spec = pl.BlockSpec(memory_space=pl.ANY)
    vmem = pl.BlockSpec(memory_space=pltpu.VMEM)
    half = inputs[0].shape[-1]
    length = 2 * half
    outs = [((length, PAIR), bf16), ((length, PAIR), f32), ((16, WIDTH), f32), ((CODE, WIDTH), f32)]
    outs += [((2, WIDTH, n), bf16) for n in COLUMNS]
    out_specs = [vmem] * 9
    scratch = block_scratch(length)
    scratch += [pltpu.VMEM((length, WIDTH), f32), pltpu.VMEM((16, WIDTH), f32)]
    extra = {}
    if tuned:
        in_specs = [vmem] + [any_spec] * 2 + [vmem] * 8
        outs += [((half, WIDTH), f32), ((half, WIDTH), bf16), ((2, half, WIDTH), bf16)]
        outs += [((2, 1, half), i32), ((WIDTH, PAIR), bf16)]
        out_specs += [vmem] * 5
        outs += [(SPLIT + (32, n), bf16) for n in COLUMNS]
        out_specs += [any_spec] * 5
        scratch += [
            pltpu.VMEM((2, half, WIDTH), bf16),
            pltpu.VMEM((2, 1, half), i32),
            pltpu.VMEM((1, half), i32),
            pltpu.VMEM((PAIR, PAIR), f32),
        ]
        scratch += [pltpu.VMEM((32, n), bf16) for n in COLUMNS + COLUMNS]
        scratch += [pltpu.VMEM((80, PAIR), bf16)]
        scratch += [pltpu.VMEM(SPLIT + (32, n), bf16) for n in COLUMNS]
        scratch += [pltpu.VMEM(SPLIT + (80, PAIR), bf16)]
        scratch += [dma(11), dma(11, 12), dma(11, 12), dma(3), dma(3), dma(3)]
        extra = dict(collective_id=0, has_side_effects=True)
    else:
        in_specs = [vmem] * 9
        outs += [((length, WIDTH), f32)]
        out_specs += [vmem]
    return pl.pallas_call(
        functools.partial(decoder_kernel, tuned),
        out_shape=[jax.ShapeDtypeStruct(shape, dtype) for shape, dtype in outs],
        in_specs=in_specs,
        out_specs=out_specs,
        scratch_shapes=scratch,
        compiler_params=pltpu.CompilerParams(vmem_limit_bytes=VMEM_LIMIT, **extra),
        name="decoder",
    )(*inputs, *raw)


def run_encoder(tuned, inputs, late=(), partials=()):
    f32, bf16 = jnp.float32, jnp.bfloat16
    any_spec = pl.BlockSpec(memory_space=pl.ANY)
    vmem = pl.BlockSpec(memory_space=pltpu.VMEM)
    half = inputs[1].shape[2]
    length = 2 * half
    in_specs = [pl.BlockSpec(memory_space=pltpu.SMEM)] + [vmem] * 10
    scratch = block_scratch(length)
    scratch += [
        pltpu.VMEM((16, WIDTH), f32),
        pltpu.VMEM((length, WIDTH), f32),
        pltpu.VMEM((length, PAIR), f32),
    ]
    extra = {}
    if tuned:
        in_specs += [vmem] * 3 + [any_spec] * 5
        sizes = [(32, n) for n in COLUMNS]
        own_sizes = sizes + [(64, PAIR), (16, PAIR)]
        outs = [((half, WIDTH), bf16), ((half, WIDTH), f32), ((half, WIDTH), bf16), ((1, 1), f32)]
        outs += [(size, f32) for size in own_sizes + sizes]
        out_specs = [vmem] * 16
        scratch += [
            pltpu.VMEM((16, WIDTH), f32),
            pltpu.VMEM((CODE, WIDTH), f32),
            pltpu.VMEM((half, WIDTH), bf16),
            pltpu.VMEM((PAIR, WIDTH), f32),
            pltpu.VMEM((12, 8, 128), f32),
        ]
        dtypes = [bf16] * 6 + [f32]
        scratch += [pltpu.VMEM(SPLIT + s, d) for s, d in zip(own_sizes, dtypes)]
        scratch += [pltpu.VMEM((2, 4, 2) + size, bf16) for size in sizes]
        for size, dtype in zip(own_sizes, dtypes):
            scratch += reduce_scratch(size, dtype)
        scratch += [dma(12), dma(12, 8), dma(12, 8), dma(2), dma(2), dma(10), dma(10)]
        extra = dict(collective_id=1, has_side_effects=True)
    else:
        outs = [((length, WIDTH), f32), ((16, WIDTH), f32), ((CODE, WIDTH), f32)]
        outs += [((2048, PAIR), bf16)]
        outs += [((2, WIDTH, n), bf16) for n in COLUMNS]
        out_specs = [vmem] * 9
    return pl.pallas_call(
        functools.partial(encoder_kernel, tuned),
        out_shape=[jax.ShapeDtypeStruct(shape, dtype) for shape, dtype in outs],
        in_specs=in_specs,
        out_specs=out_specs,
        scratch_shapes=scratch,
        compiler_params=pltpu.CompilerParams(vmem_limit_bytes=VMEM_LIMIT, **extra),
        name="encoder",
    )(*inputs, *late, *partials)


def run_update(frames_out, norm, totals, masters, firsts, seconds):
    vmem = pl.BlockSpec(memory_space=pltpu.VMEM)
    outs = []
    for master in masters:
        outs += [jax.ShapeDtypeStruct(master.shape, jnp.float32)] * 3
        outs += [jax.ShapeDtypeStruct(master.shape, jnp.bfloat16)]
    args = [*frames_out, norm, *totals, *masters, *firsts, *seconds]
    outs += [jax.ShapeDtypeStruct((2,) + frames_out[0].shape, jnp.float32)] * 2
    return pl.pallas_call(
        update_kernel,
        out_shape=outs,
        in_specs=[vmem] * len(args),
        out_specs=[vmem] * len(outs),
        compiler_params=pltpu.CompilerParams(vmem_limit_bytes=VMEM_LIMIT),
        name="update",
    )(*args)


def turned_states(states):
    heads, merge, expand, shrink, vectors, encode, codebook, decode = states
    merge, shrink = merge.transpose(0, 2, 1), shrink.transpose(0, 2, 1)
    return (heads, merge, expand, shrink, vectors, encode, codebook.T, decode.T)


def local_tuned(frames, codes, clip_frames, out_cotangent, masters, firsts, seconds):
    masters, firsts, seconds = [turned_states(s) for s in (masters, firsts, seconds)]
    results = run_decoder(True, (codes, frames, out_cotangent), masters)
    entries, dchosen, vector_grads, ddecode = results[0:4]
    partials = [g.reshape(SPLIT + (32, g.shape[2])) for g in results[4:9]]
    decoded_near, decoded_far, frame, codes_here, ved = results[9:14]
    weights = [w.reshape(2, WIDTH, w.shape[5]) for w in results[14:19]]
    inputs = (clip_frames, codes_here, frame, entries, dchosen, ved, *weights)
    results = run_encoder(True, inputs, (vector_grads, ddecode, decoded_far), partials)
    decoded_got, dx_near, dx_got, norm = results[0:4]
    frames_out = (decoded_near, decoded_got, dx_near, dx_got)
    *updates, decoded, dframe = run_update(
        frames_out, norm, results[4:], masters, firsts, seconds
    )
    kinds = [turned_states(updates[k::4]) for k in range(4)]
    updates = [kinds[k][member] for member in range(8) for k in range(4)]
    return (decoded, dframe, norm.reshape(()), *updates)


def swap_half(rows):
    return lax.ppermute(rows, "tensor", [(0, 1), (1, 0)])


def join_frame(pair):
    mine = lax.axis_index("tensor")
    own = lax.dynamic_index_in_dim(pair, mine, axis=0, keepdims=False)
    other = lax.dynamic_index_in_dim(pair, 1 - mine, axis=0, keepdims=False)
    return jnp.stack([own, swap_half(other)])


def split_frame(rows):
    mine = lax.axis_index("tensor")
    half = rows.shape[0] // 2
    other = swap_half(rows[half:].astype(jnp.bfloat16)).astype(jnp.float32)
    own = rows[:half]
    return jnp.where(mine == 0, jnp.stack([own, other]), jnp.stack([other, own]))


def gather_plain(shard):
    gathered = lax.all_gather(shard, ("dp", "tensor"), axis=0, tiled=False)
    split = gathered.reshape((lax.axis_size("dp"), 2) + shard.shape)
    return split.transpose(1, 0, 2, 3).reshape(2, -1, shard.shape[1])


def scatter_plain(partial):
    return lax.psum_scatter(
        partial.astype(jnp.float32), ("dp", "tensor"), scatter_dimension=0, tiled=True
    )


def reduce_plain(partial):
    split = partial.reshape(2, lax.axis_size("dp"), -1, partial.shape[2]).transpose(1, 0, 2, 3)
    return scatter_plain(split.reshape(-1, partial.shape[2]))


def local_plain(frames, codes, clip_frames, out_cotangent, masters, firsts, seconds):
    heads, merge, expand, shrink, vectors, encode, codebook, decode = masters
    weights = []
    for b in range(2):
        even = jnp.concatenate([heads[b, m, :, :PAIR] for m in range(3)], axis=1)
        odd = jnp.concatenate([heads[b, m, :, PAIR:] for m in range(3)], axis=1)
        shards = (even, odd, merge[b].T, expand[b], shrink[b].T)
        weights.append([gather_plain(low(shard)) for shard in shards])
    both = ("dp", "tensor")
    columns = vectors.shape[1]
    blank = jnp.zeros((columns, CODE), jnp.float32)
    tall = jnp.pad(vectors.T, ((0, 0), (0, CODE - vectors.shape[0])))
    ved = low(jnp.concatenate([encode, tall, decode.T, blank], axis=1))
    ved = lax.all_gather(ved, both, axis=0, tiled=True)
    book = lax.all_gather(low(codebook), both, axis=0, tiled=True)
    book = book.reshape(4, 2048, CODE).transpose(1, 0, 2).reshape(2048, PAIR)
    code_rows = join_frame(codes).reshape(codes.shape[0], 1, codes.shape[1])
    results = run_decoder(False, (code_rows, join_frame(out_cotangent), ved, book, *weights[1]))
    entries, dchosen, vg_other, ddecode = results[0:4]
    decoder_grads, decoded = results[4:9], results[9]
    inputs = (clip_frames, code_rows, join_frame(frames), entries, dchosen, ved, *weights[0])
    results = run_encoder(False, inputs)
    dframe, vg, dencode, dbook = results[0:4]
    encoder_grads = results[4:9]
    sums = [[reduce_plain(g) for g in grads] for grads in (encoder_grads, decoder_grads)]
    dheads, dmerge, dexpand, dshrink = [], [], [], []
    for even, odd, merge_sum, expand_sum, shrink_sum in sums:
        parts = [
            jnp.concatenate([part[:, m * PAIR : (m + 1) * PAIR] for part in (even, odd)], axis=1)
            for m in range(3)
        ]
        dheads.append(jnp.stack(parts))
        dmerge.append(merge_sum.T)
        dexpand.append(expand_sum)
        dshrink.append(shrink_sum.T)
    small = jnp.concatenate([dencode, vg + vg_other, ddecode], axis=0).T
    small = scatter_plain(small)
    dbook = dbook.reshape(2048, 4, CODE).transpose(1, 0, 2).reshape(-1, CODE)
    gradients = (
        jnp.stack(dheads),
        jnp.stack(dmerge),
        jnp.stack(dexpand),
        jnp.stack(dshrink),
        small[:, CODE : CODE + vectors.shape[0]].T,
        small[:, :CODE],
        scatter_plain(dbook),
        small[:, CODE + 16 :].T,
    )
    squares = sum(jnp.sum(gradient * gradient) for gradient in gradients)
    norm_before = jnp.sqrt(lax.psum(squares, both))
    factor = MAX_NORM / jnp.maximum(norm_before, MAX_NORM)
    updates = []
    for member in range(8):
        updates += adam_parts(
            masters[member],
            gradients[member] * factor,
            firsts[member],
            seconds[member],
            RATES[member],
            DECAYS[member],
        )
    return (split_frame(decoded), split_frame(dframe), norm_before, *updates)


def local(frames, codes, clip_frames, out_cotangent, *states):
    tuned = lax.axis_size("dp") == 16 and lax.axis_size("tensor") == 2
    run = local_tuned if tuned and not FORCE_PLAIN else local_plain
    return run(frames, codes, clip_frames, out_cotangent, states[0:8], states[8:16], states[16:24])


FORCE_PLAIN = False


def solution(mesh):
    return jax.shard_map(
        local,
        mesh=mesh,
        in_specs=(
            P("dp", "tensor", None),
            P("dp", "tensor"),
            P(),
            P("dp", "tensor", None),
            P(None, None, "dp", "tensor"),
            P(None, "tensor", "dp"),
            P(None, "dp", "tensor"),
            P(None, "tensor", "dp"),
            P(None, ("dp", "tensor")),
            P(("dp", "tensor"), None),
            P(("dp", "tensor"), None),
            P(None, ("dp", "tensor")),
            P(None, None, "dp", "tensor"),
            P(None, "tensor", "dp"),
            P(None, "dp", "tensor"),
            P(None, "tensor", "dp"),
            P(None, ("dp", "tensor")),
            P(("dp", "tensor"), None),
            P(("dp", "tensor"), None),
            P(None, ("dp", "tensor")),
            P(None, None, "dp", "tensor"),
            P(None, "tensor", "dp"),
            P(None, "dp", "tensor"),
            P(None, "tensor", "dp"),
            P(None, ("dp", "tensor")),
            P(("dp", "tensor"), None),
            P(("dp", "tensor"), None),
            P(None, ("dp", "tensor")),
        ),
        out_specs=(
            P("dp", "tensor", None),
            P("dp", "tensor", None),
            P(),
            P(None, None, "dp", "tensor"),
            P(None, None, "dp", "tensor"),
            P(None, None, "dp", "tensor"),
            P(None, None, "dp", "tensor"),
            P(None, "tensor", "dp"),
            P(None, "tensor", "dp"),
            P(None, "tensor", "dp"),
            P(None, "tensor", "dp"),
            P(None, "dp", "tensor"),
            P(None, "dp", "tensor"),
            P(None, "dp", "tensor"),
            P(None, "dp", "tensor"),
            P(None, "tensor", "dp"),
            P(None, "tensor", "dp"),
            P(None, "tensor", "dp"),
            P(None, "tensor", "dp"),
            P(None, ("dp", "tensor")),
            P(None, ("dp", "tensor")),
            P(None, ("dp", "tensor")),
            P(None, ("dp", "tensor")),
            P(("dp", "tensor"), None),
            P(("dp", "tensor"), None),
            P(("dp", "tensor"), None),
            P(("dp", "tensor"), None),
            P(("dp", "tensor"), None),
            P(("dp", "tensor"), None),
            P(("dp", "tensor"), None),
            P(("dp", "tensor"), None),
            P(None, ("dp", "tensor")),
            P(None, ("dp", "tensor")),
            P(None, ("dp", "tensor")),
            P(None, ("dp", "tensor")),
        ),
        check_vma=False,
    )
```

```python
import functools
from types import SimpleNamespace

import jax
import jax.numpy as jnp
from jax import lax
from jax.experimental import pallas as pl
from jax.experimental.pallas import tpu as pltpu
from jax.sharding import PartitionSpec as P

HEAD_DIM = 64
STEP = 10


EPS_NORM = 1e-05
EPS_UNIT = 1e-06
COMMIT_WEIGHT = 100.0
MAX_NORM = 1.0
MEAN_DECAY = 0.9
SQUARE_DECAY = 0.95
ADAM_EPS = 1e-08
RATES = (0.1, 0.5, 0.1, 0.05, 1.0, 0.1, 1.0, 0.3)
DECAYS = (0.1, 0.1, 0.1, 0.1, 0.0, 0.1, 0.1, 0.1)

NT = (((1,), (1,)), ((), ()))
NN = (((1,), (0,)), ((), ()))
MESH = pl.DeviceIdType.MESH
PAIR = 128
WIDTH = 512
HIDDEN = 2048
CODE = 32
VEC_ROW = 32
DECODE_ROW = 64
SPLIT = (2, 4, 2, 2)
GELU_SCALE = (2.0 / 3.141592653589793) ** 0.5
GELU_CUBE = 0.044715
GROUPS = ("heads", "mlp", "shrink")
COLUMNS = (768, 1280, 1024)
OWN = ("even", "odd", "mlp", "shrink")
OWN_COLUMNS = (384, 384, 1280, 1024)


def mxu(first, second, dims=NN):
    return lax.dot_general(first, second, dims, preferred_element_type=jnp.float32)


def low(values):
    return values.astype(jnp.bfloat16)


def wide(values):
    return values.astype(jnp.float32)


def two_low(values):
    top = low(values)
    return top, low(values - wide(top))


def head_mask(shape, head):
    return (lax.broadcasted_iota(jnp.int32, shape, 1) // HEAD_DIM) == head


def keep_head(values, head):
    return jnp.where(head_mask(values.shape, head), values, jnp.zeros_like(values))


def norm_parts(rows):
    center = rows - jnp.mean(rows, axis=-1, keepdims=True)
    spread = jnp.mean(center * center, axis=-1, keepdims=True)
    scale = lax.rsqrt(spread + EPS_NORM)
    return center * scale, scale


def norm_back(xhat, scale, gain, grad):
    dxhat = grad * gain
    mean_grad = jnp.mean(dxhat, axis=-1, keepdims=True)
    mean_cross = jnp.mean(dxhat * xhat, axis=-1, keepdims=True)
    return scale * (dxhat - mean_grad - xhat * mean_cross)


def unit_scale(values):
    return lax.rsqrt(jnp.sum(values * values, axis=-1, keepdims=True) + EPS_UNIT)


def unit_back(values, grad):
    inverse = unit_scale(values)
    cross = jnp.sum(values * grad, axis=-1, keepdims=True)
    return inverse * grad - values * (inverse * inverse * inverse * cross)


def add_row(ref, row, values):
    ref[row : row + 1, :] += jnp.sum(values, axis=0, keepdims=True)


def tile_rows(step, tile):
    return pl.ds(pl.multiple_of(step * tile, tile), tile)


def views_of(refs):
    if len(refs) == 3:
        heads, mlp, shrink = refs
        even, odd = (heads, 0, 384), (heads, 384, 384)
    else:
        even, odd, mlp, shrink = refs
        even, odd = (even, 0, 384), (odd, 0, 384)
    merge, expand, shrink = (mlp, 0, 256), (mlp, 256, 1024), (shrink, 0, 1024)
    return SimpleNamespace(even=even, odd=odd, merge=merge, expand=expand, shrink=shrink)


def half_of(view, half, start=0, width=None):
    ref, first, full = view
    columns = slice(first + start, first + start + (width or full))
    if len(ref.shape) == 3:
        return ref[half, :, columns]
    values = ref[half, :, :, :, :, columns]
    return values.reshape(WIDTH, values.shape[-1])


def put_half(view, half, start, values):
    ref, first, _ = view
    columns = slice(first + start, first + start + values.shape[1])
    if len(ref.shape) == 3:
        ref[half, :, columns] = values
    else:
        ref[half, :, :, :, :, columns] = values.reshape(ref.shape[1:5] + (values.shape[-1],))


def remote(src, dst, sems, slot, target):
    send, recv = sems
    return pltpu.make_async_remote_copy(
        src_ref=src,
        dst_ref=dst,
        send_sem=send.at[slot],
        recv_sem=recv.at[slot],
        device_id=target,
        device_id_type=MESH,
    )


def coordinates():
    dp_index = lax.axis_index("dp")
    y = lax.axis_index("tensor")
    return dp_index // 4, (dp_index // 2) % 2, dp_index % 2, y


def partners(z, x, c, y):
    along_z = [(((z + step) % 4) * 4 + x * 2 + c, y) for step in (1, 2, 3)]
    along_x = (z * 4 + (1 - x) * 2 + c, y)
    along_y = (z * 4 + x * 2 + c, 1 - y)
    along_core = (z * 4 + x * 2 + (1 - c), y)
    return along_z, along_x, along_y, along_core


def octet(z, x, c, y):
    places = [(dx, dy, dc) for dx in (0, 1) for dy in (0, 1) for dc in (0, 1)][1:]
    return [
        (z * 4 + ((x + dx) % 2) * 2 + (c + dc) % 2, (y + dy) % 2) for dx, dy, dc in places
    ]


def greet(targets):
    barrier = pltpu.get_barrier_semaphore()
    for target in targets:
        pl.semaphore_signal(barrier, inc=1, device_id=target, device_id_type=MESH)
    return functools.partial(pl.semaphore_wait, barrier, len(targets))


def cuts_of(rows):
    if rows < 32:
        return ((0, rows, True),)
    middle = rows // 32 * 16
    return ((0, middle, True), (middle, rows, False))


class GatherFlow:
    def __init__(self, shard, out, local_sem, sems, slot):
        z, x, c, y = coordinates()
        along_z, along_x, along_y, along_core = partners(z, x, c, y)
        mine = out.at[y, z, x, c]
        column = out.at[y, :, x, c]
        self.own = pltpu.make_async_copy(shard, mine, local_sem.at[slot])
        self.first = [remote(shard, mine, sems, (slot, k), along_z[k]) for k in range(3)]
        self.core_first = [remote(column, column, sems, (slot, 3), along_core)]
        self.second, self.third, self.core_second, self.core_third = [], [], [], []
        for n, (start, stop, by_x) in enumerate(cuts_of(shard.shape[0])):
            rows = slice(start, stop)
            part = out.at[y, :, x, c, rows]
            plane = out.at[y, :, :, c, rows] if by_x else out.at[:, :, x, c, rows]
            got_second = out.at[y, :, 1 - x, c, rows] if by_x else out.at[1 - y, :, x, c, rows]
            got_third = out.at[1 - y, :, :, c, rows] if by_x else out.at[:, :, 1 - x, c, rows]
            near, far = (along_x, along_y) if by_x else (along_y, along_x)
            base = 4 + 4 * n
            self.second.append(remote(part, part, sems, (slot, base), near))
            self.third.append(remote(plane, plane, sems, (slot, base + 1), far))
            self.core_second.append(remote(got_second, got_second, sems, (slot, base + 2), along_core))
            self.core_third.append(remote(got_third, got_third, sems, (slot, base + 3), along_core))

    def begin(self):
        self.own.start()
        for copy in self.first:
            copy.start()

    def after_first(self):
        self.own.wait()
        for copy in self.first:
            copy.wait_recv()
        for copy in self.second + self.core_first:
            copy.start()

    def after_second(self):
        for copy in self.second:
            copy.wait_recv()
        for copy in self.third + self.core_second:
            copy.start()

    def after_third(self):
        for copy in self.third:
            copy.wait_recv()
        for copy in self.core_third:
            copy.start()

    def arrived(self):
        for copy in self.core_first + self.core_second + self.core_third:
            copy.wait_recv()

    def sent(self):
        for copy in self.first + self.second + self.third:
            copy.wait_send()
        for copy in self.core_first + self.core_second + self.core_third:
            copy.wait_send()


class ReduceFlow:
    def __init__(self, partial, held, scratch, local_sem, sems, slot, out):
        z, x, c, y = coordinates()
        along_z, along_x, along_y, along_core = partners(z, x, c, y)
        from_core, from_second, from_first, *from_third = scratch
        self.scratch, self.place, self.out = scratch, (z, x, y), out
        self.own = None
        if held is None:
            self.held, self.tail = partial, (c,)
        else:
            self.held, self.tail = held, ()
            self.own = pltpu.make_async_copy(partial.at[:, :, :, c], held, local_sem.at[slot])
        every = slice(None)
        self.cuts = cuts_of(partial.shape[4])

        def part(*index):
            return self.held.at[index[:3] + self.tail + index[3:]]

        self.core = remote(partial.at[:, :, :, 1 - c], from_core, sems, (slot, 0), along_core)
        self.third, self.second = [], []
        for n, (start, stop, by_x) in enumerate(self.cuts):
            rows = slice(start, stop)
            if by_x:
                leaving, target = part(1 - y, every, every, rows), along_y
                going, near = part(y, every, 1 - x, rows), along_x
            else:
                leaving, target = part(every, every, 1 - x, rows), along_x
                going, near = part(1 - y, every, x, rows), along_y
            self.third.append(remote(leaving, from_third[n], sems, (slot, 1 + n), target))
            landing = from_second.at[:, rows]
            self.second.append(remote(going, landing, sems, (slot, 3 + n), near))
        self.first = [
            remote(
                part(y, (z + k + 1) % 4, x), from_first.at[k], sems, (slot, 5 + k), along_z[k]
            )
            for k in range(3)
        ]

    def begin(self):
        self.core.start()
        if self.own is not None:
            self.own.start()

    def add(self, index, rows, values):
        place = index + self.tail + (rows,)
        self.held[place] = self.held[place] + values

    def after_core(self):
        self.core.wait_recv()
        if self.own is not None:
            self.own.wait()

        @pl.loop(0, 16)
        def _(n):
            index = (n // 8, (n // 2) % 4, n % 2)
            self.add(index, slice(None), self.scratch[0][index])

        for copy in self.third:
            copy.start()

    def after_third(self):
        z, x, y = self.place
        for cut, (start, stop, by_x) in enumerate(self.cuts):
            self.third[cut].wait_recv()

            @pl.loop(0, 8)
            def _(n):
                index = (n // 2, n % 2) if by_x else (n // 4, n % 4)
                place = (y,) + index if by_x else index + (x,)
                self.add(place, slice(start, stop), self.scratch[3 + cut][index])

            self.second[cut].start()

    def after_second(self):
        for copy in self.second:
            copy.wait_recv()
        z, x, y = self.place
        for k in range(4):
            self.add((y, k, x), slice(None), self.scratch[1][k])
        for copy in self.first:
            copy.start()

    def finish(self):
        z, x, y = self.place
        result = wide(self.held[(y, z, x) + self.tail])
        for k in range(3):
            self.first[k].wait_recv()
            result = result + wide(self.scratch[2][k])
        self.out[...] = result

    def sent(self):
        for copy in [self.core] + self.third + self.second + self.first:
            copy.wait_send()


def dma(*shape):
    return pltpu.SemaphoreType.DMA(shape)


def reduce_scratch(size, dtype):
    shapes = [(2, 4, 2) + size, (4,) + size, (3,) + size]
    for start, stop, by_x in cuts_of(size[0]):
        shapes.append(((4, 2) if by_x else (2, 4)) + (stop - start, size[1]))
    return [pltpu.VMEM(shape, dtype) for shape in shapes]


def begin(*flows):
    for flow in flows:
        flow.begin()


def after_first(*flows):
    for flow in flows:
        flow.after_first()


def after_second(*flows):
    for flow in flows:
        flow.after_second()


def after_third(*flows):
    for flow in flows:
        flow.after_third()


def after_core(*flows):
    for flow in flows:
        flow.after_core()


def finish(*flows):
    for flow in flows:
        flow.finish()


def arrived(*flows):
    for flow in flows:
        flow.arrived()


def sent(*flows):
    for flow in flows:
        flow.sent()


def at_pairs(actions):
    def run(count):
        for n, action in enumerate(actions):
            if action is not None:
                pl.when(count == n)(action)

    return run


def nothing():
    pass


class NoPlan:
    attend = back = ()

    def __getattr__(self, name):
        return nothing


def pair_place(count):
    pair = (count % 2) * 2 + count // 2
    wide_start = pl.multiple_of(pair * 384, 384)
    return pair, wide_start, pl.ds(pl.multiple_of(pair * PAIR, PAIR), PAIR)


def pair_columns(wide_start):
    return [pl.ds(pl.multiple_of(wide_start + member * PAIR, PAIR), PAIR) for member in range(3)]


def norm_stage(x_rows, vec, base, n_ref, tile):
    @pl.loop(0, n_ref.shape[0] // tile)
    def _(step):
        rows = tile_rows(step, tile)
        xhat, _ = norm_parts(x_rows(rows, step))
        n_ref[rows, :] = low(xhat * vec[base : base + 1, :] + vec[base + 1 : base + 2, :])


def project_stage(n_ref, weights, p_ref, tile, odd):
    @pl.loop(0, n_ref.shape[0] // tile)
    def _(step):
        rows = tile_rows(step, tile)
        normed = n_ref[rows, :]
        for half in range(2):
            start = (half * 2 + odd) * 384
            p_ref[rows, start : start + 384] = low(mxu(normed, half_of(weights[odd], half)))


def attend_stage(p_ref, mix_ref, lse_ref, tile, first, last, after_pair):
    length = p_ref.shape[0]

    @pl.loop(first, last)
    def _(count):
        pair, wide_start, columns = pair_place(count)
        query_at, key_at, value_at = pair_columns(wide_start)
        keys = p_ref[:, key_at] * (HEAD_DIM**-0.5)
        values = p_ref[:, value_at]
        for start in range(0, length, tile):
            query = p_ref[start : start + tile, query_at]
            out = None
            for head in range(2):
                ones_beside = jnp.where(
                    head_mask(values.shape, head), values, jnp.ones_like(values)
                )
                scores = mxu(keep_head(query, head), keys, NT)
                top = jnp.max(scores, axis=1, keepdims=True)
                raised = low(jnp.exp(scores - top))
                mixed = mxu(raised, ones_beside)
                total = pltpu.roll(mixed, HEAD_DIM, 1)
                mixed = mixed / total
                log_sum = top + jnp.log(total)
                if out is None:
                    out, log_sums = mixed, log_sum
                else:
                    is_first = head_mask(mixed.shape, 0)
                    out = jnp.where(is_first, out, mixed)
                    log_sums = jnp.where(is_first, log_sums, log_sum)
            mix_ref[start : start + tile, columns] = low(out)
            turned = log_sums.T
            for head in range(2):
                lse_ref[pair * 2 + head, :, start : start + tile] = jnp.broadcast_to(
                    turned[head * HEAD_DIM : head * HEAD_DIM + 1], (8, tile)
                )
        after_pair(count)


def expand_stage(x_rows, mix_ref, vec, base, merge_w, expand_w, h_ref, nm_ref, slope_ref, act_ref, tile):
    @pl.loop(0, h_ref.shape[0] // tile)
    def _(step):
        rows = tile_rows(step, tile)
        hidden = x_rows(rows, step) + vec[base + 2 : base + 3, :]
        for half in range(2):
            hidden = hidden + mxu(
                mix_ref[rows, half * 256 : half * 256 + 256], half_of(merge_w, half), NT
            )
        h_ref[rows, :] = hidden
        xhat, _ = norm_parts(hidden)
        normed = low(xhat * vec[base + 3 : base + 4, :] + vec[base + 4 : base + 5, :])
        nm_ref[rows, :] = normed
        for half in range(2):
            for start in range(0, 1024, 512):
                values = mxu(normed, half_of(expand_w, half, start, 512))
                place = slice(half * 1024 + start, half * 1024 + start + 512)
                square = values * values
                bend = jnp.tanh(values * (GELU_SCALE + (GELU_SCALE * GELU_CUBE) * square))
                share = 0.5 + 0.5 * bend
                active = values * share
                act_ref[rows, place] = low(active)
                slope_ref[rows, place] = low(
                    share
                    + (active - active * share)
                    * (2.0 * GELU_SCALE + (6.0 * GELU_SCALE * GELU_CUBE) * square)
                )


def shrink_stage(h_ref, act_ref, vec, base, shrink_w, tile, give):
    @pl.loop(0, h_ref.shape[0] // tile)
    def _(step):
        rows = tile_rows(step, tile)
        out = h_ref[rows, :] + vec[base + 5 : base + 6, :]
        for half in range(2):
            out = out + mxu(
                act_ref[rows, half * 1024 : half * 1024 + 1024], half_of(shrink_w, half), NT
            )
        give(rows, out, step)


def mlp_back_stage(
    dout_rows, h_ref, slope_ref, vec, base, merge_w, expand_w, shrink_w, dmix_ref, vg_ref, tile
):
    @pl.loop(0, h_ref.shape[0] // tile)
    def _(step):
        rows = tile_rows(step, tile)
        dout = wide(dout_rows(rows, step))
        dout_low = low(dout)
        dnormed = None
        for half in range(2):
            for start in range(0, 1024, 512):
                place = slice(half * 1024 + start, half * 1024 + start + 512)
                dactive = mxu(dout_low, half_of(shrink_w, half, start, 512))
                dexpanded = low(dactive * wide(slope_ref[rows, place]))
                slope_ref[rows, place] = dexpanded
                part = mxu(dexpanded, half_of(expand_w, half, start, 512), NT)
                dnormed = part if dnormed is None else dnormed + part
        xhat, scale = norm_parts(h_ref[rows, :])
        dhidden = dout + norm_back(xhat, scale, vec[base + 3 : base + 4, :], dnormed)
        h_ref[rows, :] = dhidden
        dhidden_low = low(dhidden)
        for half in range(2):
            dmix_ref[rows, half * 256 : half * 256 + 256] = low(
                mxu(dhidden_low, half_of(merge_w, half))
            )
        add_row(vg_ref, base + 2, dhidden)
        add_row(vg_ref, base + 3, dnormed * xhat)
        add_row(vg_ref, base + 4, dnormed)
        add_row(vg_ref, base + 5, dout)


def turn_stage(read, turned_ref):
    length = turned_ref.shape[1]
    for start in range(0, length, 256):
        turned_ref[:, start : start + 256] = low(read(start, start + 256)).T


def weight_grad_stage(turned_ref, right_ref, out_ref, half, first, width, chunk):
    for start in range(0, width, chunk):
        product = mxu(turned_ref[...], right_ref[:, first + start : first + start + chunk])
        put_half(out_ref, half, start, low(product))


def attend_back_stage(
    p_ref, mix_ref, dmix_ref, lse_ref, dk_acc, dv_acc, tile, first, last, after_pair
):
    length = p_ref.shape[0]

    @pl.loop(first, last)
    def _(count):
        pair, wide_start, columns = pair_place(count)
        query_at, key_at, value_at = pair_columns(wide_start)
        keys = p_ref[:, key_at] * (HEAD_DIM**-0.5)
        values = p_ref[:, value_at]
        keys_turned = keys.T
        for start in range(0, length, tile):
            rows = slice(start, start + tile)
            query = p_ref[rows, query_at]
            dmix = dmix_ref[rows, columns]
            inner = (wide(dmix) * wide(mix_ref[rows, columns])).T
            dquery, dkeys, dvalues = [], None, None
            for head in range(2):
                span = slice(head * HEAD_DIM, head * HEAD_DIM + HEAD_DIM)
                query_here = keep_head(query, head)
                dmix_here = keep_head(dmix, head)
                delta = jnp.sum(inner[span], axis=0, keepdims=True)
                log_sum = lse_ref[pair * 2 + head, 0:1, rows]
                attend = jnp.exp(mxu(keys, query_here, NT) - log_sum)
                dscores = low(attend * (mxu(values, dmix_here, NT) - delta))
                part = mxu(low(attend), dmix_here)
                dvalues = part if dvalues is None else dvalues + part
                part = mxu(dscores, query_here)
                dkeys = part if dkeys is None else dkeys + part
                dquery.append(mxu(keys_turned[span], dscores))
            p_ref[rows, query_at] = low(jnp.concatenate(dquery, axis=0).T)
            if start == 0:
                dk_acc[...] = dkeys
                dv_acc[...] = dvalues
            elif start + tile < length:
                dk_acc[...] += dkeys
                dv_acc[...] += dvalues
            else:
                p_ref[:, key_at] = low((dk_acc[...] + dkeys) * (HEAD_DIM**-0.5))
                p_ref[:, value_at] = low(dv_acc[...] + dvalues)
        after_pair(count)


def project_back_tile(step, tile, x_rows, h_ref, p_ref, vec, base, weights, vg_ref, give):
    rows = slice(step * tile, step * tile + tile)
    dnormed = None
    for odd in range(2):
        for half in range(2):
            start = (half * 2 + odd) * 384
            product = mxu(p_ref[rows, start : start + 384], half_of(weights[odd], half), NT)
            dnormed = product if dnormed is None else dnormed + product
    xhat, scale = norm_parts(x_rows(rows, step))
    dx = h_ref[rows, :] + norm_back(xhat, scale, vec[base : base + 1, :], dnormed)
    add_row(vg_ref, base, dnormed * xhat)
    add_row(vg_ref, base + 1, dnormed)
    give(rows, dx)


def code_place(codes, tuned):
    if tuned:
        owner = codes // 256
        return ((owner % 2) * 16 + owner // 2) * 64 + codes % 64, (codes // 64) % 4
    return codes % 2048, codes // 2048


def one_hot(place):
    shape = (2048, place.shape[1])
    return low(jnp.where(lax.broadcasted_iota(jnp.int32, shape, 0) == place, 1.0, 0.0))


def in_group(group, values):
    rows = lax.broadcasted_iota(jnp.int32, values.shape, 0) // CODE
    return jnp.where(rows == group, values, jnp.zeros_like(values))


def look_up_stage(codes, codebook, entries_ref, tuned):
    tile = 256
    book_turned = codebook.T
    for start in range(0, entries_ref.shape[0], tile):
        place, group = code_place(codes(start, tile), tuned)
        found = in_group(group, mxu(book_turned, one_hot(place)))
        found = found[0:32] + found[32:64] + found[64:96] + found[96:128]
        found = jnp.concatenate([found, jnp.zeros((96, tile), jnp.float32)], axis=0)
        entries_ref[start : start + tile, :] = low(found.T)


def scatter_stage(codes, dentries_ref, give, tuned):
    tile = 512
    total = None
    for start in range(0, dentries_ref.shape[0], tile):
        place, group = code_place(codes(start, tile), tuned)
        turned = low(dentries_ref[start : start + tile, :].T[0:CODE])
        placed = in_group(group, wide(jnp.concatenate([turned] * 4, axis=0)))
        part = mxu(one_hot(place), low(placed), NT)
        total = part if total is None else total + part
    give(low(total))


def square_sum(values):
    rows, width = values.shape
    values = values * values
    total = jnp.zeros((8, 128), jnp.float32)
    for r in range(0, rows, 8):
        for w in range(0, width, 128):
            total = total + values[r : r + 8, w : w + 128]
    return total


def sum_over_devices(square, squares, sums):
    z, x, c, y = coordinates()
    total = jnp.broadcast_to(jnp.sum(square, keepdims=True), (8, 128))
    stage = 0
    for n, targets in enumerate((octet(z, x, c, y), partners(z, x, c, y)[0])):
        squares[n] = total
        copies = []
        for target in targets:
            copy = remote(squares.at[n], squares.at[2 + stage], sums, stage, target)
            copy.start()
            copies.append((copy, 2 + stage))
            stage += 1
        for copy, place in copies:
            copy.wait()
            total = total + squares[place]
    return total


class Swap:
    def __init__(self, source, target, sems, local_sem, slot):
        z, x, c, y = coordinates()
        along_y = partners(z, x, c, y)[2]
        self.own = pltpu.make_async_copy(source.at[y], target.at[0], local_sem.at[slot])
        self.other = remote(source.at[1 - y], target.at[1], sems, slot, along_y)

    def begin(self):
        self.other.start()
        self.own.start()

    def arrived(self):
        self.own.wait()
        self.other.wait_recv()

    def sent(self):
        self.other.wait_send()


class Send:
    def __init__(self, give, got, sems, slot):
        z, x, c, y = coordinates()
        self.other = remote(give, got, sems, slot, partners(z, x, c, y)[2])

    def begin(self):
        self.other.start()

    def arrived(self):
        self.other.wait_recv()

    def sent(self):
        self.other.wait_send()


class DecoderPlan(NoPlan):
    def __init__(self, flows):
        self.f = flows
        self.attend = (self.attend0, self.attend1, self.attend2, self.attend3)
        self.back = (self.back0, None, self.back2, None)

    def start(self):
        f = self.f
        begin(f.codes, f.small, f.heads, f.cot)

    def packed(self):
        f = self.f
        after_first(f.small, f.heads)
        begin(f.mlp)
        after_second(f.small, f.heads)
        after_third(f.small)
        arrived(f.small, f.codes)

    def look(self):
        f = self.f
        after_third(f.heads)
        after_first(f.mlp)
        begin(f.shrink)
        arrived(f.heads)

    def attend0(self):
        after_second(self.f.mlp)

    def attend1(self):
        after_first(self.f.shrink)
        begin(self.f.e_heads)

    def attend2(self):
        after_third(self.f.mlp)
        after_second(self.f.shrink)
        begin(self.f.e_mlp)

    def attend3(self):
        arrived(self.f.mlp)

    def expand(self):
        f = self.f
        after_third(f.shrink)
        after_first(f.e_heads, f.e_mlp)
        arrived(f.shrink)

    def shrink(self):
        begin(self.f.e_shrink)
        arrived(self.f.cot)

    def mlp_back(self):
        after_second(self.f.e_heads, self.f.e_mlp)

    def dexpand(self):
        after_first(self.f.e_shrink)

    def back0(self):
        f = self.f
        after_third(f.e_heads, f.e_mlp)
        after_second(f.e_shrink)
        begin(f.frame)

    def back2(self):
        after_third(self.f.e_shrink)

    def end(self):
        f = self.f
        arrived(f.e_heads, f.e_mlp, f.e_shrink, f.frame)
        sent(f.codes, f.small, f.heads, f.mlp, f.shrink, f.cot, f.frame)
        sent(f.e_heads, f.e_mlp, f.e_shrink)


class EncoderPlan(NoPlan):
    def __init__(self, flows):
        self.f = flows
        self.attend = (self.attend0, self.attend1, self.attend2, self.attend3)
        self.back = (self.back0, self.back1, self.back2, self.back3)

    def start(self):
        f = self.f
        begin(f.d_shrink, f.d_mlp, f.d_heads)

    def project(self):
        after_core(self.f.d_shrink)

    def attend0(self):
        after_core(self.f.d_mlp)

    def attend1(self):
        after_core(self.f.d_heads)

    def attend2(self):
        after_third(self.f.d_shrink)

    def attend3(self):
        after_third(self.f.d_mlp)

    def expand(self):
        after_second(self.f.d_shrink)
        after_third(self.f.d_heads)

    def shrink(self):
        after_second(self.f.d_mlp)
        finish(self.f.d_shrink)
        begin(self.f.decoded)

    def mlp_back(self):
        after_second(self.f.d_heads)
        finish(self.f.d_mlp)
        begin(self.f.book)

    def dshrink(self):
        after_core(self.f.book)
        begin(self.f.shrink)
        finish(self.f.d_heads)

    def dmerge(self):
        begin(self.f.mlp)
        after_third(self.f.book)
        after_core(self.f.shrink)

    def back0(self):
        after_second(self.f.book)
        after_core(self.f.mlp)

    def back1(self):
        finish(self.f.book)
        after_third(self.f.shrink)

    def deven(self):
        begin(self.f.even)

    def back2(self):
        after_third(self.f.mlp)
        after_second(self.f.shrink)
        after_core(self.f.even)

    def back3(self):
        after_second(self.f.mlp)
        after_third(self.f.even)
        finish(self.f.shrink)

    def dodd(self):
        begin(self.f.odd)
        after_core(self.f.odd)

    def far(self):
        after_second(self.f.even)

    def near(self):
        finish(self.f.mlp)

    def vectors(self):
        f = self.f
        begin(f.small)
        after_third(f.odd)
        begin(f.dframe)
        after_core(f.small)
        finish(f.even)
        after_third(f.small)
        after_second(f.odd)
        after_second(f.small)

    def last(self):
        finish(self.f.odd, self.f.small)

    def end(self):
        f = self.f
        arrived(f.decoded, f.dframe)
        sent(f.d_shrink, f.d_mlp, f.d_heads, f.decoded, f.dframe)
        sent(f.even, f.odd, f.mlp, f.shrink, f.small, f.book)


def name_refs(names, refs, start):
    stop = start + len(names)
    return SimpleNamespace(**dict(zip(names, refs[start:stop]))), stop


BLOCK_SCRATCH = ("n", "p", "mix", "lse", "h", "nm", "slope", "act", "dmix", "dk", "dv", "turned")


def block_scratch(length):
    f32, bf16 = jnp.float32, jnp.bfloat16
    shapes = [
        ((length, WIDTH), bf16),
        ((length, 3 * WIDTH), bf16),
        ((length, WIDTH), bf16),
        ((8, 8, length), f32),
        ((length, WIDTH), f32),
        ((length, WIDTH), bf16),
        ((length, HIDDEN), bf16),
        ((length, HIDDEN), bf16),
        ((length, WIDTH), bf16),
        ((length, PAIR), f32),
        ((length, PAIR), f32),
        ((WIDTH, length), bf16),
    ]
    return [pltpu.VMEM(shape, dtype) for shape, dtype in shapes]


def pack_heads(raw, shard, b):
    for odd in range(2):
        for member in range(3):
            start = odd * 384 + member * PAIR
            shard[:, start : start + PAIR] = low(raw.heads[b, member, :, odd * PAIR : odd * PAIR + PAIR])


def pack_rest(raw, mlp, shrink, b):
    mlp[:, 0:256] = low(raw.merge[b])
    mlp[:, 256:1280] = low(raw.expand[b])
    shrink[...] = low(raw.shrink[b])


def pack_small(raw, small, turn):
    turn[...] = jnp.zeros_like(turn)
    turn[VEC_ROW : VEC_ROW + 15, 0:16] = raw.vectors[...]
    rows = turn[...].T[0:16]
    blank = jnp.zeros((16, CODE), jnp.float32)
    sides = jnp.concatenate([raw.encode[...], blank, raw.decode[...], blank], axis=1)
    small[0:16, :] = low(rows + sides)
    codebook = raw.codebook[...].T
    book = [codebook[j * 64 : j * 64 + 64, :] for j in range(4)]
    small[16:80, :] = low(jnp.concatenate(book, axis=1))


RAW = ("heads", "merge", "expand", "shrink", "vectors", "encode", "codebook", "decode")
E_GROUPS = ("e_heads", "e_mlp", "e_shrink")
D_GROUPS = ("d_heads", "d_mlp", "d_shrink")
TOTALS = OWN + ("book", "small") + D_GROUPS


def decoder_kernel(tuned, *refs):
    at = 0
    if tuned:
        (codes_in, frames_in, cot_in), at = refs[:3], 3
        raw, at = name_refs(RAW, refs, at)
    else:
        (codes, cot, ved, book), at = refs[:4], 4
        weights, at = views_of(refs[at : at + 3]), at + 3
    (entries, dchosen, vg, ddecode), at = refs[at : at + 4], at + 4
    grads, at = views_of(refs[at : at + 3]), at + 3
    if tuned:
        (near, far, frame, codes_out, ved), at = refs[at : at + 5], at + 5
        moved, at = refs[at : at + 3], at + 3
    else:
        (out_buf,), at = refs[at : at + 1], at + 1
    s, at = name_refs(BLOCK_SCRATCH, refs, at)
    (x_buf, vec), at = refs[at : at + 2], at + 2
    plan = NoPlan()
    tile = 512
    if tuned:
        (cot, codes, code_give, turn), at = refs[at : at + 4], at + 4
        shards, at = name_refs(GROUPS + E_GROUPS + ("small",), refs, at)
        gathered, at = refs[at : at + 3], at + 3
        (small, local_sem, send, recv, swap_local, swap_send, swap_recv) = refs[at:]
        weights = views_of(gathered)
        f = SimpleNamespace()
        targets = tuple(gathered) + tuple(moved) + (small,)
        for slot, (name, shard) in enumerate(vars(shards).items()):
            flow = GatherFlow(shard, targets[slot], local_sem, (send, recv), slot)
            setattr(f, name, flow)
        swaps = (swap_send, swap_recv)
        f.codes = Send(code_give, codes.at[1], swaps, 0)
        f.cot = Swap(cot_in, cot, swaps, swap_local, 1)
        f.frame = Swap(frames_in, frame, swaps, swap_local, 2)
        along_z, along_x, along_y, along_core = partners(*coordinates())
        greeted = greet(along_z + [along_x, along_y, along_core])
        pack_small(raw, shards.small, turn)
        pack_heads(raw, shards.heads, 1)
        y = lax.axis_index("tensor")
        codes[0] = jnp.where(y == 0, codes_in[0:1, :], codes_in[1:2, :])
        code_give[...] = jnp.where(y == 0, codes_in[1:2, :], codes_in[0:1, :])
        greeted()
        plan = DecoderPlan(f)
    plan.start()
    if tuned:
        pack_rest(raw, shards.mlp, shards.shrink, 1)
        pack_heads(raw, shards.e_heads, 0)
        pack_rest(raw, shards.e_mlp, shards.e_shrink, 0)
        plan.packed()
        for dp in range(16):
            for t in range(2):
                row = (dp * 2 + t) * 16
                ved[row : row + 16, :] = small[t, dp // 4, (dp // 2) % 2, dp % 2, 0:16, :]
        book_rows = small[:, :, :, :, 16:80, :].reshape(2048, PAIR)
        codes_out[...] = codes[...]
    else:
        book_rows = book[...]
    turned_small = wide(ved[...]).T
    vec[...] = turned_small[VEC_ROW : VEC_ROW + 16]
    decode = low(turned_small[DECODE_ROW : DECODE_ROW + CODE])
    decode = jnp.concatenate([decode, jnp.zeros((96, WIDTH), jnp.bfloat16)], axis=0)

    def read_codes(start, size):
        half, first = start // 512, start % 512
        return codes[half, :, first : first + size]

    vg[...] = jnp.zeros_like(vg)
    ddecode[...] = jnp.zeros_like(ddecode)
    look_up_stage(read_codes, book_rows, entries, tuned)
    values = wide(entries[...])
    x_buf[...] = mxu(low(values * unit_scale(values)), decode) + vec[14:15, :]
    base = 6
    x_rows = lambda rows, _: x_buf[rows, :]
    norm_stage(x_rows, vec, base, s.n, tile)
    plan.look()
    first_w = (weights.even, weights.odd)
    for odd in range(2):
        project_stage(s.n, first_w, s.p, tile, odd)
    plan.project()
    attend_stage(
        s.p, s.mix, s.lse, tile, 0, 4, at_pairs(plan.attend)
    )
    expand_stage(
        x_rows, s.mix, vec, base, weights.merge, weights.expand, s.h, s.nm,
        s.slope, s.act, tile,
    )
    plan.expand()

    def give_out(rows, out, part):
        if not tuned:
            out_buf[rows, :] = out
            return

        @pl.when(part == 0)
        def _():
            near[...] = out

        @pl.when(part == 1)
        def _():
            far[...] = low(out)

    shrink_stage(s.h, s.act, vec, base, weights.shrink, tile, give_out)
    plan.shrink()
    mlp_back_stage(
        lambda rows, half: cot[half], s.h, s.slope, vec, base, weights.merge,
        weights.expand, weights.shrink, s.dmix, vg, tile,
    )
    plan.mlp_back()
    turned = s.turned
    turn_stage(lambda a, b: cot[a // 512, a % 512 : a % 512 + 256, :], turned)
    for half in range(2):
        weight_grad_stage(turned, s.act, grads.shrink, half, half * 1024, 1024, 512)
    plan.dshrink()
    turn_stage(lambda a, b: s.nm[a:b, :], turned)
    for half in range(2):
        weight_grad_stage(turned, s.slope, grads.expand, half, half * 1024, 1024, 512)
    plan.dexpand()
    turn_stage(lambda a, b: s.h[a:b, :], turned)
    for half in range(2):
        weight_grad_stage(turned, s.mix, grads.merge, half, half * 256, 256, 256)
    attend_back_stage(
        s.p, s.mix, s.dmix, s.lse, s.dk, s.dv, tile, 0, 4,
        at_pairs(plan.back),
    )
    turn_stage(lambda a, b: s.n[a:b, :], turned)
    for odd, target in enumerate((grads.even, grads.odd)):
        for half in range(2):
            weight_grad_stage(turned, s.p, target, half, (half * 2 + odd) * 384, 384, 384)

    def give_dx(rows, dx):
        add_row(vg, 14, dx)
        picked = wide(entries[rows, :])
        chosen_turned = low(picked * unit_scale(picked)).T[0:CODE]
        total = None
        for part in two_low(dx):
            ddecode[...] += mxu(chosen_turned, part)
            product = mxu(part, decode, NT)
            total = product if total is None else total + product
        dchosen[rows, :] = total

    for half in (1, 0):
        project_back_tile(
            half, tile, x_rows, s.h, s.p, vec, base, first_w, vg, give_dx
        )
    plan.end()


def encoder_kernel(tuned, *refs):
    (clip_frames, codes, frame, entries, dchosen, ved), at = refs[:6], 6
    weights, at = views_of(refs[at : at + 3]), at + 3
    if tuned:
        (vg_other, ddecode, decoded_far), at = refs[at : at + 3], at + 3
        partials, at = refs[at : at + 3], at + 3
        (decoded_got, dx_near, dx_got, norm), at = refs[at : at + 4], at + 4
        totals, at = name_refs(TOTALS, refs, at)
    else:
        (dx_buf, vg, dencode, dbook), at = refs[at : at + 4], at + 4
        grads, at = views_of(refs[at : at + 3]), at + 3
    s, at = name_refs(BLOCK_SCRATCH, refs, at)
    (vec, dout_buf, dentries), at = refs[at : at + 3], at + 3
    plan = NoPlan()
    tile = 512
    if tuned:
        (vg, dencode, give, collect, squares), at = refs[at : at + 5], at + 5
        own, at = refs[at : at + 6], at + 6
        grads, (dbook, dsmall) = views_of(own[:4]), own[4:]
        held, at = refs[at : at + 3], at + 3
        receive = []
        for rows in (32, 32, 32, 64, 16):
            count = 3 + len(cuts_of(rows))
            receive.append(refs[at : at + count])
            at += count
        local_sem, send, recv, swap_send, swap_recv, sum_send, sum_recv = refs[at:]
        heads, mlp, shrink, book, small = receive
        even, odd = [
            [ref.at[(slice(None),) * (len(ref.shape) - 1) + (slice(c, c + 384),)] for ref in heads]
            for c in (0, 384)
        ]
        sources = list(zip(own, (even, odd, mlp, shrink, book, small), [None] * 6))
        sources += list(zip(partials, (heads, mlp, shrink), held))
        f = SimpleNamespace()
        for slot, (name, out) in enumerate(vars(totals).items()):
            source, scratch, kept = sources[slot]
            flow = ReduceFlow(source, kept, scratch, local_sem, (send, recv), slot, out)
            setattr(f, name, flow)
        swaps = (swap_send, swap_recv)
        f.decoded = Send(decoded_far, decoded_got, swaps, 0)
        f.dframe = Send(give, dx_got, swaps, 1)
        place = coordinates()
        greet(octet(*place) + partners(*place)[0])()
        plan = EncoderPlan(f)
    plan.start()
    turned_small = wide(ved[...]).T
    vec[...] = turned_small[VEC_ROW : VEC_ROW + 16]
    encode = jnp.where(
        lax.broadcasted_iota(jnp.int32, ved.shape, 1) < CODE, ved[...], jnp.zeros_like(ved)
    )
    frame_id = lax.axis_index("dp") * 2 + lax.axis_index("tensor")
    clip_end, clip_count = 0, 1
    for clip in range(clip_frames.shape[0]):
        size = clip_frames[clip]
        inside = (frame_id >= clip_end) & (frame_id < clip_end + size)
        clip_count = jnp.where(inside, size, clip_count)
        clip_end = clip_end + size
    clip_weight = (2.0 * COMMIT_WEIGHT) / jnp.full((1, 1), clip_count).astype(jnp.float32)
    vg[...] = jnp.zeros_like(vg)
    dencode[...] = jnp.zeros_like(dencode)
    base = 0
    x_rows = lambda rows, half: wide(frame[half])
    norm_stage(x_rows, vec, base, s.n, tile)
    first_w = (weights.even, weights.odd)
    for odd in range(2):
        project_stage(s.n, first_w, s.p, tile, odd)
    plan.project()
    attend_stage(
        s.p, s.mix, s.lse, tile, 0, 4, at_pairs(plan.attend)
    )
    expand_stage(
        x_rows, s.mix, vec, base, weights.merge, weights.expand, s.h, s.nm,
        s.slope, s.act, tile,
    )
    plan.expand()

    def give_out(rows, out, _):
        xhat, scale = norm_parts(out)
        normed = low(xhat * vec[12:13, :] + vec[13:14, :])
        raw = mxu(normed, encode)
        picked = wide(entries[rows, :])
        pull = clip_weight * (
            raw * unit_scale(raw) - picked * unit_scale(picked)
        )
        dentries[rows, :] = unit_back(picked, dchosen[rows, :] - pull)
        draw = unit_back(raw, pull)
        dnormed = None
        for part in two_low(draw):
            product = mxu(part, encode, NT)
            dnormed = product if dnormed is None else dnormed + product
            dencode[...] += mxu(part.T[0:CODE], normed)
        dout_buf[rows, :] = norm_back(xhat, scale, vec[12:13, :], dnormed)
        add_row(vg, 12, dnormed * xhat)
        add_row(vg, 13, dnormed)

    shrink_stage(s.h, s.act, vec, base, weights.shrink, tile, give_out)
    plan.shrink()

    def read_codes(start, size):
        half, first = start // 512, start % 512
        return codes[half, :, first : first + size]

    def give_book(total):
        if tuned:
            dbook[...] = total.reshape(SPLIT + (64, PAIR))
        else:
            dbook[...] = total

    scatter_stage(read_codes, dentries, give_book, tuned)
    mlp_back_stage(
        lambda rows, _: dout_buf[rows, :], s.h, s.slope, vec, base, weights.merge,
        weights.expand, weights.shrink, s.dmix, vg, tile,
    )
    plan.mlp_back()
    turned = s.turned
    turn_stage(lambda a, b: dout_buf[a:b, :], turned)
    for half in range(2):
        weight_grad_stage(turned, s.act, grads.shrink, half, half * 1024, 1024, 512)
    plan.dshrink()
    turn_stage(lambda a, b: s.nm[a:b, :], turned)
    for half in range(2):
        weight_grad_stage(turned, s.slope, grads.expand, half, half * 1024, 1024, 512)
    plan.dexpand()
    turn_stage(lambda a, b: s.h[a:b, :], turned)
    for half in range(2):
        weight_grad_stage(turned, s.mix, grads.merge, half, half * 256, 256, 256)
    plan.dmerge()
    turn_stage(lambda a, b: s.n[a:b, :], turned)
    after = (plan.deven, plan.dodd)
    for odd, target in enumerate((grads.even, grads.odd)):
        attend_back_stage(
            s.p, s.mix, s.dmix, s.lse, s.dk, s.dv, tile, odd * 2, odd * 2 + 2,
            at_pairs(plan.back),
        )
        for half in range(2):
            weight_grad_stage(turned, s.p, target, half, (half * 2 + odd) * 384, 384, 384)
        after[odd]()

    def give_dx(rows, dx):
        if not tuned:
            dx_buf[rows, :] = dx
        elif rows.start == 0:
            dx_near[...] = dx
        else:
            give[...] = low(dx)

    for half, done in ((1, plan.far), (0, plan.near)):
        project_back_tile(
            half, tile, x_rows, s.h, s.p, vec, base, first_w, vg, give_dx
        )
        done()
    if not tuned:
        return
    collect[...] = jnp.zeros_like(collect)
    collect[0:CODE, :] = dencode[...]
    collect[VEC_ROW : VEC_ROW + 16, :] = vg[...] + vg_other[...]
    collect[DECODE_ROW : DECODE_ROW + CODE, :] = ddecode[...]
    rows = collect[...].T
    for dp in range(16):
        for t in range(2):
            row = (dp * 2 + t) * 16
            dsmall[t, dp // 4, (dp // 2) % 2, dp % 2] = rows[row : row + 16]
    plan.vectors()
    square = jnp.zeros((8, 128), jnp.float32)
    late = (totals.odd, totals.small)
    for total in vars(totals).values():
        if not any(total is other for other in late):
            square = square + square_sum(total[...])
    plan.last()
    for total in late:
        square = square + square_sum(total[...])
    norm[...] = jnp.sqrt(sum_over_devices(square, squares, (sum_send, sum_recv)))[0:1, 0:1]
    plan.end()


def adam_parts(master, gradient, first_state, second_state, step_rate, decay_rate):
    mean_new = MEAN_DECAY * first_state + (1.0 - MEAN_DECAY) * gradient
    square_new = SQUARE_DECAY * second_state + (1.0 - SQUARE_DECAY) * gradient * gradient
    normal_step = (
        mean_new
        / (1.0 - MEAN_DECAY**STEP)
        / (jnp.sqrt(square_new / (1.0 - SQUARE_DECAY**STEP)) + ADAM_EPS)
    )
    updated = master - step_rate * (normal_step + decay_rate * master)
    return (mean_new, square_new, updated, updated.astype(jnp.bfloat16))


def update_kernel(*refs):
    y = lax.axis_index("tensor")
    for n in range(2):
        refs[n - 2][y] = refs[2 * n][...]
        refs[n - 2][1 - y] = wide(refs[2 * n + 1][...])
    norm = refs[4]
    totals, at = name_refs(TOTALS, refs, 5)
    masters, firsts, seconds = refs[at : at + 8], refs[at + 8 : at + 16], refs[at + 16 : at + 24]
    outs = refs[at + 24 :]
    factor = MAX_NORM / jnp.maximum(norm[...], MAX_NORM)

    def apply(member, index, gradient):
        results = adam_parts(
            masters[member][index],
            gradient * factor,
            firsts[member][index],
            seconds[member][index],
            RATES[member],
            DECAYS[member],
        )
        for k, result in enumerate(results):
            outs[member * 4 + k][index] = result

    def view(ref, start, width):
        return ref[:, start : start + width]

    heads = (
        lambda start: view(totals.even if start < 384 else totals.odd, start % 384, PAIR),
        lambda start: view(totals.d_heads, start, PAIR),
    )
    rest = ((totals.mlp, totals.shrink), (totals.d_mlp, totals.d_shrink))
    for b in range(2):
        for m in range(3):
            for odd in range(2):
                columns = slice(odd * PAIR, odd * PAIR + PAIR)
                apply(0, (b, m, slice(None), columns), heads[b](odd * 384 + m * PAIR))
        apply(1, (b,), rest[b][0][:, 0:256])
        apply(2, (b,), rest[b][0][:, 256:1280])
        apply(3, (b,), rest[b][1][...])
    small = totals.small[...]
    turned = jnp.concatenate([small, jnp.zeros((112, PAIR), jnp.float32)], axis=0).T
    everything = (slice(None), slice(None))
    apply(4, everything, turned[VEC_ROW : VEC_ROW + 15, 0:16])
    apply(5, everything, small[:, 0:CODE])
    book = totals.book[...].T
    book = jnp.concatenate([book[j * CODE : j * CODE + CODE] for j in range(4)], axis=1)
    apply(6, everything, book)
    apply(7, everything, small[:, DECODE_ROW : DECODE_ROW + CODE])


VMEM_LIMIT = 62 * 1024 * 1024


def run_decoder(tuned, inputs, raw=()):
    f32, bf16, i32 = jnp.float32, jnp.bfloat16, jnp.int32
    any_spec = pl.BlockSpec(memory_space=pl.ANY)
    vmem = pl.BlockSpec(memory_space=pltpu.VMEM)
    half = inputs[0].shape[-1]
    length = 2 * half
    outs = [((length, PAIR), bf16), ((length, PAIR), f32), ((16, WIDTH), f32), ((CODE, WIDTH), f32)]
    outs += [((2, WIDTH, n), bf16) for n in COLUMNS]
    out_specs = [vmem] * 7
    scratch = block_scratch(length)
    scratch += [pltpu.VMEM((length, WIDTH), f32), pltpu.VMEM((16, WIDTH), f32)]
    extra = {}
    if tuned:
        in_specs = [vmem] + [any_spec] * 2 + [vmem] * 8
        outs += [((half, WIDTH), f32), ((half, WIDTH), bf16), ((2, half, WIDTH), bf16)]
        outs += [((2, 1, half), i32), ((WIDTH, PAIR), bf16)]
        out_specs += [vmem] * 5
        outs += [(SPLIT + (32, n), bf16) for n in COLUMNS]
        out_specs += [any_spec] * 3
        scratch += [
            pltpu.VMEM((2, half, WIDTH), bf16),
            pltpu.VMEM((2, 1, half), i32),
            pltpu.VMEM((1, half), i32),
            pltpu.VMEM((PAIR, PAIR), f32),
        ]
        scratch += [pltpu.VMEM((32, n), bf16) for n in COLUMNS + COLUMNS]
        scratch += [pltpu.VMEM((80, PAIR), bf16)]
        scratch += [pltpu.VMEM(SPLIT + (32, n), bf16) for n in COLUMNS]
        scratch += [pltpu.VMEM(SPLIT + (80, PAIR), bf16)]
        scratch += [dma(7), dma(7, 12), dma(7, 12), dma(3), dma(3), dma(3)]
        extra = dict(collective_id=0, has_side_effects=True)
    else:
        in_specs = [vmem] * 7
        outs += [((length, WIDTH), f32)]
        out_specs += [vmem]
    return pl.pallas_call(
        functools.partial(decoder_kernel, tuned),
        out_shape=[jax.ShapeDtypeStruct(shape, dtype) for shape, dtype in outs],
        in_specs=in_specs,
        out_specs=out_specs,
        scratch_shapes=scratch,
        compiler_params=pltpu.CompilerParams(vmem_limit_bytes=VMEM_LIMIT, **extra),
        name="decoder",
    )(*inputs, *raw)


def run_encoder(tuned, inputs, late=(), partials=()):
    f32, bf16 = jnp.float32, jnp.bfloat16
    any_spec = pl.BlockSpec(memory_space=pl.ANY)
    vmem = pl.BlockSpec(memory_space=pltpu.VMEM)
    half = inputs[1].shape[2]
    length = 2 * half
    in_specs = [pl.BlockSpec(memory_space=pltpu.SMEM)] + [vmem] * 8
    scratch = block_scratch(length)
    scratch += [
        pltpu.VMEM((16, WIDTH), f32),
        pltpu.VMEM((length, WIDTH), f32),
        pltpu.VMEM((length, PAIR), f32),
    ]
    extra = {}
    if tuned:
        in_specs += [vmem] * 3 + [any_spec] * 3
        sizes = [(32, n) for n in COLUMNS]
        own_sizes = [(32, n) for n in OWN_COLUMNS] + [(64, PAIR), (16, PAIR)]
        outs = [((half, WIDTH), bf16), ((half, WIDTH), f32), ((half, WIDTH), bf16), ((1, 1), f32)]
        outs += [(size, f32) for size in own_sizes + sizes]
        out_specs = [vmem] * 13
        scratch += [
            pltpu.VMEM((16, WIDTH), f32),
            pltpu.VMEM((CODE, WIDTH), f32),
            pltpu.VMEM((half, WIDTH), bf16),
            pltpu.VMEM((PAIR, WIDTH), f32),
            pltpu.VMEM((12, 8, 128), f32),
        ]
        dtypes = [bf16] * 5 + [f32]
        scratch += [pltpu.VMEM(SPLIT + s, d) for s, d in zip(own_sizes, dtypes)]
        scratch += [pltpu.VMEM((2, 4, 2) + size, bf16) for size in sizes]
        for size, dtype in zip(sizes + own_sizes[4:], [bf16] * 4 + [f32]):
            scratch += reduce_scratch(size, dtype)
        scratch += [dma(9), dma(9, 8), dma(9, 8), dma(2), dma(2), dma(10), dma(10)]
        extra = dict(collective_id=1, has_side_effects=True)
    else:
        outs = [((length, WIDTH), f32), ((16, WIDTH), f32), ((CODE, WIDTH), f32)]
        outs += [((2048, PAIR), bf16)]
        outs += [((2, WIDTH, n), bf16) for n in COLUMNS]
        out_specs = [vmem] * 7
    return pl.pallas_call(
        functools.partial(encoder_kernel, tuned),
        out_shape=[jax.ShapeDtypeStruct(shape, dtype) for shape, dtype in outs],
        in_specs=in_specs,
        out_specs=out_specs,
        scratch_shapes=scratch,
        compiler_params=pltpu.CompilerParams(vmem_limit_bytes=VMEM_LIMIT, **extra),
        name="encoder",
    )(*inputs, *late, *partials)


def run_update(frames_out, norm, totals, masters, firsts, seconds):
    vmem = pl.BlockSpec(memory_space=pltpu.VMEM)
    outs = []
    for master in masters:
        outs += [jax.ShapeDtypeStruct(master.shape, jnp.float32)] * 3
        outs += [jax.ShapeDtypeStruct(master.shape, jnp.bfloat16)]
    args = [*frames_out, norm, *totals, *masters, *firsts, *seconds]
    outs += [jax.ShapeDtypeStruct((2,) + frames_out[0].shape, jnp.float32)] * 2
    return pl.pallas_call(
        update_kernel,
        out_shape=outs,
        in_specs=[vmem] * len(args),
        out_specs=[vmem] * len(outs),
        compiler_params=pltpu.CompilerParams(vmem_limit_bytes=VMEM_LIMIT),
        name="update",
    )(*args)


def turned_states(states):
    heads, merge, expand, shrink, vectors, encode, codebook, decode = states
    merge, shrink = merge.transpose(0, 2, 1), shrink.transpose(0, 2, 1)
    return (heads, merge, expand, shrink, vectors, encode, codebook.T, decode.T)


def local_tuned(frames, codes, clip_frames, out_cotangent, masters, firsts, seconds):
    masters, firsts, seconds = [turned_states(s) for s in (masters, firsts, seconds)]
    results = run_decoder(True, (codes, frames, out_cotangent), masters)
    entries, dchosen, vector_grads, ddecode = results[0:4]
    partials = [g.reshape(SPLIT + (32, g.shape[2])) for g in results[4:7]]
    decoded_near, decoded_far, frame, codes_here, ved = results[7:12]
    weights = [w.reshape(2, WIDTH, w.shape[5]) for w in results[12:15]]
    inputs = (clip_frames, codes_here, frame, entries, dchosen, ved, *weights)
    results = run_encoder(True, inputs, (vector_grads, ddecode, decoded_far), partials)
    decoded_got, dx_near, dx_got, norm = results[0:4]
    frames_out = (decoded_near, decoded_got, dx_near, dx_got)
    *updates, decoded, dframe = run_update(
        frames_out, norm, results[4:], masters, firsts, seconds
    )
    kinds = [turned_states(updates[k::4]) for k in range(4)]
    updates = [kinds[k][member] for member in range(8) for k in range(4)]
    return (decoded, dframe, norm.reshape(()), *updates)


def swap_half(rows):
    return lax.ppermute(rows, "tensor", [(0, 1), (1, 0)])


def join_frame(pair):
    mine = lax.axis_index("tensor")
    own = lax.dynamic_index_in_dim(pair, mine, axis=0, keepdims=False)
    other = lax.dynamic_index_in_dim(pair, 1 - mine, axis=0, keepdims=False)
    return jnp.stack([own, swap_half(other)])


def split_frame(rows):
    mine = lax.axis_index("tensor")
    half = rows.shape[0] // 2
    other = swap_half(rows[half:].astype(jnp.bfloat16)).astype(jnp.float32)
    own = rows[:half]
    return jnp.where(mine == 0, jnp.stack([own, other]), jnp.stack([other, own]))


def gather_plain(shard):
    gathered = lax.all_gather(shard, ("dp", "tensor"), axis=0, tiled=False)
    split = gathered.reshape((lax.axis_size("dp"), 2) + shard.shape)
    return split.transpose(1, 0, 2, 3).reshape(2, -1, shard.shape[1])


def scatter_plain(partial):
    return lax.psum_scatter(
        partial.astype(jnp.float32), ("dp", "tensor"), scatter_dimension=0, tiled=True
    )


def reduce_plain(partial):
    split = partial.reshape(2, lax.axis_size("dp"), -1, partial.shape[2]).transpose(1, 0, 2, 3)
    return scatter_plain(split.reshape(-1, partial.shape[2]))


def local_plain(frames, codes, clip_frames, out_cotangent, masters, firsts, seconds):
    heads, merge, expand, shrink, vectors, encode, codebook, decode = masters
    weights = []
    for b in range(2):
        even = jnp.concatenate([heads[b, m, :, :PAIR] for m in range(3)], axis=1)
        odd = jnp.concatenate([heads[b, m, :, PAIR:] for m in range(3)], axis=1)
        mlp = jnp.concatenate([merge[b].T, expand[b]], axis=1)
        shards = (jnp.concatenate([even, odd], axis=1), mlp, shrink[b].T)
        weights.append([gather_plain(low(shard)) for shard in shards])
    both = ("dp", "tensor")
    columns = vectors.shape[1]
    blank = jnp.zeros((columns, CODE), jnp.float32)
    tall = jnp.pad(vectors.T, ((0, 0), (0, CODE - vectors.shape[0])))
    ved = low(jnp.concatenate([encode, tall, decode.T, blank], axis=1))
    ved = lax.all_gather(ved, both, axis=0, tiled=True)
    book = lax.all_gather(low(codebook), both, axis=0, tiled=True)
    book = book.reshape(4, 2048, CODE).transpose(1, 0, 2).reshape(2048, PAIR)
    code_rows = join_frame(codes).reshape(codes.shape[0], 1, codes.shape[1])
    results = run_decoder(False, (code_rows, join_frame(out_cotangent), ved, book, *weights[1]))
    entries, dchosen, vg_other, ddecode = results[0:4]
    decoder_grads, decoded = results[4:7], results[7]
    inputs = (clip_frames, code_rows, join_frame(frames), entries, dchosen, ved, *weights[0])
    results = run_encoder(False, inputs)
    dframe, vg, dencode, dbook = results[0:4]
    encoder_grads = results[4:7]
    sums = [[reduce_plain(g) for g in grads] for grads in (encoder_grads, decoder_grads)]
    dheads, dmerge, dexpand, dshrink = [], [], [], []
    for heads_sum, mlp_sum, shrink_sum in sums:
        even, odd = heads_sum[:, :384], heads_sum[:, 384:]
        parts = [
            jnp.concatenate([part[:, m * PAIR : (m + 1) * PAIR] for part in (even, odd)], axis=1)
            for m in range(3)
        ]
        dheads.append(jnp.stack(parts))
        dmerge.append(mlp_sum[:, :256].T)
        dexpand.append(mlp_sum[:, 256:])
        dshrink.append(shrink_sum.T)
    small = jnp.concatenate([dencode, vg + vg_other, ddecode], axis=0).T
    small = scatter_plain(small)
    dbook = dbook.reshape(2048, 4, CODE).transpose(1, 0, 2).reshape(-1, CODE)
    gradients = (
        jnp.stack(dheads),
        jnp.stack(dmerge),
        jnp.stack(dexpand),
        jnp.stack(dshrink),
        small[:, CODE : CODE + vectors.shape[0]].T,
        small[:, :CODE],
        scatter_plain(dbook),
        small[:, CODE + 16 :].T,
    )
    squares = sum(jnp.sum(gradient * gradient) for gradient in gradients)
    norm_before = jnp.sqrt(lax.psum(squares, both))
    factor = MAX_NORM / jnp.maximum(norm_before, MAX_NORM)
    updates = []
    for member in range(8):
        updates += adam_parts(
            masters[member],
            gradients[member] * factor,
            firsts[member],
            seconds[member],
            RATES[member],
            DECAYS[member],
        )
    return (split_frame(decoded), split_frame(dframe), norm_before, *updates)


def local(frames, codes, clip_frames, out_cotangent, *states):
    tuned = lax.axis_size("dp") == 16 and lax.axis_size("tensor") == 2
    run = local_tuned if tuned and not FORCE_PLAIN else local_plain
    return run(frames, codes, clip_frames, out_cotangent, states[0:8], states[8:16], states[16:24])


FORCE_PLAIN = False


def solution(mesh):
    return jax.shard_map(
        local,
        mesh=mesh,
        in_specs=(
            P("dp", "tensor", None),
            P("dp", "tensor"),
            P(),
            P("dp", "tensor", None),
            P(None, None, "dp", "tensor"),
            P(None, "tensor", "dp"),
            P(None, "dp", "tensor"),
            P(None, "tensor", "dp"),
            P(None, ("dp", "tensor")),
            P(("dp", "tensor"), None),
            P(("dp", "tensor"), None),
            P(None, ("dp", "tensor")),
            P(None, None, "dp", "tensor"),
            P(None, "tensor", "dp"),
            P(None, "dp", "tensor"),
            P(None, "tensor", "dp"),
            P(None, ("dp", "tensor")),
            P(("dp", "tensor"), None),
            P(("dp", "tensor"), None),
            P(None, ("dp", "tensor")),
            P(None, None, "dp", "tensor"),
            P(None, "tensor", "dp"),
            P(None, "dp", "tensor"),
            P(None, "tensor", "dp"),
            P(None, ("dp", "tensor")),
            P(("dp", "tensor"), None),
            P(("dp", "tensor"), None),
            P(None, ("dp", "tensor")),
        ),
        out_specs=(
            P("dp", "tensor", None),
            P("dp", "tensor", None),
            P(),
            P(None, None, "dp", "tensor"),
            P(None, None, "dp", "tensor"),
            P(None, None, "dp", "tensor"),
            P(None, None, "dp", "tensor"),
            P(None, "tensor", "dp"),
            P(None, "tensor", "dp"),
            P(None, "tensor", "dp"),
            P(None, "tensor", "dp"),
            P(None, "dp", "tensor"),
            P(None, "dp", "tensor"),
            P(None, "dp", "tensor"),
            P(None, "dp", "tensor"),
            P(None, "tensor", "dp"),
            P(None, "tensor", "dp"),
            P(None, "tensor", "dp"),
            P(None, "tensor", "dp"),
            P(None, ("dp", "tensor")),
            P(None, ("dp", "tensor")),
            P(None, ("dp", "tensor")),
            P(None, ("dp", "tensor")),
            P(("dp", "tensor"), None),
            P(("dp", "tensor"), None),
            P(("dp", "tensor"), None),
            P(("dp", "tensor"), None),
            P(("dp", "tensor"), None),
            P(("dp", "tensor"), None),
            P(("dp", "tensor"), None),
            P(("dp", "tensor"), None),
            P(None, ("dp", "tensor")),
            P(None, ("dp", "tensor")),
            P(None, ("dp", "tensor")),
            P(None, ("dp", "tensor")),
        ),
        check_vma=False,
    )
```

```python
import functools
from types import SimpleNamespace

import jax
import jax.numpy as jnp
from jax import lax
from jax.experimental import pallas as pl
from jax.experimental.pallas import tpu as pltpu
from jax.sharding import PartitionSpec as P

HEAD_DIM = 64
STEP = 10


EPS_NORM = 1e-05
EPS_UNIT = 1e-06
COMMIT_WEIGHT = 100.0
MAX_NORM = 1.0
MEAN_DECAY = 0.9
SQUARE_DECAY = 0.95
ADAM_EPS = 1e-08
RATES = (0.1, 0.5, 0.1, 0.05, 1.0, 0.1, 1.0, 0.3)
DECAYS = (0.1, 0.1, 0.1, 0.1, 0.0, 0.1, 0.1, 0.1)

NT = (((1,), (1,)), ((), ()))
NN = (((1,), (0,)), ((), ()))
MESH = pl.DeviceIdType.MESH
PAIR = 128
WIDTH = 512
HIDDEN = 2048
CODE = 32
VEC_ROW = 32
DECODE_ROW = 64
SPLIT = (2, 4, 2, 2)
GELU_SCALE = (2.0 / 3.141592653589793) ** 0.5
GELU_CUBE = 0.044715
GROUPS = ("heads", "mlp", "shrink")
COLUMNS = (768, 1280, 1024)
OWN = ("even", "odd", "mlp", "shrink")
OWN_COLUMNS = (384, 384, 1280, 1024)


def mxu(first, second, dims=NN):
    return lax.dot_general(first, second, dims, preferred_element_type=jnp.float32)


def low(values):
    return values.astype(jnp.bfloat16)


def wide(values):
    return values.astype(jnp.float32)


def two_low(values):
    top = low(values)
    return top, low(values - wide(top))


def head_mask(shape, head):
    return (lax.broadcasted_iota(jnp.int32, shape, 1) // HEAD_DIM) == head


def keep_head(values, head):
    return jnp.where(head_mask(values.shape, head), values, jnp.zeros_like(values))


def norm_parts(rows):
    center = rows - jnp.mean(rows, axis=-1, keepdims=True)
    spread = jnp.mean(center * center, axis=-1, keepdims=True)
    scale = lax.rsqrt(spread + EPS_NORM)
    return center * scale, scale


def norm_back(xhat, scale, gain, grad):
    dxhat = grad * gain
    mean_grad = jnp.mean(dxhat, axis=-1, keepdims=True)
    mean_cross = jnp.mean(dxhat * xhat, axis=-1, keepdims=True)
    return scale * (dxhat - mean_grad - xhat * mean_cross)


def unit_scale(values):
    return lax.rsqrt(jnp.sum(values * values, axis=-1, keepdims=True) + EPS_UNIT)


def unit_back(values, grad):
    inverse = unit_scale(values)
    cross = jnp.sum(values * grad, axis=-1, keepdims=True)
    return inverse * grad - values * (inverse * inverse * inverse * cross)


def add_row(ref, row, values):
    ref[row : row + 1, :] += jnp.sum(values, axis=0, keepdims=True)


def tile_rows(step, tile):
    return pl.ds(pl.multiple_of(step * tile, tile), tile)


def views_of(refs):
    if len(refs) == 3:
        heads, mlp, shrink = refs
        even, odd = (heads, 0, 384), (heads, 384, 384)
    else:
        even, odd, mlp, shrink = refs
        even, odd = (even, 0, 384), (odd, 0, 384)
    merge, expand, shrink = (mlp, 0, 256), (mlp, 256, 1024), (shrink, 0, 1024)
    return SimpleNamespace(even=even, odd=odd, merge=merge, expand=expand, shrink=shrink)


def half_of(view, half, start=0, width=None):
    ref, first, full = view
    columns = slice(first + start, first + start + (width or full))
    if len(ref.shape) == 3:
        return ref[half, :, columns]
    values = ref[half, :, :, :, :, columns]
    return values.reshape(WIDTH, values.shape[-1])


def put_half(view, half, start, values):
    ref, first, _ = view
    columns = slice(first + start, first + start + values.shape[1])
    if len(ref.shape) == 3:
        ref[half, :, columns] = values
    else:
        ref[half, :, :, :, :, columns] = values.reshape(ref.shape[1:5] + (values.shape[-1],))


def remote(src, dst, sems, slot, target):
    send, recv = sems
    return pltpu.make_async_remote_copy(
        src_ref=src,
        dst_ref=dst,
        send_sem=send.at[slot],
        recv_sem=recv.at[slot],
        device_id=target,
        device_id_type=MESH,
    )


def coordinates():
    dp_index = lax.axis_index("dp")
    y = lax.axis_index("tensor")
    return dp_index // 4, (dp_index // 2) % 2, dp_index % 2, y


def partners(z, x, c, y):
    along_z = [(((z + step) % 4) * 4 + x * 2 + c, y) for step in (1, 2, 3)]
    along_x = (z * 4 + (1 - x) * 2 + c, y)
    along_y = (z * 4 + x * 2 + c, 1 - y)
    along_core = (z * 4 + x * 2 + (1 - c), y)
    return along_z, along_x, along_y, along_core


def octet(z, x, c, y):
    places = [(dx, dy, dc) for dx in (0, 1) for dy in (0, 1) for dc in (0, 1)][1:]
    return [
        (z * 4 + ((x + dx) % 2) * 2 + (c + dc) % 2, (y + dy) % 2) for dx, dy, dc in places
    ]


def greet(targets):
    barrier = pltpu.get_barrier_semaphore()
    for target in targets:
        pl.semaphore_signal(barrier, inc=1, device_id=target, device_id_type=MESH)
    return functools.partial(pl.semaphore_wait, barrier, len(targets))


def cuts_of(rows):
    if rows < 32:
        return ((0, rows, True),)
    middle = rows // 32 * 16
    return ((0, middle, True), (middle, rows, False))


class GatherFlow:
    def __init__(self, shard, out, local_sem, sems, slot):
        z, x, c, y = coordinates()
        along_z, along_x, along_y, along_core = partners(z, x, c, y)
        mine = out.at[y, z, x, c]
        column = out.at[y, :, x, c]
        self.own = pltpu.make_async_copy(shard, mine, local_sem.at[slot])
        self.first = [remote(shard, mine, sems, (slot, k), along_z[k]) for k in range(3)]
        self.core_first = [remote(column, column, sems, (slot, 3), along_core)]
        self.second, self.third, self.core_second, self.core_third = [], [], [], []
        for n, (start, stop, by_x) in enumerate(cuts_of(shard.shape[0])):
            rows = slice(start, stop)
            part = out.at[y, :, x, c, rows]
            plane = out.at[y, :, :, c, rows] if by_x else out.at[:, :, x, c, rows]
            got_second = out.at[y, :, 1 - x, c, rows] if by_x else out.at[1 - y, :, x, c, rows]
            got_third = out.at[1 - y, :, :, c, rows] if by_x else out.at[:, :, 1 - x, c, rows]
            near, far = (along_x, along_y) if by_x else (along_y, along_x)
            base = 4 + 4 * n
            self.second.append(remote(part, part, sems, (slot, base), near))
            self.third.append(remote(plane, plane, sems, (slot, base + 1), far))
            self.core_second.append(remote(got_second, got_second, sems, (slot, base + 2), along_core))
            self.core_third.append(remote(got_third, got_third, sems, (slot, base + 3), along_core))

    def begin(self):
        self.own.start()
        for copy in self.first:
            copy.start()

    def after_first(self):
        self.own.wait()
        for copy in self.first:
            copy.wait_recv()
        for copy in self.second + self.core_first:
            copy.start()

    def after_second(self):
        for copy in self.second:
            copy.wait_recv()
        for copy in self.third + self.core_second:
            copy.start()

    def after_third(self):
        for copy in self.third:
            copy.wait_recv()
        for copy in self.core_third:
            copy.start()

    def arrived(self):
        for copy in self.core_first + self.core_second + self.core_third:
            copy.wait_recv()

    def sent(self):
        for copy in self.first + self.second + self.third:
            copy.wait_send()
        for copy in self.core_first + self.core_second + self.core_third:
            copy.wait_send()


class ReduceFlow:
    def __init__(self, partial, held, scratch, local_sem, sems, slot, out):
        z, x, c, y = coordinates()
        along_z, along_x, along_y, along_core = partners(z, x, c, y)
        from_core, from_second, from_first, *from_third = scratch
        self.scratch, self.place, self.out = scratch, (z, x, y), out
        self.own = None
        if held is None:
            self.held, self.tail = partial, (c,)
        else:
            self.held, self.tail = held, ()
            self.own = pltpu.make_async_copy(partial.at[:, :, :, c], held, local_sem.at[slot])
        every = slice(None)
        self.cuts = cuts_of(partial.shape[4])

        def part(*index):
            return self.held.at[index[:3] + self.tail + index[3:]]

        self.core = remote(partial.at[:, :, :, 1 - c], from_core, sems, (slot, 0), along_core)
        self.third, self.second = [], []
        for n, (start, stop, by_x) in enumerate(self.cuts):
            rows = slice(start, stop)
            if by_x:
                leaving, target = part(1 - y, every, every, rows), along_y
                going, near = part(y, every, 1 - x, rows), along_x
            else:
                leaving, target = part(every, every, 1 - x, rows), along_x
                going, near = part(1 - y, every, x, rows), along_y
            self.third.append(remote(leaving, from_third[n], sems, (slot, 1 + n), target))
            landing = from_second.at[:, rows]
            self.second.append(remote(going, landing, sems, (slot, 3 + n), near))
        self.first = [
            remote(
                part(y, (z + k + 1) % 4, x), from_first.at[k], sems, (slot, 5 + k), along_z[k]
            )
            for k in range(3)
        ]

    def begin(self):
        self.core.start()
        if self.own is not None:
            self.own.start()

    def add(self, index, rows, values):
        place = index + self.tail + (rows,)
        self.held[place] = self.held[place] + values

    def after_core(self):
        self.core.wait_recv()
        if self.own is not None:
            self.own.wait()

        @pl.loop(0, 16)
        def _(n):
            index = (n // 8, (n // 2) % 4, n % 2)
            self.add(index, slice(None), self.scratch[0][index])

        for copy in self.third:
            copy.start()

    def after_third(self):
        z, x, y = self.place
        for cut, (start, stop, by_x) in enumerate(self.cuts):
            self.third[cut].wait_recv()

            @pl.loop(0, 8)
            def _(n):
                index = (n // 2, n % 2) if by_x else (n // 4, n % 4)
                place = (y,) + index if by_x else index + (x,)
                self.add(place, slice(start, stop), self.scratch[3 + cut][index])

            self.second[cut].start()

    def after_second(self):
        for copy in self.second:
            copy.wait_recv()
        z, x, y = self.place
        for k in range(4):
            self.add((y, k, x), slice(None), self.scratch[1][k])
        for copy in self.first:
            copy.start()

    def finish(self):
        z, x, y = self.place
        result = wide(self.held[(y, z, x) + self.tail])
        for k in range(3):
            self.first[k].wait_recv()
            result = result + wide(self.scratch[2][k])
        self.out[...] = result

    def sent(self):
        for copy in [self.core] + self.third + self.second + self.first:
            copy.wait_send()


def dma(*shape):
    return pltpu.SemaphoreType.DMA(shape)


def reduce_scratch(size, dtype):
    shapes = [(2, 4, 2) + size, (4,) + size, (3,) + size]
    for start, stop, by_x in cuts_of(size[0]):
        shapes.append(((4, 2) if by_x else (2, 4)) + (stop - start, size[1]))
    return [pltpu.VMEM(shape, dtype) for shape in shapes]


def begin(*flows):
    for flow in flows:
        flow.begin()


def after_first(*flows):
    for flow in flows:
        flow.after_first()


def after_second(*flows):
    for flow in flows:
        flow.after_second()


def after_third(*flows):
    for flow in flows:
        flow.after_third()


def after_core(*flows):
    for flow in flows:
        flow.after_core()


def finish(*flows):
    for flow in flows:
        flow.finish()


def arrived(*flows):
    for flow in flows:
        flow.arrived()


def sent(*flows):
    for flow in flows:
        flow.sent()


def at_pairs(actions):
    def run(count):
        for n, action in enumerate(actions):
            if action is not None:
                pl.when(count == n)(action)

    return run


def nothing():
    pass


class NoPlan:
    attend = back = ()

    def __getattr__(self, name):
        return nothing


def pair_place(count):
    pair = (count % 2) * 2 + count // 2
    wide_start = pl.multiple_of(pair * 384, 384)
    return pair, wide_start, pl.ds(pl.multiple_of(pair * PAIR, PAIR), PAIR)


def pair_columns(wide_start):
    return [pl.ds(pl.multiple_of(wide_start + member * PAIR, PAIR), PAIR) for member in range(3)]


def norm_stage(x_rows, vec, base, n_ref, tile):
    @pl.loop(0, n_ref.shape[0] // tile)
    def _(step):
        rows = tile_rows(step, tile)
        xhat, _ = norm_parts(x_rows(rows, step))
        n_ref[rows, :] = low(xhat * vec[base : base + 1, :] + vec[base + 1 : base + 2, :])


def project_stage(n_ref, weights, p_ref, tile, odd):
    @pl.loop(0, n_ref.shape[0] // tile)
    def _(step):
        rows = tile_rows(step, tile)
        normed = n_ref[rows, :]
        for half in range(2):
            start = (half * 2 + odd) * 384
            p_ref[rows, start : start + 384] = low(mxu(normed, half_of(weights[odd], half)))


def attend_stage(p_ref, mix_ref, lse_ref, tile, first, last, after_pair):
    length = p_ref.shape[0]

    @pl.loop(first, last)
    def _(count):
        pair, wide_start, columns = pair_place(count)
        query_at, key_at, value_at = pair_columns(wide_start)
        keys = p_ref[:, key_at] * (HEAD_DIM**-0.5)
        values = p_ref[:, value_at]
        for start in range(0, length, tile):
            query = p_ref[start : start + tile, query_at]
            out = None
            for head in range(2):
                ones_beside = jnp.where(
                    head_mask(values.shape, head), values, jnp.ones_like(values)
                )
                scores = mxu(keep_head(query, head), keys, NT)
                top = jnp.max(scores, axis=1, keepdims=True)
                raised = low(jnp.exp(scores - top))
                mixed = mxu(raised, ones_beside)
                total = pltpu.roll(mixed, HEAD_DIM, 1)
                mixed = mixed / total
                log_sum = top + jnp.log(total)
                if out is None:
                    out, log_sums = mixed, log_sum
                else:
                    is_first = head_mask(mixed.shape, 0)
                    out = jnp.where(is_first, out, mixed)
                    log_sums = jnp.where(is_first, log_sums, log_sum)
            mix_ref[start : start + tile, columns] = low(out)
            turned = log_sums.T
            for head in range(2):
                lse_ref[pair * 2 + head, :, start : start + tile] = jnp.broadcast_to(
                    turned[head * HEAD_DIM : head * HEAD_DIM + 1], (8, tile)
                )
        after_pair(count)


def expand_stage(x_rows, mix_ref, vec, base, merge_w, expand_w, h_ref, nm_ref, slope_ref, act_ref, tile):
    @pl.loop(0, h_ref.shape[0] // tile)
    def _(step):
        rows = tile_rows(step, tile)
        hidden = x_rows(rows, step) + vec[base + 2 : base + 3, :]
        for half in range(2):
            hidden = hidden + mxu(
                mix_ref[rows, half * 256 : half * 256 + 256], half_of(merge_w, half), NT
            )
        h_ref[rows, :] = hidden
        xhat, _ = norm_parts(hidden)
        normed = low(xhat * vec[base + 3 : base + 4, :] + vec[base + 4 : base + 5, :])
        nm_ref[rows, :] = normed
        for half in range(2):
            for start in range(0, 1024, 512):
                values = mxu(normed, half_of(expand_w, half, start, 512))
                place = slice(half * 1024 + start, half * 1024 + start + 512)
                square = values * values
                bend = jnp.tanh(values * (GELU_SCALE + (GELU_SCALE * GELU_CUBE) * square))
                share = 0.5 + 0.5 * bend
                active = values * share
                act_ref[rows, place] = low(active)
                slope_ref[rows, place] = low(
                    share
                    + (active - active * share)
                    * (2.0 * GELU_SCALE + (6.0 * GELU_SCALE * GELU_CUBE) * square)
                )


def shrink_stage(h_ref, act_ref, vec, base, shrink_w, tile, give):
    @pl.loop(0, h_ref.shape[0] // tile)
    def _(step):
        rows = tile_rows(step, tile)
        out = h_ref[rows, :] + vec[base + 5 : base + 6, :]
        for half in range(2):
            out = out + mxu(
                act_ref[rows, half * 1024 : half * 1024 + 1024], half_of(shrink_w, half), NT
            )
        give(rows, out, step)


def mlp_back_stage(
    dout_rows, h_ref, slope_ref, vec, base, merge_w, expand_w, shrink_w, dmix_ref, vg_ref, tile
):
    @pl.loop(0, h_ref.shape[0] // tile)
    def _(step):
        rows = tile_rows(step, tile)
        dout = wide(dout_rows(rows, step))
        dout_low = low(dout)
        dnormed = None
        for half in range(2):
            for start in range(0, 1024, 512):
                place = slice(half * 1024 + start, half * 1024 + start + 512)
                dactive = mxu(dout_low, half_of(shrink_w, half, start, 512))
                dexpanded = low(dactive * wide(slope_ref[rows, place]))
                slope_ref[rows, place] = dexpanded
                part = mxu(dexpanded, half_of(expand_w, half, start, 512), NT)
                dnormed = part if dnormed is None else dnormed + part
        xhat, scale = norm_parts(h_ref[rows, :])
        dhidden = dout + norm_back(xhat, scale, vec[base + 3 : base + 4, :], dnormed)
        h_ref[rows, :] = dhidden
        dhidden_low = low(dhidden)
        for half in range(2):
            dmix_ref[rows, half * 256 : half * 256 + 256] = low(
                mxu(dhidden_low, half_of(merge_w, half))
            )
        add_row(vg_ref, base + 2, dhidden)
        add_row(vg_ref, base + 3, dnormed * xhat)
        add_row(vg_ref, base + 4, dnormed)
        add_row(vg_ref, base + 5, dout)


def turn_stage(read, turned_ref):
    length = turned_ref.shape[1]
    for start in range(0, length, 256):
        turned_ref[:, start : start + 256] = low(read(start, start + 256)).T


def weight_grad_stage(turned_ref, right_ref, out_ref, half, first, width, chunk):
    for start in range(0, width, chunk):
        product = mxu(turned_ref[...], right_ref[:, first + start : first + start + chunk])
        put_half(out_ref, half, start, low(product))


def attend_back_stage(
    p_ref, mix_ref, dmix_ref, lse_ref, dk_acc, dv_acc, tile, first, last, after_pair
):
    length = p_ref.shape[0]

    @pl.loop(first, last)
    def _(count):
        pair, wide_start, columns = pair_place(count)
        query_at, key_at, value_at = pair_columns(wide_start)
        keys = p_ref[:, key_at] * (HEAD_DIM**-0.5)
        values = p_ref[:, value_at]
        keys_turned = keys.T
        for start in range(0, length, tile):
            rows = slice(start, start + tile)
            query = p_ref[rows, query_at]
            dmix = dmix_ref[rows, columns]
            inner = (wide(dmix) * wide(mix_ref[rows, columns])).T
            dquery, dkeys, dvalues = [], None, None
            for head in range(2):
                span = slice(head * HEAD_DIM, head * HEAD_DIM + HEAD_DIM)
                query_here = keep_head(query, head)
                dmix_here = keep_head(dmix, head)
                delta = jnp.sum(inner[span], axis=0, keepdims=True)
                log_sum = lse_ref[pair * 2 + head, 0:1, rows]
                attend = jnp.exp(mxu(keys, query_here, NT) - log_sum)
                dscores = low(attend * (mxu(values, dmix_here, NT) - delta))
                part = mxu(low(attend), dmix_here)
                dvalues = part if dvalues is None else dvalues + part
                part = mxu(dscores, query_here)
                dkeys = part if dkeys is None else dkeys + part
                dquery.append(mxu(keys_turned[span], dscores))
            p_ref[rows, query_at] = low(jnp.concatenate(dquery, axis=0).T)
            if start == 0:
                dk_acc[...] = dkeys
                dv_acc[...] = dvalues
            elif start + tile < length:
                dk_acc[...] += dkeys
                dv_acc[...] += dvalues
            else:
                p_ref[:, key_at] = low((dk_acc[...] + dkeys) * (HEAD_DIM**-0.5))
                p_ref[:, value_at] = low(dv_acc[...] + dvalues)
        after_pair(count)


def project_back_tile(step, tile, x_rows, h_ref, p_ref, vec, base, weights, vg_ref, give):
    rows = slice(step * tile, step * tile + tile)
    dnormed = None
    for odd in range(2):
        for half in range(2):
            start = (half * 2 + odd) * 384
            product = mxu(p_ref[rows, start : start + 384], half_of(weights[odd], half), NT)
            dnormed = product if dnormed is None else dnormed + product
    xhat, scale = norm_parts(x_rows(rows, step))
    dx = h_ref[rows, :] + norm_back(xhat, scale, vec[base : base + 1, :], dnormed)
    add_row(vg_ref, base, dnormed * xhat)
    add_row(vg_ref, base + 1, dnormed)
    give(rows, dx)


def code_place(codes, tuned):
    if tuned:
        owner = codes // 256
        return ((owner % 2) * 16 + owner // 2) * 64 + codes % 64, (codes // 64) % 4
    return codes % 2048, codes // 2048


def one_hot(place):
    shape = (2048, place.shape[1])
    return low(jnp.where(lax.broadcasted_iota(jnp.int32, shape, 0) == place, 1.0, 0.0))


def in_group(group, values):
    rows = lax.broadcasted_iota(jnp.int32, values.shape, 0) // CODE
    return jnp.where(rows == group, values, jnp.zeros_like(values))


def look_up_stage(codes, codebook, entries_ref, tuned):
    tile = 256
    book_turned = codebook.T
    for start in range(0, entries_ref.shape[0], tile):
        place, group = code_place(codes(start, tile), tuned)
        found = in_group(group, mxu(book_turned, one_hot(place)))
        found = found[0:32] + found[32:64] + found[64:96] + found[96:128]
        found = jnp.concatenate([found, jnp.zeros((96, tile), jnp.float32)], axis=0)
        entries_ref[start : start + tile, :] = low(found.T)


def scatter_stage(codes, dentries_ref, give, tuned):
    tile = 512
    total = None
    for start in range(0, dentries_ref.shape[0], tile):
        place, group = code_place(codes(start, tile), tuned)
        turned = low(dentries_ref[start : start + tile, :].T[0:CODE])
        placed = in_group(group, wide(jnp.concatenate([turned] * 4, axis=0)))
        part = mxu(one_hot(place), low(placed), NT)
        total = part if total is None else total + part
    give(low(total))


def square_sum(values):
    rows, width = values.shape
    values = values * values
    total = jnp.zeros((8, 128), jnp.float32)
    for r in range(0, rows, 8):
        for w in range(0, width, 128):
            total = total + values[r : r + 8, w : w + 128]
    return total


def sum_over_devices(square, squares, sums):
    z, x, c, y = coordinates()
    total = jnp.broadcast_to(jnp.sum(square, keepdims=True), (8, 128))
    stage = 0
    for n, targets in enumerate((octet(z, x, c, y), partners(z, x, c, y)[0])):
        squares[n] = total
        copies = []
        for target in targets:
            copy = remote(squares.at[n], squares.at[2 + stage], sums, stage, target)
            copy.start()
            copies.append((copy, 2 + stage))
            stage += 1
        for copy, place in copies:
            copy.wait()
            total = total + squares[place]
    return total


class Swap:
    def __init__(self, source, target, sems, local_sem, slot):
        z, x, c, y = coordinates()
        along_y = partners(z, x, c, y)[2]
        self.own = pltpu.make_async_copy(source.at[y], target.at[0], local_sem.at[slot])
        self.other = remote(source.at[1 - y], target.at[1], sems, slot, along_y)

    def begin(self):
        self.other.start()
        self.own.start()

    def arrived(self):
        self.own.wait()
        self.other.wait_recv()

    def sent(self):
        self.other.wait_send()


class Send:
    def __init__(self, give, got, sems, slot):
        z, x, c, y = coordinates()
        self.other = remote(give, got, sems, slot, partners(z, x, c, y)[2])

    def begin(self):
        self.other.start()

    def arrived(self):
        self.other.wait_recv()

    def sent(self):
        self.other.wait_send()


class Move:
    def __init__(self, source, target, sem):
        self.copy = pltpu.make_async_copy(source, target, sem)

    def begin(self):
        self.copy.start()

    def arrived(self):
        self.copy.wait()


class DecoderPlan(NoPlan):
    def __init__(self, flows):
        self.f = flows
        self.attend = (self.attend0, self.attend1, self.attend2, self.attend3)
        self.back = (self.back0, None, self.back2, None)

    def start(self):
        f = self.f
        begin(f.codes, f.small, f.heads, f.cot)

    def packed(self):
        f = self.f
        after_first(f.small, f.heads)
        begin(f.mlp)
        after_second(f.small, f.heads)
        after_third(f.small)
        arrived(f.small, f.codes)

    def look(self):
        f = self.f
        after_third(f.heads)
        after_first(f.mlp)
        begin(f.shrink)
        arrived(f.heads)

    def attend0(self):
        after_second(self.f.mlp)

    def attend1(self):
        after_first(self.f.shrink)
        begin(self.f.e_heads)

    def attend2(self):
        begin(self.f.e_mlp)

    def attend3(self):
        after_third(self.f.mlp)
        after_second(self.f.shrink)
        arrived(self.f.mlp)

    def expand(self):
        f = self.f
        after_third(f.shrink)
        after_first(f.e_heads, f.e_mlp)
        arrived(f.shrink)

    def shrink(self):
        begin(self.f.e_shrink)
        arrived(self.f.cot)

    def mlp_back(self):
        after_second(self.f.e_heads, self.f.e_mlp)

    def dshrink(self):
        begin(self.f.g_shrink)

    def dexpand(self):
        after_first(self.f.e_shrink)

    def dmerge(self):
        begin(self.f.g_mlp)

    def dheads(self):
        begin(self.f.g_heads)

    def back0(self):
        f = self.f
        after_third(f.e_heads, f.e_mlp)
        after_second(f.e_shrink)
        begin(f.frame)

    def back2(self):
        after_third(self.f.e_shrink)

    def end(self):
        f = self.f
        arrived(f.e_heads, f.e_mlp, f.e_shrink, f.frame)
        sent(f.codes, f.small, f.heads, f.mlp, f.shrink, f.cot, f.frame)
        sent(f.e_heads, f.e_mlp, f.e_shrink)
        arrived(f.g_heads, f.g_mlp, f.g_shrink)


class EncoderPlan(NoPlan):
    def __init__(self, flows):
        self.f = flows
        self.attend = (self.attend0, self.attend1, self.attend2, self.attend3)
        self.back = (self.back0, self.back1, self.back2, self.back3)

    def start(self):
        f = self.f
        begin(f.d_shrink, f.d_mlp, f.d_heads)

    def norm(self):
        arrived(self.f.w_heads)

    def project(self):
        after_core(self.f.d_shrink)

    def attend0(self):
        after_core(self.f.d_mlp)

    def attend1(self):
        after_core(self.f.d_heads)

    def attend2(self):
        after_third(self.f.d_shrink)

    def attend3(self):
        after_third(self.f.d_mlp)
        arrived(self.f.w_mlp)

    def expand(self):
        arrived(self.f.w_shrink)
        after_second(self.f.d_shrink)
        after_third(self.f.d_heads)

    def shrink(self):
        after_second(self.f.d_mlp)
        finish(self.f.d_shrink)
        begin(self.f.decoded)

    def mlp_back(self):
        after_second(self.f.d_heads)
        finish(self.f.d_mlp)
        begin(self.f.book)

    def dshrink(self):
        after_core(self.f.book)
        begin(self.f.shrink)
        finish(self.f.d_heads)

    def dmerge(self):
        begin(self.f.mlp)
        after_third(self.f.book)
        after_core(self.f.shrink)

    def back0(self):
        after_second(self.f.book)
        after_core(self.f.mlp)

    def back1(self):
        finish(self.f.book)
        after_third(self.f.shrink)

    def deven(self):
        begin(self.f.even)

    def back2(self):
        after_third(self.f.mlp)
        after_second(self.f.shrink)
        after_core(self.f.even)

    def back3(self):
        after_second(self.f.mlp)
        after_third(self.f.even)
        finish(self.f.shrink)

    def dodd(self):
        begin(self.f.odd)
        after_core(self.f.odd)

    def far(self):
        after_second(self.f.even)

    def near(self):
        finish(self.f.mlp)

    def vectors(self):
        f = self.f
        begin(f.small)
        after_third(f.odd)
        after_core(f.small)
        after_second(f.odd)
        begin(f.dframe)
        after_third(f.small)
        finish(f.even)
        after_second(f.small)

    def last(self):
        finish(self.f.odd, self.f.small)

    def end(self):
        f = self.f
        arrived(f.decoded, f.dframe)
        sent(f.d_shrink, f.d_mlp, f.d_heads, f.decoded, f.dframe)
        sent(f.even, f.odd, f.mlp, f.shrink, f.small, f.book)


def name_refs(names, refs, start):
    stop = start + len(names)
    return SimpleNamespace(**dict(zip(names, refs[start:stop]))), stop


BLOCK_SCRATCH = ("n", "p", "mix", "lse", "h", "nm", "slope", "act", "dmix", "dk", "dv", "turned")


def block_scratch(length):
    f32, bf16 = jnp.float32, jnp.bfloat16
    shapes = [
        ((length, WIDTH), bf16),
        ((length, 3 * WIDTH), bf16),
        ((length, WIDTH), bf16),
        ((8, 8, length), f32),
        ((length, WIDTH), f32),
        ((length, WIDTH), bf16),
        ((length, HIDDEN), bf16),
        ((length, HIDDEN), bf16),
        ((length, WIDTH), bf16),
        ((length, PAIR), f32),
        ((length, PAIR), f32),
        ((WIDTH, length), bf16),
    ]
    return [pltpu.VMEM(shape, dtype) for shape, dtype in shapes]


def pack_heads(raw, shard, b):
    for odd in range(2):
        for member in range(3):
            start = odd * 384 + member * PAIR
            shard[:, start : start + PAIR] = low(raw.heads[b, member, :, odd * PAIR : odd * PAIR + PAIR])


def pack_rest(raw, mlp, shrink, b):
    mlp[:, 0:256] = low(raw.merge[b])
    mlp[:, 256:1280] = low(raw.expand[b])
    shrink[...] = low(raw.shrink[b])


def pack_small(raw, small, turn):
    turn[...] = jnp.zeros_like(turn)
    turn[VEC_ROW : VEC_ROW + 15, 0:16] = raw.vectors[...]
    rows = turn[...].T[0:16]
    blank = jnp.zeros((16, CODE), jnp.float32)
    sides = jnp.concatenate([raw.encode[...], blank, raw.decode[...], blank], axis=1)
    small[0:16, :] = low(rows + sides)
    codebook = raw.codebook[...].T
    book = [codebook[j * 64 : j * 64 + 64, :] for j in range(4)]
    small[16:80, :] = low(jnp.concatenate(book, axis=1))


RAW = ("heads", "merge", "expand", "shrink", "vectors", "encode", "codebook", "decode")
E_GROUPS = ("e_heads", "e_mlp", "e_shrink")
D_GROUPS = ("d_heads", "d_mlp", "d_shrink")
TOTALS = OWN + ("book", "small") + D_GROUPS


def decoder_kernel(tuned, *refs):
    at = 0
    if tuned:
        (codes_in, frames_in, cot_in), at = refs[:3], 3
        raw, at = name_refs(RAW, refs, at)
    else:
        (codes, cot, ved, book), at = refs[:4], 4
        weights, at = views_of(refs[at : at + 3]), at + 3
    (entries, dchosen, vg, ddecode), at = refs[at : at + 4], at + 4
    grad_outs, at = refs[at : at + 3], at + 3
    grads = views_of(grad_outs)
    if tuned:
        (near, far, frame, codes_out, ved), at = refs[at : at + 5], at + 5
        moved, at = refs[at : at + 3], at + 3
    else:
        (out_buf,), at = refs[at : at + 1], at + 1
    s, at = name_refs(BLOCK_SCRATCH, refs, at)
    (x_buf, vec), at = refs[at : at + 2], at + 2
    plan = NoPlan()
    tile = 512
    if tuned:
        (cot, codes, code_give, turn), at = refs[at : at + 4], at + 4
        shards, at = name_refs(GROUPS + E_GROUPS + ("small",), refs, at)
        gathered, at = refs[at : at + 3], at + 3
        made, at = refs[at : at + 3], at + 3
        grads = views_of(made)
        (small, local_sem, send, recv, swap_local, swap_send, swap_recv, made_sem) = refs[at:]
        weights = views_of(gathered)
        f = SimpleNamespace()
        f.g_heads, f.g_mlp, f.g_shrink = [
            Move(made[n], grad_outs[n], made_sem.at[n]) for n in range(3)
        ]
        targets = tuple(gathered) + tuple(moved) + (small,)
        for slot, (name, shard) in enumerate(vars(shards).items()):
            flow = GatherFlow(shard, targets[slot], local_sem, (send, recv), slot)
            setattr(f, name, flow)
        swaps = (swap_send, swap_recv)
        f.codes = Send(code_give, codes.at[1], swaps, 0)
        f.cot = Swap(cot_in, cot, swaps, swap_local, 1)
        f.frame = Swap(frames_in, frame, swaps, swap_local, 2)
        along_z, along_x, along_y, along_core = partners(*coordinates())
        greeted = greet(along_z + [along_x, along_y, along_core])
        pack_small(raw, shards.small, turn)
        pack_heads(raw, shards.heads, 1)
        y = lax.axis_index("tensor")
        codes[0] = jnp.where(y == 0, codes_in[0:1, :], codes_in[1:2, :])
        code_give[...] = jnp.where(y == 0, codes_in[1:2, :], codes_in[0:1, :])
        greeted()
        plan = DecoderPlan(f)
    plan.start()
    if tuned:
        pack_rest(raw, shards.mlp, shards.shrink, 1)
        pack_heads(raw, shards.e_heads, 0)
        pack_rest(raw, shards.e_mlp, shards.e_shrink, 0)
        plan.packed()
        for dp in range(16):
            for t in range(2):
                row = (dp * 2 + t) * 16
                ved[row : row + 16, :] = small[t, dp // 4, (dp // 2) % 2, dp % 2, 0:16, :]
        book_rows = small[:, :, :, :, 16:80, :].reshape(2048, PAIR)
        codes_out[...] = codes[...]
    else:
        book_rows = book[...]
    turned_small = wide(ved[...]).T
    vec[...] = turned_small[VEC_ROW : VEC_ROW + 16]
    decode = low(turned_small[DECODE_ROW : DECODE_ROW + CODE])
    decode = jnp.concatenate([decode, jnp.zeros((96, WIDTH), jnp.bfloat16)], axis=0)

    def read_codes(start, size):
        half, first = start // 512, start % 512
        return codes[half, :, first : first + size]

    vg[...] = jnp.zeros_like(vg)
    ddecode[...] = jnp.zeros_like(ddecode)
    look_up_stage(read_codes, book_rows, entries, tuned)
    values = wide(entries[...])
    x_buf[...] = mxu(low(values * unit_scale(values)), decode) + vec[14:15, :]
    base = 6
    x_rows = lambda rows, _: x_buf[rows, :]
    norm_stage(x_rows, vec, base, s.n, tile)
    plan.look()
    first_w = (weights.even, weights.odd)
    for odd in range(2):
        project_stage(s.n, first_w, s.p, tile, odd)
    plan.project()
    attend_stage(
        s.p, s.mix, s.lse, tile, 0, 4, at_pairs(plan.attend)
    )
    expand_stage(
        x_rows, s.mix, vec, base, weights.merge, weights.expand, s.h, s.nm,
        s.slope, s.act, tile,
    )
    plan.expand()

    def give_out(rows, out, part):
        if not tuned:
            out_buf[rows, :] = out
            return

        @pl.when(part == 0)
        def _():
            near[...] = out

        @pl.when(part == 1)
        def _():
            far[...] = low(out)

    shrink_stage(s.h, s.act, vec, base, weights.shrink, tile, give_out)
    plan.shrink()
    mlp_back_stage(
        lambda rows, half: cot[half], s.h, s.slope, vec, base, weights.merge,
        weights.expand, weights.shrink, s.dmix, vg, tile,
    )
    plan.mlp_back()
    turned = s.turned
    turn_stage(lambda a, b: cot[a // 512, a % 512 : a % 512 + 256, :], turned)
    for half in range(2):
        weight_grad_stage(turned, s.act, grads.shrink, half, half * 1024, 1024, 512)
    plan.dshrink()
    turn_stage(lambda a, b: s.nm[a:b, :], turned)
    for half in range(2):
        weight_grad_stage(turned, s.slope, grads.expand, half, half * 1024, 1024, 512)
    plan.dexpand()
    turn_stage(lambda a, b: s.h[a:b, :], turned)
    for half in range(2):
        weight_grad_stage(turned, s.mix, grads.merge, half, half * 256, 256, 256)
    plan.dmerge()
    attend_back_stage(
        s.p, s.mix, s.dmix, s.lse, s.dk, s.dv, tile, 0, 4,
        at_pairs(plan.back),
    )
    turn_stage(lambda a, b: s.n[a:b, :], turned)
    for odd, target in enumerate((grads.even, grads.odd)):
        for half in range(2):
            weight_grad_stage(turned, s.p, target, half, (half * 2 + odd) * 384, 384, 384)
    plan.dheads()

    def give_dx(rows, dx):
        add_row(vg, 14, dx)
        picked = wide(entries[rows, :])
        chosen_turned = low(picked * unit_scale(picked)).T[0:CODE]
        total = None
        for part in two_low(dx):
            ddecode[...] += mxu(chosen_turned, part)
            product = mxu(part, decode, NT)
            total = product if total is None else total + product
        dchosen[rows, :] = total

    for half in (1, 0):
        project_back_tile(
            half, tile, x_rows, s.h, s.p, vec, base, first_w, vg, give_dx
        )
    plan.end()


def encoder_kernel(tuned, *refs):
    (clip_frames, codes, frame, entries, dchosen, ved), at = refs[:6], 6
    weight_ins, at = refs[at : at + 3], at + 3
    weights = views_of(weight_ins)
    if tuned:
        (vg_other, ddecode, decoded_far), at = refs[at : at + 3], at + 3
        partials, at = refs[at : at + 3], at + 3
        (decoded_got, dx_near, dx_got, norm), at = refs[at : at + 4], at + 4
        totals, at = name_refs(TOTALS, refs, at)
    else:
        (dx_buf, vg, dencode, dbook), at = refs[at : at + 4], at + 4
        grads, at = views_of(refs[at : at + 3]), at + 3
    s, at = name_refs(BLOCK_SCRATCH, refs, at)
    (vec, dout_buf, dentries), at = refs[at : at + 3], at + 3
    plan = NoPlan()
    tile = 512
    if tuned:
        (vg, dencode, give, collect, squares), at = refs[at : at + 5], at + 5
        brought, at = refs[at : at + 3], at + 3
        weights = views_of(brought)
        own, at = refs[at : at + 6], at + 6
        grads, (dbook, dsmall) = views_of(own[:4]), own[4:]
        held, at = refs[at : at + 3], at + 3
        receive = []
        for rows in (32, 32, 32, 64, 16):
            count = 3 + len(cuts_of(rows))
            receive.append(refs[at : at + count])
            at += count
        local_sem, send, recv, swap_send, swap_recv, sum_send, sum_recv, brought_sem = refs[at:]
        heads, mlp, shrink, book, small = receive
        even, odd = [
            [ref.at[(slice(None),) * (len(ref.shape) - 1) + (slice(c, c + 384),)] for ref in heads]
            for c in (0, 384)
        ]
        sources = list(zip(own, (even, odd, mlp, shrink, book, small), [None] * 6))
        sources += list(zip(partials, (heads, mlp, shrink), held))
        f = SimpleNamespace()
        f.w_heads, f.w_mlp, f.w_shrink = [
            Move(weight_ins[n], brought[n], brought_sem.at[n]) for n in range(3)
        ]
        begin(f.w_heads, f.w_mlp, f.w_shrink)
        for slot, (name, out) in enumerate(vars(totals).items()):
            source, scratch, kept = sources[slot]
            flow = ReduceFlow(source, kept, scratch, local_sem, (send, recv), slot, out)
            setattr(f, name, flow)
        swaps = (swap_send, swap_recv)
        f.decoded = Send(decoded_far, decoded_got, swaps, 0)
        f.dframe = Send(give, dx_got, swaps, 1)
        place = coordinates()
        greet(octet(*place) + partners(*place)[0])()
        plan = EncoderPlan(f)
    plan.start()
    turned_small = wide(ved[...]).T
    vec[...] = turned_small[VEC_ROW : VEC_ROW + 16]
    encode = jnp.where(
        lax.broadcasted_iota(jnp.int32, ved.shape, 1) < CODE, ved[...], jnp.zeros_like(ved)
    )
    frame_id = lax.axis_index("dp") * 2 + lax.axis_index("tensor")
    clip_end, clip_count = 0, 1
    for clip in range(clip_frames.shape[0]):
        size = clip_frames[clip]
        inside = (frame_id >= clip_end) & (frame_id < clip_end + size)
        clip_count = jnp.where(inside, size, clip_count)
        clip_end = clip_end + size
    clip_weight = (2.0 * COMMIT_WEIGHT) / jnp.full((1, 1), clip_count).astype(jnp.float32)
    vg[...] = jnp.zeros_like(vg)
    dencode[...] = jnp.zeros_like(dencode)
    base = 0
    x_rows = lambda rows, half: wide(frame[half])
    norm_stage(x_rows, vec, base, s.n, tile)
    plan.norm()
    first_w = (weights.even, weights.odd)
    for odd in range(2):
        project_stage(s.n, first_w, s.p, tile, odd)
    plan.project()
    attend_stage(
        s.p, s.mix, s.lse, tile, 0, 4, at_pairs(plan.attend)
    )
    expand_stage(
        x_rows, s.mix, vec, base, weights.merge, weights.expand, s.h, s.nm,
        s.slope, s.act, tile,
    )
    plan.expand()

    def give_out(rows, out, _):
        xhat, scale = norm_parts(out)
        normed = low(xhat * vec[12:13, :] + vec[13:14, :])
        raw = mxu(normed, encode)
        picked = wide(entries[rows, :])
        pull = clip_weight * (
            raw * unit_scale(raw) - picked * unit_scale(picked)
        )
        dentries[rows, :] = unit_back(picked, dchosen[rows, :] - pull)
        draw = unit_back(raw, pull)
        dnormed = None
        for part in two_low(draw):
            product = mxu(part, encode, NT)
            dnormed = product if dnormed is None else dnormed + product
            dencode[...] += mxu(part.T[0:CODE], normed)
        dout_buf[rows, :] = norm_back(xhat, scale, vec[12:13, :], dnormed)
        add_row(vg, 12, dnormed * xhat)
        add_row(vg, 13, dnormed)

    shrink_stage(s.h, s.act, vec, base, weights.shrink, tile, give_out)
    plan.shrink()

    def read_codes(start, size):
        half, first = start // 512, start % 512
        return codes[half, :, first : first + size]

    def give_book(total):
        if tuned:
            dbook[...] = total.reshape(SPLIT + (64, PAIR))
        else:
            dbook[...] = total

    scatter_stage(read_codes, dentries, give_book, tuned)
    mlp_back_stage(
        lambda rows, _: dout_buf[rows, :], s.h, s.slope, vec, base, weights.merge,
        weights.expand, weights.shrink, s.dmix, vg, tile,
    )
    plan.mlp_back()
    turned = s.turned
    turn_stage(lambda a, b: dout_buf[a:b, :], turned)
    for half in range(2):
        weight_grad_stage(turned, s.act, grads.shrink, half, half * 1024, 1024, 512)
    plan.dshrink()
    turn_stage(lambda a, b: s.nm[a:b, :], turned)
    for half in range(2):
        weight_grad_stage(turned, s.slope, grads.expand, half, half * 1024, 1024, 512)
    plan.dexpand()
    turn_stage(lambda a, b: s.h[a:b, :], turned)
    for half in range(2):
        weight_grad_stage(turned, s.mix, grads.merge, half, half * 256, 256, 256)
    plan.dmerge()
    turn_stage(lambda a, b: s.n[a:b, :], turned)
    after = (plan.deven, plan.dodd)
    for odd, target in enumerate((grads.even, grads.odd)):
        attend_back_stage(
            s.p, s.mix, s.dmix, s.lse, s.dk, s.dv, tile, odd * 2, odd * 2 + 2,
            at_pairs(plan.back),
        )
        for half in range(2):
            weight_grad_stage(turned, s.p, target, half, (half * 2 + odd) * 384, 384, 384)
        after[odd]()

    def give_dx(rows, dx):
        if not tuned:
            dx_buf[rows, :] = dx
        elif rows.start == 0:
            dx_near[...] = dx
        else:
            give[...] = low(dx)

    for half, done in ((1, plan.far), (0, plan.near)):
        project_back_tile(
            half, tile, x_rows, s.h, s.p, vec, base, first_w, vg, give_dx
        )
        done()
    if not tuned:
        return
    collect[...] = jnp.zeros_like(collect)
    collect[0:CODE, :] = dencode[...]
    collect[VEC_ROW : VEC_ROW + 16, :] = vg[...] + vg_other[...]
    collect[DECODE_ROW : DECODE_ROW + CODE, :] = ddecode[...]
    rows = collect[...].T
    for dp in range(16):
        for t in range(2):
            row = (dp * 2 + t) * 16
            dsmall[t, dp // 4, (dp // 2) % 2, dp % 2] = rows[row : row + 16]
    plan.vectors()
    square = jnp.zeros((8, 128), jnp.float32)
    late = (totals.odd, totals.small)
    for total in vars(totals).values():
        if not any(total is other for other in late):
            square = square + square_sum(total[...])
    plan.last()
    for total in late:
        square = square + square_sum(total[...])
    norm[...] = jnp.sqrt(sum_over_devices(square, squares, (sum_send, sum_recv)))[0:1, 0:1]
    plan.end()


def adam_parts(master, gradient, first_state, second_state, step_rate, decay_rate):
    mean_new = MEAN_DECAY * first_state + (1.0 - MEAN_DECAY) * gradient
    square_new = SQUARE_DECAY * second_state + (1.0 - SQUARE_DECAY) * gradient * gradient
    normal_step = (
        mean_new
        / (1.0 - MEAN_DECAY**STEP)
        / (jnp.sqrt(square_new / (1.0 - SQUARE_DECAY**STEP)) + ADAM_EPS)
    )
    updated = master - step_rate * (normal_step + decay_rate * master)
    return (mean_new, square_new, updated, updated.astype(jnp.bfloat16))


def update_kernel(*refs):
    y = lax.axis_index("tensor")
    for n in range(2):
        refs[n - 2][y] = refs[2 * n][...]
        refs[n - 2][1 - y] = wide(refs[2 * n + 1][...])
    norm = refs[4]
    totals, at = name_refs(TOTALS, refs, 5)
    masters, firsts, seconds = refs[at : at + 8], refs[at + 8 : at + 16], refs[at + 16 : at + 24]
    outs = refs[at + 24 :]
    factor = MAX_NORM / jnp.maximum(norm[...], MAX_NORM)

    def apply(member, index, gradient):
        results = adam_parts(
            masters[member][index],
            gradient * factor,
            firsts[member][index],
            seconds[member][index],
            RATES[member],
            DECAYS[member],
        )
        for k, result in enumerate(results):
            outs[member * 4 + k][index] = result

    def view(ref, start, width):
        return ref[:, start : start + width]

    heads = (
        lambda start: view(totals.even if start < 384 else totals.odd, start % 384, PAIR),
        lambda start: view(totals.d_heads, start, PAIR),
    )
    rest = ((totals.mlp, totals.shrink), (totals.d_mlp, totals.d_shrink))
    for b in range(2):
        for m in range(3):
            for odd in range(2):
                columns = slice(odd * PAIR, odd * PAIR + PAIR)
                apply(0, (b, m, slice(None), columns), heads[b](odd * 384 + m * PAIR))
        apply(1, (b,), rest[b][0][:, 0:256])
        apply(2, (b,), rest[b][0][:, 256:1280])
        apply(3, (b,), rest[b][1][...])
    small = totals.small[...]
    turned = jnp.concatenate([small, jnp.zeros((112, PAIR), jnp.float32)], axis=0).T
    everything = (slice(None), slice(None))
    apply(4, everything, turned[VEC_ROW : VEC_ROW + 15, 0:16])
    apply(5, everything, small[:, 0:CODE])
    book = totals.book[...].T
    book = jnp.concatenate([book[j * CODE : j * CODE + CODE] for j in range(4)], axis=1)
    apply(6, everything, book)
    apply(7, everything, small[:, DECODE_ROW : DECODE_ROW + CODE])


VMEM_LIMIT = 62 * 1024 * 1024


def run_decoder(tuned, inputs, raw=()):
    f32, bf16, i32 = jnp.float32, jnp.bfloat16, jnp.int32
    any_spec = pl.BlockSpec(memory_space=pl.ANY)
    vmem = pl.BlockSpec(memory_space=pltpu.VMEM)
    half = inputs[0].shape[-1]
    length = 2 * half
    outs = [((length, PAIR), bf16), ((length, PAIR), f32), ((16, WIDTH), f32), ((CODE, WIDTH), f32)]
    outs += [((2, WIDTH, n), bf16) for n in COLUMNS]
    out_specs = [vmem] * 7
    scratch = block_scratch(length)
    scratch += [pltpu.VMEM((length, WIDTH), f32), pltpu.VMEM((16, WIDTH), f32)]
    extra = {}
    if tuned:
        in_specs = [vmem] + [any_spec] * 2 + [vmem] * 8
        out_specs[4:7] = [any_spec] * 3
        outs += [((half, WIDTH), f32), ((half, WIDTH), bf16), ((2, half, WIDTH), bf16)]
        outs += [((2, 1, half), i32), ((WIDTH, PAIR), bf16)]
        out_specs += [vmem] * 5
        outs += [(SPLIT + (32, n), bf16) for n in COLUMNS]
        out_specs += [any_spec] * 3
        scratch += [
            pltpu.VMEM((2, half, WIDTH), bf16),
            pltpu.VMEM((2, 1, half), i32),
            pltpu.VMEM((1, half), i32),
            pltpu.VMEM((PAIR, PAIR), f32),
        ]
        scratch += [pltpu.VMEM((32, n), bf16) for n in COLUMNS + COLUMNS]
        scratch += [pltpu.VMEM((80, PAIR), bf16)]
        scratch += [pltpu.VMEM(SPLIT + (32, n), bf16) for n in COLUMNS]
        scratch += [pltpu.VMEM((2, WIDTH, n), bf16) for n in COLUMNS]
        scratch += [pltpu.VMEM(SPLIT + (80, PAIR), bf16)]
        scratch += [dma(7), dma(7, 12), dma(7, 12), dma(3), dma(3), dma(3), dma(3)]
        extra = dict(collective_id=0, has_side_effects=True)
    else:
        in_specs = [vmem] * 7
        outs += [((length, WIDTH), f32)]
        out_specs += [vmem]
    return pl.pallas_call(
        functools.partial(decoder_kernel, tuned),
        out_shape=[jax.ShapeDtypeStruct(shape, dtype) for shape, dtype in outs],
        in_specs=in_specs,
        out_specs=out_specs,
        scratch_shapes=scratch,
        compiler_params=pltpu.CompilerParams(vmem_limit_bytes=VMEM_LIMIT, **extra),
        name="decoder",
    )(*inputs, *raw)


def run_encoder(tuned, inputs, late=(), partials=()):
    f32, bf16 = jnp.float32, jnp.bfloat16
    any_spec = pl.BlockSpec(memory_space=pl.ANY)
    vmem = pl.BlockSpec(memory_space=pltpu.VMEM)
    half = inputs[1].shape[2]
    length = 2 * half
    in_specs = [pl.BlockSpec(memory_space=pltpu.SMEM)] + [vmem] * 8
    scratch = block_scratch(length)
    scratch += [
        pltpu.VMEM((16, WIDTH), f32),
        pltpu.VMEM((length, WIDTH), f32),
        pltpu.VMEM((length, PAIR), f32),
    ]
    extra = {}
    if tuned:
        in_specs[6:9] = [any_spec] * 3
        in_specs += [vmem] * 3 + [any_spec] * 3
        sizes = [(32, n) for n in COLUMNS]
        own_sizes = [(32, n) for n in OWN_COLUMNS] + [(64, PAIR), (16, PAIR)]
        outs = [((half, WIDTH), bf16), ((half, WIDTH), f32), ((half, WIDTH), bf16), ((1, 1), f32)]
        outs += [(size, f32) for size in own_sizes + sizes]
        out_specs = [vmem] * 13
        scratch += [
            pltpu.VMEM((16, WIDTH), f32),
            pltpu.VMEM((CODE, WIDTH), f32),
            pltpu.VMEM((half, WIDTH), bf16),
            pltpu.VMEM((PAIR, WIDTH), f32),
            pltpu.VMEM((12, 8, 128), f32),
        ]
        scratch += [pltpu.VMEM((2, WIDTH, n), bf16) for n in COLUMNS]
        dtypes = [bf16] * 5 + [f32]
        scratch += [pltpu.VMEM(SPLIT + s, d) for s, d in zip(own_sizes, dtypes)]
        scratch += [pltpu.VMEM((2, 4, 2) + size, bf16) for size in sizes]
        for size, dtype in zip(sizes + own_sizes[4:], [bf16] * 4 + [f32]):
            scratch += reduce_scratch(size, dtype)
        scratch += [dma(9), dma(9, 8), dma(9, 8), dma(2), dma(2), dma(10), dma(10), dma(3)]
        extra = dict(collective_id=1, has_side_effects=True)
    else:
        outs = [((length, WIDTH), f32), ((16, WIDTH), f32), ((CODE, WIDTH), f32)]
        outs += [((2048, PAIR), bf16)]
        outs += [((2, WIDTH, n), bf16) for n in COLUMNS]
        out_specs = [vmem] * 7
    return pl.pallas_call(
        functools.partial(encoder_kernel, tuned),
        out_shape=[jax.ShapeDtypeStruct(shape, dtype) for shape, dtype in outs],
        in_specs=in_specs,
        out_specs=out_specs,
        scratch_shapes=scratch,
        compiler_params=pltpu.CompilerParams(vmem_limit_bytes=VMEM_LIMIT, **extra),
        name="encoder",
    )(*inputs, *late, *partials)


def run_update(frames_out, norm, totals, masters, firsts, seconds):
    vmem = pl.BlockSpec(memory_space=pltpu.VMEM)
    outs = []
    for master in masters:
        outs += [jax.ShapeDtypeStruct(master.shape, jnp.float32)] * 3
        outs += [jax.ShapeDtypeStruct(master.shape, jnp.bfloat16)]
    args = [*frames_out, norm, *totals, *masters, *firsts, *seconds]
    outs += [jax.ShapeDtypeStruct((2,) + frames_out[0].shape, jnp.float32)] * 2
    return pl.pallas_call(
        update_kernel,
        out_shape=outs,
        in_specs=[vmem] * len(args),
        out_specs=[vmem] * len(outs),
        compiler_params=pltpu.CompilerParams(vmem_limit_bytes=VMEM_LIMIT),
        name="update",
    )(*args)


def turned_states(states):
    heads, merge, expand, shrink, vectors, encode, codebook, decode = states
    merge, shrink = merge.transpose(0, 2, 1), shrink.transpose(0, 2, 1)
    return (heads, merge, expand, shrink, vectors, encode, codebook.T, decode.T)


def local_tuned(frames, codes, clip_frames, out_cotangent, masters, firsts, seconds):
    masters, firsts, seconds = [turned_states(s) for s in (masters, firsts, seconds)]
    results = run_decoder(True, (codes, frames, out_cotangent), masters)
    entries, dchosen, vector_grads, ddecode = results[0:4]
    partials = [g.reshape(SPLIT + (32, g.shape[2])) for g in results[4:7]]
    decoded_near, decoded_far, frame, codes_here, ved = results[7:12]
    weights = [w.reshape(2, WIDTH, w.shape[5]) for w in results[12:15]]
    inputs = (clip_frames, codes_here, frame, entries, dchosen, ved, *weights)
    results = run_encoder(True, inputs, (vector_grads, ddecode, decoded_far), partials)
    decoded_got, dx_near, dx_got, norm = results[0:4]
    frames_out = (decoded_near, decoded_got, dx_near, dx_got)
    *updates, decoded, dframe = run_update(
        frames_out, norm, results[4:], masters, firsts, seconds
    )
    kinds = [turned_states(updates[k::4]) for k in range(4)]
    updates = [kinds[k][member] for member in range(8) for k in range(4)]
    return (decoded, dframe, norm.reshape(()), *updates)


def swap_half(rows):
    return lax.ppermute(rows, "tensor", [(0, 1), (1, 0)])


def join_frame(pair):
    mine = lax.axis_index("tensor")
    own = lax.dynamic_index_in_dim(pair, mine, axis=0, keepdims=False)
    other = lax.dynamic_index_in_dim(pair, 1 - mine, axis=0, keepdims=False)
    return jnp.stack([own, swap_half(other)])


def split_frame(rows):
    mine = lax.axis_index("tensor")
    half = rows.shape[0] // 2
    other = swap_half(rows[half:].astype(jnp.bfloat16)).astype(jnp.float32)
    own = rows[:half]
    return jnp.where(mine == 0, jnp.stack([own, other]), jnp.stack([other, own]))


def gather_plain(shard):
    gathered = lax.all_gather(shard, ("dp", "tensor"), axis=0, tiled=False)
    split = gathered.reshape((lax.axis_size("dp"), 2) + shard.shape)
    return split.transpose(1, 0, 2, 3).reshape(2, -1, shard.shape[1])


def scatter_plain(partial):
    return lax.psum_scatter(
        partial.astype(jnp.float32), ("dp", "tensor"), scatter_dimension=0, tiled=True
    )


def reduce_plain(partial):
    split = partial.reshape(2, lax.axis_size("dp"), -1, partial.shape[2]).transpose(1, 0, 2, 3)
    return scatter_plain(split.reshape(-1, partial.shape[2]))


def local_plain(frames, codes, clip_frames, out_cotangent, masters, firsts, seconds):
    heads, merge, expand, shrink, vectors, encode, codebook, decode = masters
    weights = []
    for b in range(2):
        even = jnp.concatenate([heads[b, m, :, :PAIR] for m in range(3)], axis=1)
        odd = jnp.concatenate([heads[b, m, :, PAIR:] for m in range(3)], axis=1)
        mlp = jnp.concatenate([merge[b].T, expand[b]], axis=1)
        shards = (jnp.concatenate([even, odd], axis=1), mlp, shrink[b].T)
        weights.append([gather_plain(low(shard)) for shard in shards])
    both = ("dp", "tensor")
    columns = vectors.shape[1]
    blank = jnp.zeros((columns, CODE), jnp.float32)
    tall = jnp.pad(vectors.T, ((0, 0), (0, CODE - vectors.shape[0])))
    ved = low(jnp.concatenate([encode, tall, decode.T, blank], axis=1))
    ved = lax.all_gather(ved, both, axis=0, tiled=True)
    book = lax.all_gather(low(codebook), both, axis=0, tiled=True)
    book = book.reshape(4, 2048, CODE).transpose(1, 0, 2).reshape(2048, PAIR)
    code_rows = join_frame(codes).reshape(codes.shape[0], 1, codes.shape[1])
    results = run_decoder(False, (code_rows, join_frame(out_cotangent), ved, book, *weights[1]))
    entries, dchosen, vg_other, ddecode = results[0:4]
    decoder_grads, decoded = results[4:7], results[7]
    inputs = (clip_frames, code_rows, join_frame(frames), entries, dchosen, ved, *weights[0])
    results = run_encoder(False, inputs)
    dframe, vg, dencode, dbook = results[0:4]
    encoder_grads = results[4:7]
    sums = [[reduce_plain(g) for g in grads] for grads in (encoder_grads, decoder_grads)]
    dheads, dmerge, dexpand, dshrink = [], [], [], []
    for heads_sum, mlp_sum, shrink_sum in sums:
        even, odd = heads_sum[:, :384], heads_sum[:, 384:]
        parts = [
            jnp.concatenate([part[:, m * PAIR : (m + 1) * PAIR] for part in (even, odd)], axis=1)
            for m in range(3)
        ]
        dheads.append(jnp.stack(parts))
        dmerge.append(mlp_sum[:, :256].T)
        dexpand.append(mlp_sum[:, 256:])
        dshrink.append(shrink_sum.T)
    small = jnp.concatenate([dencode, vg + vg_other, ddecode], axis=0).T
    small = scatter_plain(small)
    dbook = dbook.reshape(2048, 4, CODE).transpose(1, 0, 2).reshape(-1, CODE)
    gradients = (
        jnp.stack(dheads),
        jnp.stack(dmerge),
        jnp.stack(dexpand),
        jnp.stack(dshrink),
        small[:, CODE : CODE + vectors.shape[0]].T,
        small[:, :CODE],
        scatter_plain(dbook),
        small[:, CODE + 16 :].T,
    )
    squares = sum(jnp.sum(gradient * gradient) for gradient in gradients)
    norm_before = jnp.sqrt(lax.psum(squares, both))
    factor = MAX_NORM / jnp.maximum(norm_before, MAX_NORM)
    updates = []
    for member in range(8):
        updates += adam_parts(
            masters[member],
            gradients[member] * factor,
            firsts[member],
            seconds[member],
            RATES[member],
            DECAYS[member],
        )
    return (split_frame(decoded), split_frame(dframe), norm_before, *updates)


def local(frames, codes, clip_frames, out_cotangent, *states):
    tuned = lax.axis_size("dp") == 16 and lax.axis_size("tensor") == 2
    run = local_tuned if tuned and not FORCE_PLAIN else local_plain
    return run(frames, codes, clip_frames, out_cotangent, states[0:8], states[8:16], states[16:24])


FORCE_PLAIN = False


def solution(mesh):
    return jax.shard_map(
        local,
        mesh=mesh,
        in_specs=(
            P("dp", "tensor", None),
            P("dp", "tensor"),
            P(),
            P("dp", "tensor", None),
            P(None, None, "dp", "tensor"),
            P(None, "tensor", "dp"),
            P(None, "dp", "tensor"),
            P(None, "tensor", "dp"),
            P(None, ("dp", "tensor")),
            P(("dp", "tensor"), None),
            P(("dp", "tensor"), None),
            P(None, ("dp", "tensor")),
            P(None, None, "dp", "tensor"),
            P(None, "tensor", "dp"),
            P(None, "dp", "tensor"),
            P(None, "tensor", "dp"),
            P(None, ("dp", "tensor")),
            P(("dp", "tensor"), None),
            P(("dp", "tensor"), None),
            P(None, ("dp", "tensor")),
            P(None, None, "dp", "tensor"),
            P(None, "tensor", "dp"),
            P(None, "dp", "tensor"),
            P(None, "tensor", "dp"),
            P(None, ("dp", "tensor")),
            P(("dp", "tensor"), None),
            P(("dp", "tensor"), None),
            P(None, ("dp", "tensor")),
        ),
        out_specs=(
            P("dp", "tensor", None),
            P("dp", "tensor", None),
            P(),
            P(None, None, "dp", "tensor"),
            P(None, None, "dp", "tensor"),
            P(None, None, "dp", "tensor"),
            P(None, None, "dp", "tensor"),
            P(None, "tensor", "dp"),
            P(None, "tensor", "dp"),
            P(None, "tensor", "dp"),
            P(None, "tensor", "dp"),
            P(None, "dp", "tensor"),
            P(None, "dp", "tensor"),
            P(None, "dp", "tensor"),
            P(None, "dp", "tensor"),
            P(None, "tensor", "dp"),
            P(None, "tensor", "dp"),
            P(None, "tensor", "dp"),
            P(None, "tensor", "dp"),
            P(None, ("dp", "tensor")),
            P(None, ("dp", "tensor")),
            P(None, ("dp", "tensor")),
            P(None, ("dp", "tensor")),
            P(("dp", "tensor"), None),
            P(("dp", "tensor"), None),
            P(("dp", "tensor"), None),
            P(("dp", "tensor"), None),
            P(("dp", "tensor"), None),
            P(("dp", "tensor"), None),
            P(("dp", "tensor"), None),
            P(("dp", "tensor"), None),
            P(None, ("dp", "tensor")),
            P(None, ("dp", "tensor")),
            P(None, ("dp", "tensor")),
            P(None, ("dp", "tensor")),
        ),
        check_vma=False,
    )
```
